32 devices in a mesh: row: 4 (over z), col: 8 (over y, x, core).
Axes of the slice: x: 2, y: 2, z: 4, core: 2. Of those that a mesh axis runs over, the one named last changes fastest.
Arguments:
- tile_values: float32 [512, 512, 512], P(('row', 'col')), may hold values from -6 to 6
- tile_coords: int32 [512, 2], P(('row', 'col')), may hold values from 0 to 3, as said below
- tile_counts: int32 [32], P(('row', 'col')), may hold values from 4 to 16, as said below
- restrict_basis: float32 [8192, 256], P(('row', 'col')), may hold values from -0.25 to 0.25
- prolong_basis: float32 [16384, 256], P(('col', 'row')), may hold values from -0.25 to 0.25
- row_partner: int32 [8, 4], replicated, may hold values from 0 to 3, as said below
- col_partner: int32 [4, 8], replicated, may hold values from 0 to 7, as said below
Outputs:
- coarse: float32 [2048, 4096], P('row', 'col')
The draws below stay inside these ranges and needn't reach their ends.
Inputs may be any that keep to these rules, and one draw needn't show every extreme that they name: `tile_coords`: within one device's 16 slots no two name the same (block row, block column); first entry below 4, second below 4; dead slots also hold such positions. `tile_counts`: number of leading slots of each device that are live; some device has all 16 live. `row_partner`: each row is a pairing: the partner of a part's partner is the part itself, never the part. `col_partner`: each row is a pairing: the partner of a part's partner is the part itself, never the part.
All inputs are finite; a program needn't handle non-finite values.
Results may differ from the reference program's by a relative error of at most 0.0003.
Values sent between devices are 32-bit elements; how exact they have to be, the bound alone decides.
No kernel may reach another device: no remote copies, remote signals or barrier semaphores. Data moves between devices by JAX's collectives and lax.ppermute only.
A program may use at most 128 MiB of HBM per device.

```python
import jax
import jax.numpy as jnp
from jax import lax

TB = 512
K = 256
RB = 4
CB = 4
SLOTS = 16
FINE_ROWS = 8192
FINE_COLS = 16384
TILES = 512
N_ROW = 4
N_COL = 8


def pairing(key, parts):
    order = jax.random.permutation(key, parts).astype(jnp.int32)
    swapped = order.reshape(-1, 2)[:, ::-1].reshape(-1)
    return jnp.zeros((parts,), jnp.int32).at[order].set(swapped)


def draw_row_partner(key, part):
    row_keys = jax.random.split(jax.random.fold_in(key, 11), N_COL)
    return jax.vmap(lambda one_key: pairing(one_key, N_ROW))(row_keys).astype(jnp.int32)


def draw_col_partner(key, part):
    col_keys = jax.random.split(jax.random.fold_in(key, 13), N_ROW)
    return jax.vmap(lambda one_key: pairing(one_key, N_COL))(col_keys).astype(jnp.int32)


def draw_tile_coords(key, part):
    devices_all = N_ROW * N_COL
    device_keys = jax.random.split(jax.random.fold_in(key, 17), devices_all)
    orders = jax.vmap(lambda one_key: jax.random.permutation(one_key, SLOTS))(device_keys).astype(jnp.int32)
    flat_orders = orders.reshape(-1)
    return jnp.stack([flat_orders // CB, flat_orders % CB], axis=1).astype(jnp.int32)


def draw_tile_counts(key, part):
    devices_all = N_ROW * N_COL
    lowest = max(1, SLOTS // 4)
    count_key = jax.random.fold_in(key, 19)
    drawn = jax.random.randint(count_key, (devices_all,), lowest, SLOTS + 1).astype(jnp.int32)
    chosen = jax.random.permutation(jax.random.fold_in(key, 23), devices_all).astype(jnp.int32)
    drawn = drawn.at[chosen[0]].set(SLOTS)
    return drawn.at[chosen[1]].set(lowest)


def level_of(stream_key, dims, pieces, smallest, largest):
    factor_of = 1.0
    for axis_at, shards_of in pieces:
        draws = jax.random.uniform(jax.random.fold_in(jax.random.fold_in(stream_key, 6), axis_at), (shards_of,), jnp.float32, smallest / len(pieces), largest / len(pieces))
        factor_of = factor_of * jnp.repeat(jnp.exp(draws), dims[axis_at] // shards_of).reshape((-1,) + (1,) * (len(dims) - 1 - axis_at))
    return factor_of


def normal_values(key, shape, deviation, most, shards=(), held_as=jnp.bfloat16):
    result = jax.random.normal(key, shape, jnp.float32) * deviation
    if len(shards) > 0:
        result = level_of(key, shape, shards, -0.22, 0.18) * result
    return jnp.clip(result, min=-most, max=most).astype(held_as)


def setup_inputs(seed: int = 0) -> dict:
    key_list = jax.random.split(jax.random.key(seed), 8)
    return {
        "tile_values": normal_values(key_list[0], (TILES, TB, TB), 1.0, 6.0, ((0, 32),), jnp.float32),
        "tile_coords": draw_tile_coords(jax.random.fold_in(key_list[7], 71), 0),
        "tile_counts": draw_tile_counts(jax.random.fold_in(key_list[7], 71), 0),
        "restrict_basis": normal_values(key_list[3], (FINE_ROWS, K), TB ** -0.5, 0.25, ((0, 32),), jnp.float32),
        "prolong_basis": normal_values(key_list[4], (FINE_COLS, K), TB ** -0.5, 0.25, ((0, 32),), jnp.float32),
        "row_partner": draw_row_partner(jax.random.fold_in(key_list[7], 71), 0),
        "col_partner": draw_col_partner(jax.random.fold_in(key_list[7], 71), 0),
    }


def device_grid(tile_block, coord_block, live_count, restrict_part, prolong_part):
    def add_slot(slot_index, grid_now):
        block_row = coord_block[slot_index, 0]
        block_col = coord_block[slot_index, 1]
        left = lax.dynamic_slice_in_dim(restrict_part, (block_row * TB).astype(jnp.int32), TB, 0)
        right = lax.dynamic_slice_in_dim(prolong_part, (block_col * TB).astype(jnp.int32), TB, 0)
        applied = jnp.dot(tile_block[slot_index], right, precision=lax.Precision.HIGHEST)
        product = jnp.dot(left.T, applied, precision=lax.Precision.HIGHEST)
        product = jnp.where(slot_index < live_count, product, jnp.zeros_like(product))
        place = ((block_row * K).astype(jnp.int32), (block_col * K).astype(jnp.int32))
        current = lax.dynamic_slice(grid_now, place, (K, K))
        return lax.dynamic_update_slice(grid_now, current + product, place)

    start_grid = jnp.zeros((RB * K, CB * K), jnp.float32)
    return lax.fori_loop(0, SLOTS, add_slot, start_grid)


def reference(tile_values, tile_coords, tile_counts, restrict_basis, prolong_basis, row_partner, col_partner):
    devices_all = N_ROW * N_COL
    tile_all = tile_values.reshape(devices_all, SLOTS, TB, TB)
    coord_all = tile_coords.reshape(devices_all, SLOTS, 2)
    restrict_all = restrict_basis.reshape(N_ROW, RB * TB, K)
    prolong_all = prolong_basis.reshape(N_COL, CB * TB, K)
    device_ids = jnp.arange(devices_all, dtype=jnp.int32)

    def one_device(inputs):
        tile_block, coord_block, live_count, device_id = inputs
        row_id = device_id // N_COL
        col_id = device_id % N_COL
        return device_grid(tile_block, coord_block, live_count, restrict_all[row_id], prolong_all[col_id])

    grids = lax.map(one_device, (tile_all, coord_all, tile_counts, device_ids))
    grids = grids.reshape(N_ROW, N_COL, RB * K, CB * K)
    row_ids = jnp.arange(N_ROW, dtype=jnp.int32)
    col_ids = jnp.arange(N_COL, dtype=jnp.int32)
    partner_rows = row_partner.T
    row_sum = grids + grids[partner_rows, col_ids[None, :]]
    row_halves = row_sum.reshape(N_ROW, N_COL, 2, RB * K // 2, CB * K)
    keep_row = row_ids[:, None] > partner_rows
    rowpair = jnp.where(keep_row[:, :, None, None], row_halves[:, :, 1], row_halves[:, :, 0])
    col_sum = rowpair + rowpair[row_ids[:, None], col_partner]
    col_halves = col_sum.reshape(N_ROW, N_COL, RB * K // 2, 2, CB * K // 2)
    keep_col = col_ids[None, :] > col_partner
    quarter = jnp.where(keep_col[:, :, None, None], col_halves[:, :, :, 1], col_halves[:, :, :, 0])
    return quarter.transpose(0, 2, 1, 3).reshape(N_ROW * RB * K // 2, N_COL * CB * K // 2)
```

```python
import jax
import jax.numpy as jnp
from jax import lax
from jax.experimental import pallas as pl
from jax.experimental.pallas import tpu as pltpu
from jax.sharding import PartitionSpec as P

F32 = jnp.float32
BF16 = jnp.bfloat16
VMEM_BYTES = 48 * 1024 * 1024


def split(value):
    high = value.astype(BF16)
    low = (value - high.astype(F32)).astype(BF16)
    return high, low


def dot(left, right):
    return jnp.dot(left, right, preferred_element_type=F32)


def product(left_high, left_low, right_high, right_low):
    return dot(left_high, right_high) + (dot(left_high, right_low) + dot(left_low, right_high))


def left_kernel(shards, block_cols, *refs):
    slot_ref, live_ref, place_ref = refs[:3]
    tile_ref = refs[3]
    pieces = refs[4 : 4 + shards]
    high_out, low_out, q_high, q_low = refs[4 + shards :]
    step = pl.program_id(0)
    tile_order = tile_ref.shape[1]
    depth = q_high.shape[2]
    per_block = tile_order // depth

    @pl.when(step == 0)
    def _():
        for index, piece in enumerate(pieces):
            high, low = split(piece[...])
            q_high[place_ref[index]] = high
            q_low[place_ref[index]] = low

    @pl.when(live_ref[step] == 1)
    def _():
        first = (step // block_cols) * per_block
        total = None
        for part in range(per_block):
            high, low = split(tile_ref[0, part * depth : (part + 1) * depth, :])
            term = product(q_high[first + part], q_low[first + part], high, low)
            total = term if total is None else total + term
        high, low = split(total)
        high_out[0] = high
        low_out[0] = low

    @pl.when(live_ref[step] == 0)
    def _():
        high_out[...] = jnp.zeros_like(high_out)
        low_out[...] = jnp.zeros_like(low_out)


def left_products(tiles, slots, live, pieces, places, block_cols):
    positions = slots.shape[0]
    tile_order = tiles.shape[1]
    width, depth = pieces[0].shape
    shards = len(pieces)
    whole = pl.BlockSpec((width, depth), lambda i, *_: (0, 0))
    out_spec = pl.BlockSpec((1, width, tile_order), lambda i, *_: (i, 0, 0))
    out = jax.ShapeDtypeStruct((positions, width, tile_order), BF16)
    return pl.pallas_call(
        lambda *refs: left_kernel(shards, block_cols, *refs),
        grid_spec=pltpu.PrefetchScalarGridSpec(
            num_scalar_prefetch=3,
            grid=(positions,),
            in_specs=[pl.BlockSpec((1, tile_order, tile_order), lambda i, s, *_: (s[i], 0, 0))]
            + [whole] * shards,
            out_specs=[out_spec, out_spec],
            scratch_shapes=[pltpu.VMEM((shards, width, depth), BF16)] * 2,
        ),
        out_shape=[out, out],
        compiler_params=pltpu.CompilerParams(vmem_limit_bytes=VMEM_BYTES),
        cost_estimate=pl.CostEstimate(
            flops=6 * positions * width * tile_order * tile_order,
            bytes_accessed=4 * tiles.size + 4 * positions * width * tile_order,
            transcendentals=0,
        ),
        name="left_products",
    )(slots, live, places, tiles, *pieces)


def right_kernel(shards, chunks, per_chunk, *refs):
    place_ref, column_ref, shard_ref = refs[:3]
    high_ref, low_ref = refs[3:5]
    pieces = refs[5 : 5 + shards]
    outs = refs[5 + shards : 5 + shards + chunks]
    p_high, p_low = refs[5 + shards + chunks :]
    step = pl.program_id(0)
    tile_order = high_ref.shape[2]
    depth = pieces[0].shape[0]

    @pl.when(step == 0)
    def _():
        for index, piece in enumerate(pieces):

            @pl.when(shard_ref[index] >= 0)
            def _():
                high, low = split(piece[...])
                rows = pl.ds(pl.multiple_of(shard_ref[index] * depth, depth), depth)
                p_high[rows, :] = high
                p_low[rows, :] = low

    chunk = step // per_chunk
    start = pl.multiple_of(column_ref[chunk] * tile_order, tile_order)
    rows = pl.ds(start, tile_order)
    block = product(high_ref[0], low_ref[0], p_high[rows, :], p_low[rows, :])
    for index in range(chunks):

        @pl.when(chunk == index)
        def _():
            outs[index][...] = block


def right_products(w_high, w_low, positions, columns, pieces, shard_of, shard_count):
    steps = positions.shape[0]
    chunks = columns.shape[0]
    per_chunk = steps // chunks
    _, width, tile_order = w_high.shape
    depth, _ = pieces[0].shape
    shards = len(pieces)
    w_spec = pl.BlockSpec((1, width, tile_order), lambda i, pos, *_: (pos[i], 0, 0))
    whole = pl.BlockSpec((depth, width), lambda i, *_: (0, 0))

    def out_spec(index):
        first = index * per_chunk
        return pl.BlockSpec(
            (width, width), lambda i, *_: (jnp.clip(i - first, 0, per_chunk - 1), 0)
        )

    return pl.pallas_call(
        lambda *refs: right_kernel(shards, chunks, per_chunk, *refs),
        grid_spec=pltpu.PrefetchScalarGridSpec(
            num_scalar_prefetch=3,
            grid=(steps,),
            in_specs=[w_spec, w_spec] + [whole] * shards,
            out_specs=[out_spec(index) for index in range(chunks)],
            scratch_shapes=[pltpu.VMEM((shard_count * depth, width), BF16)] * 2,
        ),
        out_shape=[jax.ShapeDtypeStruct((per_chunk * width, width), F32)] * chunks,
        compiler_params=pltpu.CompilerParams(vmem_limit_bytes=VMEM_BYTES),
        cost_estimate=pl.CostEstimate(
            flops=6 * steps * width * width * tile_order,
            bytes_accessed=4 * steps * width * (tile_order + width),
            transcendentals=0,
        ),
        name="right_products",
    )(positions, columns, shard_of, w_high, w_low, *pieces)


def flip(value, axis, size, mask):
    return lax.ppermute(value, axis, [(i, i ^ mask) for i in range(size)])


def gather_restrict(shard, axis, size, me):
    if size == 8:
        pieces = [shard] + [flip(shard, axis, size, mask) for mask in range(1, size)]
        places = me ^ jnp.arange(size, dtype=jnp.int32)
        return pieces, places
    gathered = lax.all_gather(shard, axis)
    return [gathered[i] for i in range(size)], jnp.arange(size, dtype=jnp.int32)


def gather_prolong(shard, axis, size, me):
    if size != 4:
        gathered = lax.all_gather(shard, axis)
        return [gathered[i] for i in range(size)], jnp.arange(size, dtype=jnp.int32)
    pieces, shard_of = [shard], [me]
    up = down = shard
    for step in range(1, size):
        up = lax.ppermute(up, axis, [(i, i + 1) for i in range(step - 1, size - 1)])
        down = lax.ppermute(down, axis, [(i + 1, i) for i in range(size - step)])
        pieces += [up, down]
        shard_of += [me - step, jnp.where(me + step < size, me + step, -1)]
    return pieces, jnp.stack(shard_of).astype(jnp.int32)


def row_exchange(chunk, axis, size, kind, me, partner):
    if size != 4:
        gathered = lax.all_gather(chunk, axis)
        return lax.dynamic_index_in_dim(gathered, partner, 0, keepdims=False)
    outer = lax.ppermute(chunk, axis, [(0, 1), (3, 2)])
    own_over = lax.ppermute(chunk, axis, [(1, 2), (2, 1)])
    outer_over = lax.ppermute(outer, axis, [(1, 2), (2, 1)])
    handed = jnp.where(kind == 1, chunk, jnp.where(kind == 2, own_over, outer_over))
    handed = lax.ppermute(handed, axis, [(1, 0), (2, 3)])
    inner = jnp.where(kind == 1, outer, jnp.where(kind == 2, outer_over, own_over))
    return jnp.where((me == 1) | (me == 2), inner, handed)


def col_exchange(chunk, axis, size, me, partner, mate_partner, turn):
    if size != 8:
        gathered = lax.all_gather(chunk, axis)
        return lax.dynamic_index_in_dim(gathered, partner, 0, keepdims=False)
    over_x = flip(chunk, axis, size, 2)
    over_y = flip(chunk, axis, size, 4)
    over_both = flip(over_y, axis, size, 2) if turn else flip(over_x, axis, size, 4)

    def pick(chip):
        return jnp.where(
            chip == 0, chunk, jnp.where(chip == 2, over_x, jnp.where(chip == 4, over_y, over_both))
        )

    from_mate = flip(pick((me ^ 1 ^ mate_partner) & 6), axis, size, 1)
    mine = me ^ partner
    return jnp.where((mine & 1) == 1, from_mate, pick(mine & 6))


def solution(mesh):
    n_row = mesh.shape["row"]
    n_col = mesh.shape["col"]

    def body(tiles, coords, counts, restrict, prolong, row_partner, col_partner):
        slot_count, tile_order, _ = tiles.shape
        block_rows = restrict.shape[0] * n_col // tile_order
        block_cols = prolong.shape[0] * n_row // tile_order
        positions = jnp.arange(block_rows * block_cols, dtype=jnp.int32)
        row = lax.axis_index("row").astype(jnp.int32)
        col = lax.axis_index("col").astype(jnp.int32)

        q_pieces, q_places = gather_restrict(restrict.T, "col", n_col, col)
        p_pieces, p_shards = gather_prolong(prolong, "row", n_row, row)

        slot_ids = jnp.arange(slot_count, dtype=jnp.int32)
        hits = (coords[:, 0] * block_cols + coords[:, 1])[None, :] == positions[:, None]
        live = jnp.any(hits & (slot_ids < counts[0])[None, :], axis=1).astype(jnp.int32)
        slots = jnp.sum(jnp.where(hits, slot_ids[None, :], 0), axis=1).astype(jnp.int32)

        row_mate = row_partner[col, row]
        col_mate = col_partner[row, col]
        keep_row = (row > row_mate).astype(jnp.int32)
        keep_col = (col > col_mate).astype(jnp.int32)
        mate_keep_col = (col > col_partner[row_mate, col]).astype(jnp.int32)
        half_rows = block_rows // 2
        half_cols = block_cols // 2

        def order(row_half, col_half):
            ids = jnp.arange(block_cols, dtype=jnp.int32)
            columns = (ids + (1 - col_half) * half_cols) % block_cols
            rows = jnp.arange(half_rows, dtype=jnp.int32) + row_half * half_rows
            places = rows[None, :] * block_cols + columns[:, None]
            return places.reshape(-1).astype(jnp.int32), columns.astype(jnp.int32)

        w_high, w_low = left_products(tiles, slots, live, q_pieces, q_places, block_cols)
        places, columns = order(1 - keep_row, mate_keep_col)
        given = right_products(w_high, w_low, places, columns, p_pieces, p_shards, n_row)
        places, columns = order(keep_row, keep_col)
        kept = right_products(w_high, w_low, places, columns, p_pieces, p_shards, n_row)

        kind = row ^ row_mate
        sums = [
            own + row_exchange(chunk, "row", n_row, kind, row, row_mate)
            for own, chunk in zip(kept, given)
        ]
        mate_partner = col_partner[row, col ^ 1]
        quarters = [
            sums[half_cols + i]
            + col_exchange(sums[i], "col", n_col, col, col_mate, mate_partner, i % 2)
            for i in range(half_cols)
        ]
        return jnp.concatenate(quarters, axis=1)

    in_specs = (
        P(("row", "col"), None, None),
        P(("row", "col"), None),
        P(("row", "col")),
        P(("row", "col"), None),
        P(("col", "row"), None),
        P(),
        P(),
    )
    return jax.shard_map(
        body, mesh=mesh, in_specs=in_specs, out_specs=P("row", "col"), check_vma=False
    )
```

```python
import functools

import jax
import jax.numpy as jnp
from jax import lax
from jax.experimental import pallas as pl
from jax.experimental.pallas import tpu as pltpu
from jax.sharding import PartitionSpec as P

F32 = jnp.float32
BF16 = jnp.bfloat16
VMEM_BYTES = 48 * 1024 * 1024


def split(value):
    high = value.astype(BF16)
    low = (value - high.astype(F32)).astype(BF16)
    return high, low


def dot(left, right):
    return jnp.dot(left, right, preferred_element_type=F32)


def product(left_both, right_high, right_low):
    half = left_both.shape[0] // 2
    over_high = dot(left_both, right_high)
    over_low = dot(left_both[:half], right_low)
    return over_high[:half] + (over_high[half:] + over_low)


def slot_at(coords, place, block_cols, slot_count):
    found = jnp.int32(-1)
    for slot in range(slot_count):
        hit = coords[slot, 0] * block_cols + coords[slot, 1] == place
        found = jnp.where(hit, jnp.int32(slot), found)
    return found


def left_kernel(block_of, block_cols, slot_count, *refs):
    me, coords, counts, tile_ref, q_ref = refs[:5]
    out, q_both = refs[-2:]
    group, column = pl.program_id(0), pl.program_id(1)
    width = q_both.shape[0] // 2

    @pl.when(column == 0)
    def _():
        high, low = split(q_ref[...].T)
        q_both[:width] = high
        q_both[width:] = low

    place = block_of(me, group) * block_cols + column
    slot = slot_at(coords, place, block_cols, slot_count)
    live = (slot >= 0) & (slot < counts[0])

    @pl.when(live)
    def _():
        high, low = split(tile_ref[0])
        total_high, total_low = split(product(q_both[...], high, low))
        out[0, :width] = total_high
        out[0, width:] = total_low

    @pl.when(jnp.logical_not(live))
    def _():
        out[...] = jnp.zeros_like(out)


def left_products(me, coords, counts, tiles, q_rows, block_of, block_rows, block_cols, before):
    slot_count, tile_order, _ = tiles.shape
    width = q_rows.shape[1]
    groups = q_rows.shape[0] // tile_order
    positions = block_rows * block_cols

    def tile_at(g, b, me_ref, coords_ref, counts_ref):
        place = block_of(me_ref, g) * block_cols + b
        return jnp.maximum(slot_at(coords_ref, place, block_cols, slot_count), 0), 0, 0

    def out_at(g, b, me_ref, coords_ref, counts_ref):
        return block_of(me_ref, g) * block_cols + b, 0, 0

    in_specs = [
        pl.BlockSpec((1, tile_order, tile_order), tile_at),
        pl.BlockSpec((tile_order, width), lambda g, b, *_: (g, 0)),
    ]
    operands = [me, coords, counts, tiles, q_rows]
    aliases = {}
    if before is not None:
        in_specs.append(pl.BlockSpec(memory_space=pl.ANY))
        aliases = {len(operands): 0}
        operands.append(before)
    return pl.pallas_call(
        functools.partial(left_kernel, block_of, block_cols, slot_count),
        grid_spec=pltpu.PrefetchScalarGridSpec(
            num_scalar_prefetch=3,
            grid=(groups, block_cols),
            in_specs=in_specs,
            out_specs=pl.BlockSpec((1, 2 * width, tile_order), out_at),
            scratch_shapes=[pltpu.VMEM((2 * width, tile_order), BF16)],
        ),
        out_shape=jax.ShapeDtypeStruct((positions, 2 * width, tile_order), BF16),
        input_output_aliases=aliases,
        compiler_params=pltpu.CompilerParams(vmem_limit_bytes=VMEM_BYTES),
        cost_estimate=pl.CostEstimate(
            flops=12 * groups * block_cols * width * tile_order * tile_order,
            bytes_accessed=4 * groups * block_cols * tile_order * (tile_order + width),
            transcendentals=0,
        ),
        name="left_products",
    )(*operands)


def mates(me, row_partner, col_partner):
    row, col = me[0], me[1]
    row_mate = row_partner[col, row]
    return row, col, row_mate, col_partner[row, col], col_partner[row_mate, col]


def place_of(given, block_rows, block_cols, me, row_partner, col_partner, step):
    row, col, row_mate, col_mate, row_mates_col = mates(me, row_partner, col_partner)
    half_rows, half_cols = block_rows // 2, block_cols // 2
    quarter, inside = step // (half_rows * half_cols), step % (half_rows * half_cols)
    if given:
        row_half, keeps = row_mate > row, col > row_mates_col
    else:
        row_half, keeps = row > row_mate, col > col_mate
    col_half = jnp.where(keeps, quarter, 1 - quarter)
    block_row = jnp.where(row_half, half_rows, 0) + inside // half_cols
    block_col = col_half * half_cols + inside % half_cols
    return block_row, block_col


def right_kernel(given, block_rows, block_cols, shard_places, groups, *refs):
    me, row_partner, col_partner, w_ref = refs[:4]
    pieces = refs[4 : 4 + sum(groups)]
    out, p_high, p_low = refs[4 + sum(groups) :]
    step = pl.program_id(0)
    tile_order = w_ref.shape[2]
    depth = pieces[0].shape[0]

    @pl.when(step == 0)
    def _():
        at = 0
        for place, count in zip(shard_places(me), groups):
            value = pieces[at][...]
            for other in range(1, count):
                value = value + pieces[at + other][...]
            at += count
            rows = pl.ds(pl.multiple_of(place * depth, depth), depth)
            p_high[rows, :], p_low[rows, :] = split(value)

    _, block_col = place_of(given, block_rows, block_cols, me, row_partner, col_partner, step)
    rows = pl.ds(pl.multiple_of(block_col * tile_order, tile_order), tile_order)
    out[0] = product(w_ref[0], p_high[rows, :], p_low[rows, :])


def right_products(given, tables, w, shards, shard_places, block_rows, block_cols):
    _, both, tile_order = w.shape
    width = both // 2
    depth = shards[0][0].shape[0]
    half_rows, half_cols = block_rows // 2, block_cols // 2
    per_quarter = half_rows * half_cols
    steps = 2 * per_quarter
    groups = [len(shard) for shard in shards]
    place = functools.partial(place_of, given, block_rows, block_cols)

    def w_at(i, *refs):
        block_row, block_col = place(*refs, i)
        return block_row * block_cols + block_col, 0, 0

    def out_at(i, *refs):
        inside = i % per_quarter
        return i // per_quarter, inside // half_cols, inside % half_cols

    whole = pl.BlockSpec((depth, width), lambda i, *_: (0, 0))
    return pl.pallas_call(
        functools.partial(
            right_kernel, given, block_rows, block_cols, shard_places, groups
        ),
        grid_spec=pltpu.PrefetchScalarGridSpec(
            num_scalar_prefetch=3,
            grid=(steps,),
            in_specs=[pl.BlockSpec((1, both, tile_order), w_at)] + [whole] * sum(groups),
            out_specs=pl.BlockSpec((1, width, width), out_at),
            scratch_shapes=[pltpu.VMEM((len(shards) * depth, width), BF16)] * 2,
        ),
        out_shape=jax.ShapeDtypeStruct((2, half_rows * width, half_cols * width), F32),
        compiler_params=pltpu.CompilerParams(vmem_limit_bytes=VMEM_BYTES),
        cost_estimate=pl.CostEstimate(
            flops=12 * steps * width * width * tile_order,
            bytes_accessed=4 * steps * width * (tile_order + width),
            transcendentals=0,
        ),
        name="right_products",
    )(*tables, w, *[piece for shard in shards for piece in shard])


def flip(value, axis, size, mask):
    return lax.ppermute(value, axis, [(i, i ^ mask) for i in range(size)])


def gather_prolong(shard, axis, size):
    if size != 4:
        gathered = lax.all_gather(shard, axis)
        return [[gathered[i]] for i in range(size)], lambda me: list(range(size))
    mate = flip(shard, axis, size, 1)
    over = lax.ppermute(shard, axis, [(1, 2), (2, 1)])
    mate_over = lax.ppermute(mate, axis, [(1, 2), (2, 1)])
    handed = lax.ppermute(over, axis, [(1, 0), (2, 3)])
    mate_handed = lax.ppermute(mate_over, axis, [(1, 0), (2, 3)])

    def places(me):
        row = me[0]
        return [row, row ^ 1, jnp.where(row < 2, 2, 1), jnp.where(row < 2, 3, 0)]

    return [[shard], [mate], [over, handed], [mate_over, mate_handed]], places


def pair_switch(mine, mate, size, branch, *operands):
    if size == 2:
        return branch(1, *operands)
    branches = [functools.partial(branch, mask) for mask in range(1, size)]
    return lax.switch((mine ^ mate) - 1, branches, *operands)


def solution(mesh):
    n_row = mesh.shape["row"]
    n_col = mesh.shape["col"]

    def body(tiles, coords, counts, restrict, prolong, row_partner, col_partner):
        tile_order = tiles.shape[1]
        q_depth = restrict.shape[0]
        block_rows = q_depth * n_col // tile_order
        block_cols = prolong.shape[0] * n_row // tile_order
        row = lax.axis_index("row").astype(jnp.int32)
        col = lax.axis_index("col").astype(jnp.int32)
        me = jnp.stack([row, col])

        shards, shard_places = gather_prolong(prolong, "row", n_row)

        left = functools.partial(left_products, me, coords, counts, tiles)
        if n_col == 8 and tile_order == 2 * q_depth:
            mate = flip(restrict, "col", n_col, 1)
            odd = (col & 1) == 1
            own = jnp.concatenate(
                [jnp.where(odd, mate, restrict), jnp.where(odd, restrict, mate)], axis=0
            )
            w = None
            for chip in range(n_col // 2):
                block = own if chip == 0 else flip(own, "col", n_col, 2 * chip)
                w = left(block, lambda ref, g, chip=chip: (ref[1] // 2) ^ chip, block_rows, block_cols, w)
        else:
            blocks = lax.all_gather(restrict, "col", axis=0, tiled=True)
            w = left(blocks, lambda ref, g: g, block_rows, block_cols, None)

        tables = (me, row_partner, col_partner)
        given = right_products(True, tables, w, shards, shard_places, block_rows, block_cols)

        def row_branch(mask, given, w, shards):
            received = flip(given, "row", n_row, mask)
            kept = right_products(False, tables, w, shards, shard_places, block_rows, block_cols)
            return received, kept

        def col_branch(mask, section):
            return flip(section, "col", n_col, mask)

        received, kept = pair_switch(row, row_partner[col, row], n_row, row_branch, given, w, shards)
        section = kept[0] + received[0]
        section = pair_switch(col, col_partner[row, col], n_col, col_branch, section)
        return (kept[1] + received[1]) + section

    in_specs = (
        P(("row", "col"), None, None),
        P(("row", "col"), None),
        P(("row", "col")),
        P(("row", "col"), None),
        P(("col", "row"), None),
        P(),
        P(),
    )
    return jax.shard_map(
        body, mesh=mesh, in_specs=in_specs, out_specs=P("row", "col"), check_vma=False
    )
```

```python
import functools

import jax
import jax.numpy as jnp
from jax import lax
from jax.experimental import pallas as pl
from jax.experimental.pallas import tpu as pltpu
from jax.sharding import PartitionSpec as P

F32 = jnp.float32
BF16 = jnp.bfloat16
VMEM_BYTES = 48 * 1024 * 1024


def split(value):
    high = value.astype(BF16)
    low = (value - high.astype(F32)).astype(BF16)
    return high, low


def dot(left, right):
    return jnp.dot(left, right, preferred_element_type=F32)


def product(left_both, right_high, right_low):
    half = left_both.shape[0] // 2
    over_high = dot(left_both, right_high)
    over_low = dot(left_both[:half], right_low)
    return over_high[:half] + (over_high[half:] + over_low)


def slot_at(coords, place, block_cols, slot_count):
    found = jnp.int32(-1)
    for slot in range(slot_count):
        hit = coords[slot, 0] * block_cols + coords[slot, 1] == place
        found = jnp.where(hit, jnp.int32(slot), found)
    return found


def left_kernel(block_of, block_cols, slot_count, *refs):
    me, coords, counts, tile_ref, q_ref = refs[:5]
    out, q_both = refs[-2:]
    group, column = pl.program_id(0), pl.program_id(1)
    width = q_both.shape[0] // 2

    @pl.when(column == 0)
    def _():
        high, low = split(q_ref[...].T)
        q_both[:width] = high
        q_both[width:] = low

    place = block_of(me, group) * block_cols + column
    slot = slot_at(coords, place, block_cols, slot_count)
    live = (slot >= 0) & (slot < counts[0])

    @pl.when(live)
    def _():
        high, low = split(tile_ref[0])
        total_high, total_low = split(product(q_both[...], high, low))
        out[0, :width] = total_high
        out[0, width:] = total_low

    @pl.when(jnp.logical_not(live))
    def _():
        out[...] = jnp.zeros_like(out)


def left_products(me, coords, counts, tiles, q_rows, block_of, block_rows, block_cols, before):
    slot_count, tile_order, _ = tiles.shape
    width = q_rows.shape[1]
    groups = q_rows.shape[0] // tile_order
    positions = block_rows * block_cols

    def tile_at(g, b, me_ref, coords_ref, counts_ref):
        place = block_of(me_ref, g) * block_cols + b
        return jnp.maximum(slot_at(coords_ref, place, block_cols, slot_count), 0), 0, 0

    def out_at(g, b, me_ref, coords_ref, counts_ref):
        return block_of(me_ref, g) * block_cols + b, 0, 0

    in_specs = [
        pl.BlockSpec((1, tile_order, tile_order), tile_at),
        pl.BlockSpec((tile_order, width), lambda g, b, *_: (g, 0)),
    ]
    operands = [me, coords, counts, tiles, q_rows]
    aliases = {}
    if before is not None:
        in_specs.append(pl.BlockSpec(memory_space=pl.ANY))
        aliases = {len(operands): 0}
        operands.append(before)
    return pl.pallas_call(
        functools.partial(left_kernel, block_of, block_cols, slot_count),
        grid_spec=pltpu.PrefetchScalarGridSpec(
            num_scalar_prefetch=3,
            grid=(groups, block_cols),
            in_specs=in_specs,
            out_specs=pl.BlockSpec((1, 2 * width, tile_order), out_at),
            scratch_shapes=[pltpu.VMEM((2 * width, tile_order), BF16)],
        ),
        out_shape=jax.ShapeDtypeStruct((positions, 2 * width, tile_order), BF16),
        input_output_aliases=aliases,
        compiler_params=pltpu.CompilerParams(vmem_limit_bytes=VMEM_BYTES),
        cost_estimate=pl.CostEstimate(
            flops=12 * groups * block_cols * width * tile_order * tile_order,
            bytes_accessed=4 * groups * block_cols * tile_order * (tile_order + width),
            transcendentals=0,
        ),
        name="left_products",
    )(*operands)


def mates(me, row_partner, col_partner):
    row, col = me[0], me[1]
    row_mate = row_partner[col, row]
    return row, col, row_mate, col_partner[row, col], col_partner[row_mate, col]


def place_of(given, block_rows, block_cols, me, row_partner, col_partner, step):
    row, col, row_mate, col_mate, row_mates_col = mates(me, row_partner, col_partner)
    half_rows, half_cols = block_rows // 2, block_cols // 2
    quarter, inside = step // (half_rows * half_cols), step % (half_rows * half_cols)
    if given:
        row_half, keeps = row_mate > row, col > row_mates_col
    else:
        row_half, keeps = row > row_mate, col > col_mate
    col_half = jnp.where(keeps, quarter, 1 - quarter)
    block_row = jnp.where(row_half, half_rows, 0) + inside // half_cols
    block_col = col_half * half_cols + inside % half_cols
    return block_row, block_col


def right_kernel(given, block_rows, block_cols, shard_places, groups, *refs):
    me, row_partner, col_partner, w_ref = refs[:4]
    pieces = refs[4 : 4 + sum(groups)]
    first, second, p_high, p_low = refs[4 + sum(groups) :]
    step = pl.program_id(0)
    steps = pl.num_programs(0)
    tile_order = w_ref.shape[2]
    depth = pieces[0].shape[0]

    @pl.when(step == 0)
    def _():
        at = 0
        for place, count in zip(shard_places(me), groups):
            value = pieces[at][...]
            for other in range(1, count):
                value = value + pieces[at + other][...]
            at += count
            rows = pl.ds(pl.multiple_of(place * depth, depth), depth)
            p_high[rows, :], p_low[rows, :] = split(value)

    _, block_col = place_of(given, block_rows, block_cols, me, row_partner, col_partner, step)
    rows = pl.ds(pl.multiple_of(block_col * tile_order, tile_order), tile_order)
    block = product(w_ref[0], p_high[rows, :], p_low[rows, :])

    @pl.when(step < steps // 2)
    def _():
        first[...] = block

    @pl.when(step >= steps // 2)
    def _():
        second[...] = block


def right_products(given, tables, w, shards, shard_places, block_rows, block_cols):
    _, both, tile_order = w.shape
    width = both // 2
    depth = shards[0][0].shape[0]
    half_rows, half_cols = block_rows // 2, block_cols // 2
    per_quarter = half_rows * half_cols
    steps = 2 * per_quarter
    groups = [len(shard) for shard in shards]
    place = functools.partial(place_of, given, block_rows, block_cols)

    def w_at(i, *refs):
        block_row, block_col = place(*refs, i)
        return block_row * block_cols + block_col, 0, 0

    def out_spec(quarter):
        def out_at(i, *refs):
            inside = jnp.clip(i - quarter * per_quarter, 0, per_quarter - 1)
            return inside // half_cols, inside % half_cols

        return pl.BlockSpec((width, width), out_at)

    out = jax.ShapeDtypeStruct((half_rows * width, half_cols * width), F32)
    whole = pl.BlockSpec((depth, width), lambda i, *_: (0, 0))
    return pl.pallas_call(
        functools.partial(
            right_kernel, given, block_rows, block_cols, shard_places, groups
        ),
        grid_spec=pltpu.PrefetchScalarGridSpec(
            num_scalar_prefetch=3,
            grid=(steps,),
            in_specs=[pl.BlockSpec((1, both, tile_order), w_at)] + [whole] * sum(groups),
            out_specs=[out_spec(0), out_spec(1)],
            scratch_shapes=[pltpu.VMEM((len(shards) * depth, width), BF16)] * 2,
        ),
        out_shape=[out, out],
        compiler_params=pltpu.CompilerParams(vmem_limit_bytes=VMEM_BYTES),
        cost_estimate=pl.CostEstimate(
            flops=12 * steps * width * width * tile_order,
            bytes_accessed=4 * steps * width * (tile_order + width),
            transcendentals=0,
        ),
        name="right_products",
    )(*tables, w, *[piece for shard in shards for piece in shard])


def flip(value, axis, size, mask):
    return lax.ppermute(value, axis, [(i, i ^ mask) for i in range(size)])


def gather_prolong(shard, axis, size):
    if size != 4:
        gathered = lax.all_gather(shard, axis)
        return [[gathered[i]] for i in range(size)], lambda me: list(range(size))
    mate = flip(shard, axis, size, 1)
    over = lax.ppermute(shard, axis, [(1, 2), (2, 1)])
    mate_over = lax.ppermute(mate, axis, [(1, 2), (2, 1)])
    handed = lax.ppermute(over, axis, [(1, 0), (2, 3)])
    mate_handed = lax.ppermute(mate, axis, [(2, 0), (1, 3)])

    def places(me):
        row = me[0]
        return [row, row ^ 1, jnp.where(row < 2, 2, 1), jnp.where(row < 2, 3, 0)]

    return [[shard], [mate], [over, handed], [mate_over, mate_handed]], places


def pair_switch(mine, mate, size, branch, *operands):
    if size == 2:
        return branch(1, *operands)
    branches = [functools.partial(branch, mask) for mask in range(1, size)]
    return lax.switch((mine ^ mate) - 1, branches, *operands)


def solution(mesh):
    n_row = mesh.shape["row"]
    n_col = mesh.shape["col"]

    def body(tiles, coords, counts, restrict, prolong, row_partner, col_partner):
        tile_order = tiles.shape[1]
        q_depth = restrict.shape[0]
        block_rows = q_depth * n_col // tile_order
        block_cols = prolong.shape[0] * n_row // tile_order
        row = lax.axis_index("row").astype(jnp.int32)
        col = lax.axis_index("col").astype(jnp.int32)
        me = jnp.stack([row, col])

        shards, shard_places = gather_prolong(prolong, "row", n_row)

        left = functools.partial(left_products, me, coords, counts, tiles)
        if n_col == 8 and tile_order == 2 * q_depth:
            mate = flip(restrict, "col", n_col, 1)
            odd = (col & 1) == 1
            own = jnp.concatenate(
                [jnp.where(odd, mate, restrict), jnp.where(odd, restrict, mate)], axis=0
            )
            w = None
            for chip in range(n_col // 2):
                block = own if chip == 0 else flip(own, "col", n_col, 2 * chip)
                w = left(block, lambda ref, g, chip=chip: (ref[1] // 2) ^ chip, block_rows, block_cols, w)
        else:
            blocks = lax.all_gather(restrict, "col", axis=0, tiled=True)
            w = left(blocks, lambda ref, g: g, block_rows, block_cols, None)

        tables = (me, row_partner, col_partner)
        given = right_products(True, tables, w, shards, shard_places, block_rows, block_cols)

        def first_branch(mask, chunk, w, shards):
            received = flip(chunk, "row", n_row, mask)
            kept = right_products(False, tables, w, shards, shard_places, block_rows, block_cols)
            return received, kept

        def second_branch(mask, chunk):
            return flip(chunk, "row", n_row, mask)

        row_mate = row_partner[col, row]
        col_mate = col_partner[row, col]
        received, kept = pair_switch(row, row_mate, n_row, first_branch, given[0], w, shards)
        section = kept[0] + received
        sections = lax.all_gather(section, "col")
        chunk, _ = lax.optimization_barrier((given[1], section))
        received = pair_switch(row, row_mate, n_row, second_branch, chunk)
        section = lax.dynamic_index_in_dim(sections, col_mate, 0, keepdims=False)
        return (kept[1] + received) + section

    in_specs = (
        P(("row", "col"), None, None),
        P(("row", "col"), None),
        P(("row", "col")),
        P(("row", "col"), None),
        P(("col", "row"), None),
        P(),
        P(),
    )
    return jax.shard_map(
        body, mesh=mesh, in_specs=in_specs, out_specs=P("row", "col"), check_vma=False
    )
```

```python
import functools

import jax
import jax.numpy as jnp
from jax import lax
from jax.experimental import pallas as pl
from jax.experimental.pallas import tpu as pltpu
from jax.sharding import PartitionSpec as P

F32 = jnp.float32
BF16 = jnp.bfloat16
VMEM_BYTES = 48 * 1024 * 1024


def split(value):
    high = value.astype(BF16)
    low = (value - high.astype(F32)).astype(BF16)
    return high, low


def dot(left, right):
    return jnp.dot(left, right, preferred_element_type=F32)


def product(left_both, right_high, right_low):
    half = left_both.shape[0] // 2
    over_high = dot(left_both, right_high)
    over_low = dot(left_both[:half], right_low)
    return over_high[:half] + (over_high[half:] + over_low)


def div(value, by):
    return lax.div(value, jnp.int32(by))


def rem(value, by):
    return lax.rem(value, jnp.int32(by))


def left_kernel(row_of, load, block_cols, half_rows, *refs):
    me, slots, row_partner, tile_ref = refs[:4]
    q_refs = refs[4 : 4 + load.count]
    out, q_both = refs[-2:]
    group, column = pl.program_id(0), pl.program_id(1)
    width = q_both.shape[0] // 2

    @pl.when(column == 0)
    def _():
        def put(value, first):
            high, low = split(value.T)
            q_both[:width, first : first + value.shape[0]] = high
            q_both[width:, first : first + value.shape[0]] = low

        load(me, row_partner, group, q_refs, put)

    live = slots[row_of(me, row_partner, group) * block_cols + column] >= 0

    @pl.when(live)
    def _():
        high, low = split(tile_ref[0])
        total_high, total_low = split(product(q_both[...], high, low))
        out[0, :width] = total_high
        out[0, width:] = total_low

    @pl.when(jnp.logical_not(live))
    def _():
        out[...] = jnp.zeros_like(out)


def left_products(tables, tiles, q_pieces, q_specs, row_of, load, groups, half_rows, block_cols, before):
    _, tile_order, _ = tiles.shape
    width = q_pieces[0].shape[1]

    def tile_at(g, b, me, slots, row_partner):
        return jnp.maximum(slots[row_of(me, row_partner, g) * block_cols + b], 0), 0, 0

    def out_at(g, b, me, slots, row_partner):
        return rem(row_of(me, row_partner, g), half_rows) * block_cols + b, 0, 0

    in_specs = [pl.BlockSpec((1, tile_order, tile_order), tile_at)] + q_specs
    operands = [*tables, tiles, *q_pieces]
    aliases = {}
    if before is not None:
        in_specs.append(pl.BlockSpec(memory_space=pl.ANY))
        aliases = {len(operands): 0}
        operands.append(before)
    return pl.pallas_call(
        functools.partial(left_kernel, row_of, load, block_cols, half_rows),
        grid_spec=pltpu.PrefetchScalarGridSpec(
            num_scalar_prefetch=3,
            grid=(groups, block_cols),
            in_specs=in_specs,
            out_specs=pl.BlockSpec((1, 2 * width, tile_order), out_at),
            scratch_shapes=[pltpu.VMEM((2 * width, tile_order), BF16)],
        ),
        out_shape=jax.ShapeDtypeStruct((half_rows * block_cols, 2 * width, tile_order), BF16),
        input_output_aliases=aliases,
        compiler_params=pltpu.CompilerParams(vmem_limit_bytes=VMEM_BYTES),
        cost_estimate=pl.CostEstimate(
            flops=12 * groups * block_cols * width * tile_order * tile_order,
            bytes_accessed=4 * groups * block_cols * tile_order * (tile_order + width),
            transcendentals=0,
        ),
        name="left_products",
    )(*operands)


def half_of(given, me, row_partner):
    mate = row_partner[me[1], me[0]]
    return ((mate > me[0]) if given else (me[0] > mate)).astype(jnp.int32)


class ChipBlocks:
    def __init__(self, given, pairs):
        self.given = given
        self.pairs = pairs
        self.count = 4 * len(pairs)

    def pick(self, me, row_partner):
        chip = div(me[1], 2)
        return half_of(self.given, me, row_partner) == div(chip, 2)

    def row_of(self, me, row_partner, group):
        near_half = self.pick(me, row_partner)
        row = jnp.int32(0)
        for index, (near, far) in enumerate(self.pairs):
            chip = div(me[1], 2) ^ jnp.where(near_half, near, far)
            row = jnp.where(group == index, chip, row)
        return row

    def __call__(self, me, row_partner, group, refs, put):
        near_half = self.pick(me, row_partner)
        odd = rem(me[1], 2) == 1
        for index in range(len(self.pairs)):
            for far in range(2):
                for swap in range(2):
                    first, second = refs[4 * index + 2 * far : 4 * index + 2 * far + 2]
                    wanted = near_half if far == 0 else jnp.logical_not(near_half)
                    order = odd if swap == 1 else jnp.logical_not(odd)

                    @pl.when((group == index) & wanted & order)
                    def _():
                        depth = first.shape[0]
                        put(first[...], swap * depth)
                        put(second[...], (1 - swap) * depth)


class WholeBlocks:
    count = 1

    def __init__(self, given, half_rows):
        self.given = given
        self.half_rows = half_rows

    def row_of(self, me, row_partner, group):
        return half_of(self.given, me, row_partner) * self.half_rows + group

    def __call__(self, me, row_partner, group, refs, put):
        put(refs[0][...], 0)


def mates(me, row_partner, col_partner):
    row, col = me[0], me[1]
    row_mate = row_partner[col, row]
    return row, col, row_mate, col_partner[row, col], col_partner[row_mate, col]


def place_of(given, block_rows, block_cols, me, row_partner, col_partner, step):
    row, col, _, col_mate, row_mates_col = mates(me, row_partner, col_partner)
    half_rows, half_cols = block_rows // 2, block_cols // 2
    quarter, inside = div(step, half_rows * half_cols), rem(step, half_rows * half_cols)
    keeps = col > (row_mates_col if given else col_mate)
    col_half = jnp.where(keeps, quarter, 1 - quarter)
    return div(inside, half_cols), col_half * half_cols + rem(inside, half_cols)


def right_kernel(given, block_rows, block_cols, shard_places, groups, *refs):
    me, row_partner, col_partner, w_ref = refs[:4]
    pieces = refs[4 : 4 + sum(groups)]
    first, second, p_high, p_low = refs[4 + sum(groups) :]
    step = pl.program_id(0)
    steps = pl.num_programs(0)
    tile_order = w_ref.shape[2]
    depth = pieces[0].shape[0]

    @pl.when(step == 0)
    def _():
        at = 0
        for place, count in zip(shard_places(me), groups):
            value = pieces[at][...]
            for other in range(1, count):
                value = value + pieces[at + other][...]
            at += count
            rows = pl.ds(pl.multiple_of(place * depth, depth), depth)
            p_high[rows, :], p_low[rows, :] = split(value)

    _, block_col = place_of(given, block_rows, block_cols, me, row_partner, col_partner, step)
    rows = pl.ds(pl.multiple_of(block_col * tile_order, tile_order), tile_order)
    block = product(w_ref[0], p_high[rows, :], p_low[rows, :])

    @pl.when(step < steps // 2)
    def _():
        first[...] = block

    @pl.when(step >= steps // 2)
    def _():
        second[...] = block


def right_products(given, tables, w, shards, shard_places, block_rows, block_cols):
    _, both, tile_order = w.shape
    width = both // 2
    depth = shards[0][0].shape[0]
    half_rows, half_cols = block_rows // 2, block_cols // 2
    per_quarter = half_rows * half_cols
    steps = 2 * per_quarter
    groups = [len(shard) for shard in shards]
    place = functools.partial(place_of, given, block_rows, block_cols)

    def w_at(i, *refs):
        block_row, block_col = place(*refs, i)
        return block_row * block_cols + block_col, 0, 0

    def out_spec(quarter):
        def out_at(i, *refs):
            inside = jnp.clip(i - quarter * per_quarter, 0, per_quarter - 1)
            return div(inside, half_cols), rem(inside, half_cols)

        return pl.BlockSpec((width, width), out_at)

    out = jax.ShapeDtypeStruct((half_rows * width, half_cols * width), F32)
    whole = pl.BlockSpec((depth, width), lambda i, *_: (0, 0))
    return pl.pallas_call(
        functools.partial(
            right_kernel, given, block_rows, block_cols, shard_places, groups
        ),
        grid_spec=pltpu.PrefetchScalarGridSpec(
            num_scalar_prefetch=3,
            grid=(steps,),
            in_specs=[pl.BlockSpec((1, both, tile_order), w_at)] + [whole] * sum(groups),
            out_specs=[out_spec(0), out_spec(1)],
            scratch_shapes=[pltpu.VMEM((len(shards) * depth, width), BF16)] * 2,
        ),
        out_shape=[out, out],
        compiler_params=pltpu.CompilerParams(vmem_limit_bytes=VMEM_BYTES),
        cost_estimate=pl.CostEstimate(
            flops=12 * steps * width * width * tile_order,
            bytes_accessed=4 * steps * width * (tile_order + width),
            transcendentals=0,
        ),
        name="right_products",
    )(*tables, w, *[piece for shard in shards for piece in shard])


def flip(value, axis, size, mask):
    return lax.ppermute(value, axis, [(i, i ^ mask) for i in range(size)])


def gather_prolong(shard, axis, size):
    if size != 4:
        gathered = lax.all_gather(shard, axis)
        return [[gathered[i]] for i in range(size)], lambda me: list(range(size))
    mate = flip(shard, axis, size, 1)
    over = lax.ppermute(shard, axis, [(1, 2), (2, 1)])
    mate_over = lax.ppermute(mate, axis, [(1, 2), (2, 1)])
    handed = lax.ppermute(over, axis, [(1, 0), (2, 3)])
    mate_handed = lax.ppermute(mate, axis, [(2, 0), (1, 3)])

    def places(me):
        row = me[0]
        return [row, row ^ 1, jnp.where(row < 2, 2, 1), jnp.where(row < 2, 3, 0)]

    return [[shard], [mate], [over, handed], [mate_over, mate_handed]], places


def pair_switch(mine, mate, size, branch, *operands):
    if size == 2:
        return branch(1, *operands)
    branches = [functools.partial(branch, mask) for mask in range(1, size)]
    return lax.switch((mine ^ mate) - 1, branches, *operands)


def solution(mesh):
    n_row = mesh.shape["row"]
    n_col = mesh.shape["col"]

    def body(tiles, coords, counts, restrict, prolong, row_partner, col_partner):
        tile_order = tiles.shape[1]
        q_depth = restrict.shape[0]
        block_rows = q_depth * n_col // tile_order
        block_cols = prolong.shape[0] * n_row // tile_order
        row = lax.axis_index("row").astype(jnp.int32)
        col = lax.axis_index("col").astype(jnp.int32)
        me = jnp.stack([row, col])

        half_rows, half_cols = block_rows // 2, block_cols // 2

        shards, shard_places = gather_prolong(prolong, "row", n_row)
        by_chip = n_col == 8 and block_rows == 4 and tile_order == 2 * q_depth
        if by_chip:
            q_pieces = [restrict] + [flip(restrict, "col", n_col, m) for m in range(1, n_col)]
        else:
            q_pieces = [lax.all_gather(restrict, "col", axis=0, tiled=True)]

        slot_ids = jnp.arange(tiles.shape[0], dtype=jnp.int32)
        place_ids = jnp.arange(block_rows * block_cols, dtype=jnp.int32)
        named = (coords[:, 0] * block_cols + coords[:, 1])[None, :] == place_ids[:, None]
        hit = named & (slot_ids < counts[0])[None, :]
        slots = jnp.max(jnp.where(hit, slot_ids[None, :], -1), axis=1)

        def left(given, pairs, before=None):
            tables = (me, slots, row_partner)
            if by_chip:
                load = ChipBlocks(given, pairs)
                pieces = [
                    q_pieces[2 * chip + core] for pair in pairs for chip in pair for core in range(2)
                ]
                specs = [pl.BlockSpec(restrict.shape, lambda g, b, *_: (0, 0))] * len(pieces)
                groups = len(pairs)
            else:
                load = WholeBlocks(given, half_rows)
                pieces = q_pieces
                specs = [
                    pl.BlockSpec(
                        (tile_order, restrict.shape[1]),
                        lambda g, b, me, slots, row_partner: (load.row_of(me, row_partner, g), 0),
                    )
                ]
                groups = half_rows
            return left_products(
                tables, tiles, pieces, specs, load.row_of, load, groups, half_rows, block_cols, before
            )

        def right(given, w):
            tables = (me, row_partner, col_partner)
            return right_products(given, tables, w, shards, shard_places, block_rows, block_cols)

        if by_chip:
            given = right(True, left(True, [(1, 3)], left(True, [(0, 2)])))
        else:
            given = right(True, left(True, None))

        def first_branch(mask, chunk):
            received = flip(chunk, "row", n_row, mask)
            return received, right(False, left(False, [(0, 2), (1, 3)]))

        def second_branch(mask, chunk):
            return flip(chunk, "row", n_row, mask)

        row_mate = row_partner[col, row]
        col_mate = col_partner[row, col]
        received, kept = pair_switch(row, row_mate, n_row, first_branch, given[0])
        section = kept[0] + received
        chunk, section = lax.optimization_barrier((given[1], section))
        if n_col == 8:
            over = [section] + [flip(section, "col", n_col, 2 * chip) for chip in range(1, 4)]
        else:
            over = lax.all_gather(section, "col")
        received = pair_switch(row, row_mate, n_row, second_branch, chunk)
        over, received = lax.optimization_barrier((over, received))
        if n_col == 8:
            def pick(distance):
                chip = distance >> 1
                return jnp.where(
                    chip < 2,
                    jnp.where(chip == 0, over[0], over[1]),
                    jnp.where(chip == 2, over[2], over[3]),
                )

            handed = flip(pick(col ^ 1 ^ col_partner[row, col ^ 1]), "col", n_col, 1)
            distance = col ^ col_mate
            section = jnp.where((distance & 1) == 1, handed, pick(distance))
        else:
            section = lax.dynamic_index_in_dim(over, col_mate, 0, keepdims=False)
        return (kept[1] + received) + section

    in_specs = (
        P(("row", "col"), None, None),
        P(("row", "col"), None),
        P(("row", "col")),
        P(("row", "col"), None),
        P(("col", "row"), None),
        P(),
        P(),
    )
    return jax.shard_map(
        body, mesh=mesh, in_specs=in_specs, out_specs=P("row", "col"), check_vma=False
    )
```

```python
import functools

import jax
import jax.numpy as jnp
from jax import lax
from jax.experimental import pallas as pl
from jax.experimental.pallas import tpu as pltpu
from jax.sharding import PartitionSpec as P

F32 = jnp.float32
BF16 = jnp.bfloat16
VMEM_BYTES = 48 * 1024 * 1024
PARAMS = pltpu.CompilerParams(vmem_limit_bytes=VMEM_BYTES)


def split(value):
    high = value.astype(BF16)
    low = (value - high.astype(F32)).astype(BF16)
    return high, low


def dot(left, right):
    return jnp.dot(left, right, preferred_element_type=F32)


def product(left_both, right_high, right_low):
    half = left_both.shape[0] // 2
    over_high = dot(left_both, right_high)
    over_low = dot(left_both[:half], right_low)
    return over_high[:half] + (over_high[half:] + over_low)


def div(value, by):
    return lax.div(value, jnp.int32(by))


def rem(value, by):
    return lax.rem(value, jnp.int32(by))


def half_of(given, me, row_partner):
    mate = row_partner[me[1], me[0]]
    return ((mate > me[0]) if given else (me[0] > mate)).astype(jnp.int32)


def left_kernel(given, half_rows, block_cols, per_step, *refs):
    me, slots, row_partner, q_ref = refs[:4]
    tile_refs = refs[4 : 4 + per_step]
    out, q_both = refs[4 + per_step :]
    group, step = pl.program_id(0), pl.program_id(1)
    width = q_both.shape[0] // 2

    @pl.when(step == 0)
    def _():
        high, low = split(q_ref[...].T)
        q_both[:width] = high
        q_both[width:] = low

    block_row = half_of(given, me, row_partner) * half_rows + group
    for index, tile_ref in enumerate(tile_refs):
        live = slots[block_row * block_cols + step * per_step + index] >= 0
        high, low = split(tile_ref[0])
        total = jnp.where(live, product(q_both[...], high, low), 0.0)
        out[index, 0], out[index, 1] = split(total)


def left_products(given, me, slots, row_partner, tiles, q_rows, half_rows, block_cols):
    _, tile_order, _ = tiles.shape
    width = q_rows.shape[1]
    per_step = 2 if block_cols % 2 == 0 else 1

    def row_of(g, me, row_partner):
        return half_of(given, me, row_partner) * half_rows + g

    def tile_spec(index):
        def tile_at(g, b, me, slots, row_partner):
            place = row_of(g, me, row_partner) * block_cols + b * per_step + index
            return jnp.maximum(slots[place], 0), 0, 0

        return pl.BlockSpec((1, tile_order, tile_order), tile_at)

    return pl.pallas_call(
        functools.partial(left_kernel, given, half_rows, block_cols, per_step),
        grid_spec=pltpu.PrefetchScalarGridSpec(
            num_scalar_prefetch=3,
            grid=(half_rows, block_cols // per_step),
            in_specs=[
                pl.BlockSpec(
                    (tile_order, width),
                    lambda g, b, me, slots, row_partner: (row_of(g, me, row_partner), 0),
                )
            ]
            + [tile_spec(index) for index in range(per_step)],
            out_specs=pl.BlockSpec(
                (per_step, 2, width, tile_order), lambda g, b, *_: (b, 0, g, 0)
            ),
            scratch_shapes=[pltpu.VMEM((2 * width, tile_order), BF16)],
        ),
        out_shape=jax.ShapeDtypeStruct((block_cols, 2, half_rows * width, tile_order), BF16),
        compiler_params=PARAMS,
        cost_estimate=pl.CostEstimate(
            flops=12 * half_rows * block_cols * width * tile_order * tile_order,
            bytes_accessed=4 * half_rows * block_cols * tile_order * (tile_order + width),
            transcendentals=0,
        ),
        name="left_products",
    )(me, slots, row_partner, q_rows, *[tiles] * per_step)


def column_of(given, block_cols, step, me, row_partner, col_partner):
    row, col = me[0], me[1]
    holder = row_partner[col, row] if given else row
    keeps = col > col_partner[holder, col]
    half_cols = block_cols // 2
    later = div(step, half_cols)
    return jnp.where(keeps, later, 1 - later) * half_cols + rem(step, half_cols)


def right_kernel(given, block_cols, shard_places, groups, *refs):
    me, row_partner, col_partner, w_ref = refs[:4]
    pieces = refs[4 : 4 + sum(groups)]
    outs = refs[4 + sum(groups) : -2]
    p_high, p_low = refs[-2:]
    step = pl.program_id(0)
    tile_order = w_ref.shape[3]
    depth = pieces[0].shape[0]

    @pl.when(step == 0)
    def _():
        at = 0
        for place, count in zip(shard_places(me), groups):
            value = pieces[at][...]
            for other in range(1, count):
                value = value + pieces[at + other][...]
            at += count
            rows = pl.ds(pl.multiple_of(place * depth, depth), depth)
            p_high[rows, :], p_low[rows, :] = split(value)

    column = column_of(given, block_cols, step, me, row_partner, col_partner)
    rows = pl.ds(pl.multiple_of(column * tile_order, tile_order), tile_order)
    both = w_ref[0].reshape(2 * w_ref.shape[2], tile_order)
    block = product(both, p_high[rows, :], p_low[rows, :])
    first, second = outs
    half_cols = block_cols // 2

    @pl.when(step < half_cols)
    def _():
        first[...] = block

    @pl.when(step >= half_cols)
    def _():
        second[...] = block


def right_products(given, me, row_partner, col_partner, w, shards, shard_places):
    block_cols, _, height, tile_order = w.shape
    half_cols = block_cols // 2
    depth, width = shards[0][0].shape
    groups = [len(shard) for shard in shards]

    def w_at(i, *tables):
        return column_of(given, block_cols, i, *tables), 0, 0, 0

    def out_spec(first):
        return pl.BlockSpec(
            (height, width), lambda i, *_: (0, jnp.clip(i - first, 0, half_cols - 1))
        )

    out = jax.ShapeDtypeStruct((height, half_cols * width), F32)
    whole = pl.BlockSpec(memory_space=pltpu.VMEM)
    return pl.pallas_call(
        functools.partial(right_kernel, given, block_cols, shard_places, groups),
        grid_spec=pltpu.PrefetchScalarGridSpec(
            num_scalar_prefetch=3,
            grid=(block_cols,),
            in_specs=[pl.BlockSpec((1, 2, height, tile_order), w_at)] + [whole] * sum(groups),
            out_specs=[out_spec(0), out_spec(half_cols)],
            scratch_shapes=[pltpu.VMEM((len(shards) * depth, width), BF16)] * 2,
        ),
        out_shape=[out, out],
        compiler_params=PARAMS,
        cost_estimate=pl.CostEstimate(
            flops=6 * block_cols * height * width * tile_order,
            bytes_accessed=4 * block_cols * height * (tile_order + width),
            transcendentals=0,
        ),
        name="right_products",
    )(me, row_partner, col_partner, w, *[piece for shard in shards for piece in shard])


def sum_kernel(mate, kept_ref, received_ref, section_ref, out):
    out[...] = (kept_ref[...] + received_ref[...]) + section_ref[0]


def sum_sections(col_mate, kept, received, sections):
    height, width = kept.shape
    steps = 4 if height % 32 == 0 else 1
    rows = height // steps
    block = pl.BlockSpec((rows, width), lambda i, _: (i, 0))
    return pl.pallas_call(
        sum_kernel,
        grid_spec=pltpu.PrefetchScalarGridSpec(
            num_scalar_prefetch=1,
            grid=(steps,),
            in_specs=[block, block, pl.BlockSpec((1, rows, width), lambda i, mate: (mate[0], i, 0))],
            out_specs=block,
        ),
        out_shape=jax.ShapeDtypeStruct(kept.shape, F32),
        compiler_params=PARAMS,
        name="sum_sections",
    )(col_mate.reshape(1), kept, received, sections)


def flip(value, axis, size, mask):
    return lax.ppermute(value, axis, [(i, i ^ mask) for i in range(size)])


def gather_prolong(shard, axis, size):
    if size != 4:
        gathered = lax.all_gather(shard, axis)
        return [[gathered[i]] for i in range(size)], lambda me: list(range(size))
    mate = flip(shard, axis, size, 1)
    over = lax.ppermute(shard, axis, [(1, 2), (2, 1)])
    mate_over = lax.ppermute(mate, axis, [(1, 2), (2, 1)])
    handed = lax.ppermute(over, axis, [(1, 0), (2, 3)])
    mate_handed = lax.ppermute(mate, axis, [(2, 0), (1, 3)])

    def places(me):
        row = me[0]
        return [row, row ^ 1, jnp.where(row < 2, 2, 1), jnp.where(row < 2, 3, 0)]

    return [[shard], [mate], [over, handed], [mate_over, mate_handed]], places


def pair_switch(mine, mate, size, branch, operand):
    if size == 2:
        return branch(1, operand)
    branches = [functools.partial(branch, mask) for mask in range(1, size)]
    return lax.switch((mine ^ mate) - 1, branches, operand)


def solution(mesh):
    n_row = mesh.shape["row"]
    n_col = mesh.shape["col"]

    def body(tiles, coords, counts, restrict, prolong, row_partner, col_partner):
        tile_order = tiles.shape[1]
        block_rows = restrict.shape[0] * n_col // tile_order
        block_cols = prolong.shape[0] * n_row // tile_order
        half_rows, half_cols = block_rows // 2, block_cols // 2
        row = lax.axis_index("row").astype(jnp.int32)
        col = lax.axis_index("col").astype(jnp.int32)
        me = jnp.stack([row, col])

        q_rows = lax.all_gather(restrict, "col", axis=0, tiled=True)
        shards, shard_places = gather_prolong(prolong, "row", n_row)

        slot_ids = jnp.arange(tiles.shape[0], dtype=jnp.int32)
        place_ids = jnp.arange(block_rows * block_cols, dtype=jnp.int32)
        named = (coords[:, 0] * block_cols + coords[:, 1])[None, :] == place_ids[:, None]
        hit = named & (slot_ids < counts[0])[None, :]
        slots = jnp.max(jnp.where(hit, slot_ids[None, :], -1), axis=1)

        def half_grid(given):
            w = left_products(given, me, slots, row_partner, tiles, q_rows, half_rows, block_cols)
            return right_products(given, me, row_partner, col_partner, w, shards, shard_places)

        def swap(mask, chunk):
            return flip(chunk, "row", n_row, mask)

        def swap_first(mask, chunk):
            return flip(chunk, "row", n_row, mask), half_grid(False)

        row_mate = row_partner[col, row]
        col_mate = col_partner[row, col]
        given = half_grid(True)
        received, kept = pair_switch(row, row_mate, n_row, swap_first, given[0])
        section = kept[0] + received
        sections = lax.all_gather(section, "col")
        chunk, _ = lax.optimization_barrier((given[1], section))
        received = pair_switch(row, row_mate, n_row, swap, chunk)
        return sum_sections(col_mate, kept[1], received, sections)

    in_specs = (
        P(("row", "col"), None, None),
        P(("row", "col"), None),
        P(("row", "col")),
        P(("row", "col"), None),
        P(("col", "row"), None),
        P(),
        P(),
    )
    return jax.shard_map(
        body, mesh=mesh, in_specs=in_specs, out_specs=P("row", "col"), check_vma=False
    )
```

```python
import functools

import jax
import jax.numpy as jnp
from jax import lax
from jax.experimental import pallas as pl
from jax.experimental.pallas import tpu as pltpu
from jax.sharding import PartitionSpec as P

F32 = jnp.float32
BF16 = jnp.bfloat16
VMEM_BYTES = 48 * 1024 * 1024
PARAMS = pltpu.CompilerParams(vmem_limit_bytes=VMEM_BYTES)


def split(value):
    high = value.astype(BF16)
    low = (value - high.astype(F32)).astype(BF16)
    return high, low


def dot(left, right):
    return jnp.dot(left, right, preferred_element_type=F32)


def product(left_both, right_high, right_low):
    half = left_both.shape[0] // 2
    total = dot(left_both[half:], right_high)
    total = total + dot(left_both[:half], right_low)
    return total + dot(left_both[:half], right_high)


def div(value, by):
    return lax.div(value, jnp.int32(by))


def rem(value, by):
    return lax.rem(value, jnp.int32(by))


def half_of(given, me, row_partner):
    mate = row_partner[me[1], me[0]]
    return ((mate > me[0]) if given else (me[0] > mate)).astype(jnp.int32)


def left_kernel(given, half_rows, block_cols, per_step, *refs):
    me, slots, row_partner, q_ref = refs[:4]
    tile_refs = refs[4 : 4 + per_step]
    out, q_both = refs[4 + per_step :]
    group, step = pl.program_id(0), pl.program_id(1)
    width = q_both.shape[0] // 2

    @pl.when(step == 0)
    def _():
        high, low = split(q_ref[...].T)
        q_both[:width] = high
        q_both[width:] = low

    block_row = half_of(given, me, row_partner) * half_rows + group
    for index, tile_ref in enumerate(tile_refs):
        live = slots[block_row * block_cols + step * per_step + index] >= 0
        high, low = split(tile_ref[0])
        total = jnp.where(live, product(q_both[...], high, low), 0.0)
        out[index, 0], out[index, 1] = split(total)


def left_products(given, me, slots, row_partner, tiles, q_rows, half_rows, block_cols):
    _, tile_order, _ = tiles.shape
    width = q_rows.shape[1]
    per_step = 2 if block_cols % 2 == 0 else 1

    def row_of(g, me, row_partner):
        return half_of(given, me, row_partner) * half_rows + g

    def tile_spec(index):
        def tile_at(g, b, me, slots, row_partner):
            place = row_of(g, me, row_partner) * block_cols + b * per_step + index
            return jnp.maximum(slots[place], 0), 0, 0

        return pl.BlockSpec((1, tile_order, tile_order), tile_at)

    return pl.pallas_call(
        functools.partial(left_kernel, given, half_rows, block_cols, per_step),
        grid_spec=pltpu.PrefetchScalarGridSpec(
            num_scalar_prefetch=3,
            grid=(half_rows, block_cols // per_step),
            in_specs=[
                pl.BlockSpec(
                    (tile_order, width),
                    lambda g, b, me, slots, row_partner: (row_of(g, me, row_partner), 0),
                )
            ]
            + [tile_spec(index) for index in range(per_step)],
            out_specs=pl.BlockSpec(
                (per_step, 2, width, tile_order), lambda g, b, *_: (b, 0, g, 0)
            ),
            scratch_shapes=[pltpu.VMEM((2 * width, tile_order), BF16)],
        ),
        out_shape=jax.ShapeDtypeStruct((block_cols, 2, half_rows * width, tile_order), BF16),
        compiler_params=PARAMS,
        cost_estimate=pl.CostEstimate(
            flops=12 * half_rows * block_cols * width * tile_order * tile_order,
            bytes_accessed=4 * half_rows * block_cols * tile_order * (tile_order + width),
            transcendentals=0,
        ),
        name="left_products",
    )(me, slots, row_partner, q_rows, *[tiles] * per_step)


def column_of(given, block_cols, step, me, row_partner, col_partner):
    row, col = me[0], me[1]
    holder = row_partner[col, row] if given else row
    keeps = col > col_partner[holder, col]
    half_cols = block_cols // 2
    later = div(step, half_cols)
    return jnp.where(keeps, later, 1 - later) * half_cols + rem(step, half_cols)


def live_blocks(given, half_rows, block_cols, me, table, row_partner, col_partner):
    first = half_of(given, me, row_partner) * half_rows
    flags = []
    for step in range(block_cols):
        column = column_of(given, block_cols, jnp.int32(step), me, row_partner, col_partner)
        for block_row in range(half_rows):
            slot = table((first + block_row) * block_cols + column)
            flags.append((slot >= 0).astype(jnp.int32))
    return flags


def packed_place(flags, block):
    before = here = jnp.int32(0)
    for index, flag in enumerate(flags):
        before = before + jnp.where(index < block, flag, 0)
        here = here + jnp.where(index == block, flag, 0)
    return jnp.where(here == 1, before, sum(flags) + block - before), here


def right_kernel(given, block_cols, half_rows, shard_places, groups, *refs):
    me, slots, row_partner, col_partner, w_ref = refs[:5]
    pieces = refs[5 : 5 + sum(groups)]
    p_high, p_low = refs[-2:]
    step = pl.program_id(0)
    tile_order = w_ref.shape[3]
    depth, width = pieces[0].shape

    @pl.when(step == 0)
    def _():
        at = 0
        for place, count in zip(shard_places(me), groups):
            value = pieces[at][...]
            for other in range(1, count):
                value = value + pieces[at + other][...]
            at += count
            rows = pl.ds(pl.multiple_of(place * depth, depth), depth)
            p_high[rows, :], p_low[rows, :] = split(value)

    column = column_of(given, block_cols, step, me, row_partner, col_partner)
    rows = pl.ds(pl.multiple_of(column * tile_order, tile_order), tile_order)
    both = w_ref[0].reshape(2 * w_ref.shape[2], tile_order)
    block = product(both, p_high[rows, :], p_low[rows, :])
    if not given:
        first, second = refs[5 + sum(groups) : -2]
        half_cols = block_cols // 2

        @pl.when(step < half_cols)
        def _():
            first[...] = block

        @pl.when(step >= half_cols)
        def _():
            second[...] = block

        return
    outs = refs[5 + sum(groups) : -3]
    packed = refs[-3]
    flags = live_blocks(
        given, half_rows, block_cols, me, lambda place: slots[place], row_partner, col_partner
    )
    for block_row in range(half_rows):
        place, _ = packed_place(flags, step * half_rows + block_row)
        packed[place] = block[block_row * width : (block_row + 1) * width]

    @pl.when(step == block_cols - 1)
    def _():
        count = outs[0].shape[0]
        outs[0][...] = packed[:count]
        for index, out in enumerate(outs[1:]):
            out[...] = packed[count + index]


def right_products(given, me, slots, row_partner, col_partner, w, shards, shard_places, half_rows):
    block_cols, _, height, tile_order = w.shape
    half_cols = block_cols // 2
    depth, width = shards[0][0].shape
    groups = [len(shard) for shard in shards]
    blocks = half_rows * block_cols

    def w_at(i, me, slots, row_partner, col_partner):
        return column_of(given, block_cols, i, me, row_partner, col_partner), 0, 0, 0

    def out_spec(first):
        return pl.BlockSpec(
            (height, width), lambda i, *_: (0, jnp.clip(i - first, 0, half_cols - 1))
        )

    scratch = [pltpu.VMEM((len(shards) * depth, width), BF16)] * 2
    if given:
        shapes = [(blocks // 2, width, width)] + [(width, width)] * (blocks - blocks // 2)
        out_specs = [pl.BlockSpec(shape, lambda i, *_, n=len(shape): (0,) * n) for shape in shapes]
        scratch = [pltpu.VMEM((blocks, width, width), F32)] + scratch
    else:
        shapes = [(height, half_cols * width)] * 2
        out_specs = [out_spec(0), out_spec(half_cols)]
    whole = pl.BlockSpec(memory_space=pltpu.VMEM)
    return pl.pallas_call(
        functools.partial(right_kernel, given, block_cols, half_rows, shard_places, groups),
        grid_spec=pltpu.PrefetchScalarGridSpec(
            num_scalar_prefetch=4,
            grid=(block_cols,),
            in_specs=[pl.BlockSpec((1, 2, height, tile_order), w_at)] + [whole] * sum(groups),
            out_specs=out_specs,
            scratch_shapes=scratch,
        ),
        out_shape=[jax.ShapeDtypeStruct(shape, F32) for shape in shapes],
        compiler_params=PARAMS,
        cost_estimate=pl.CostEstimate(
            flops=6 * block_cols * height * width * tile_order,
            bytes_accessed=4 * block_cols * height * (tile_order + width),
            transcendentals=0,
        ),
        name="right_products",
    )(me, slots, row_partner, col_partner, w, *[piece for shard in shards for piece in shard])


def sum_kernel(source, first, *refs):
    tables, kept_ref, packed_ref = refs[:4], refs[4], refs[5]
    singles, out = refs[6 : 6 + source.singles], refs[-1]
    place, live = source.place(first + pl.program_id(0), *tables)
    total = kept_ref[...]
    if len(refs) > 7 + source.singles:
        total = total + refs[-2][...]
    out[...] = total + jnp.where((live == 1) & (place < source.packed), packed_ref[0], 0.0)
    for index, single in enumerate(singles):

        @pl.when((live == 1) & (place == source.packed + index))
        def _():
            out[...] = total + single[...]


class PackedSource:
    def __init__(self, half_rows, block_cols):
        self.half_rows = half_rows
        self.block_cols = block_cols
        blocks = half_rows * block_cols
        self.packed = blocks // 2
        self.singles = blocks - self.packed

    def place(self, block, me, mate_slots, row_partner, col_partner):
        flags = live_blocks(
            False,
            self.half_rows,
            self.block_cols,
            me,
            lambda place: mate_slots[place],
            row_partner,
            col_partner,
        )
        return packed_place(flags, block)


def sum_blocks(second, tables, source, kept, packed, singles, section=None):
    height, both = kept.shape
    width = packed.shape[1]
    half_rows, half_cols = source.half_rows, source.block_cols // 2
    first = half_rows * half_cols if second else 0

    def packed_at(i, *tables):
        place, _ = source.place(first + i, *tables)
        return jnp.minimum(place, source.packed - 1), 0, 0

    block = pl.BlockSpec(
        (width, width), lambda i, *_: (rem(i, half_rows), div(i, half_rows))
    )
    sections = [] if section is None else [section]
    return pl.pallas_call(
        functools.partial(sum_kernel, source, first),
        grid_spec=pltpu.PrefetchScalarGridSpec(
            num_scalar_prefetch=4,
            grid=(half_rows * half_cols,),
            in_specs=[block, pl.BlockSpec((1, width, width), packed_at)]
            + [pl.BlockSpec(memory_space=pltpu.VMEM)] * len(singles)
            + [block] * len(sections),
            out_specs=block,
        ),
        out_shape=jax.ShapeDtypeStruct((height, both), F32),
        compiler_params=PARAMS,
        name="sum_blocks",
    )(*tables, kept, packed, *singles, *sections)


def flip(value, axis, size, mask):
    return lax.ppermute(value, axis, [(i, i ^ mask) for i in range(size)])


def gather_prolong(shard, axis, size):
    if size != 4:
        gathered = lax.all_gather(shard, axis)
        return [[gathered[i]] for i in range(size)], lambda me: list(range(size))
    by_two = flip(shard, axis, size, 2)
    by_one = flip(shard, axis, size, 1)
    middle = lax.ppermute(shard, axis, [(1, 2), (2, 1)])
    handed = lax.ppermute(by_two, axis, [(1, 0), (2, 3)])
    return [[shard], [by_one], [by_two], [middle, handed]], lambda me: [me[0] ^ m for m in range(4)]


def pair_switch(mine, mate, size, branch, operand, sizes=(None,), choice=0):
    branches = [functools.partial(branch, mask, each) for mask in range(1, size) for each in sizes]
    if len(branches) == 1:
        return branches[0](operand)
    return lax.switch(((mine ^ mate) - 1) * len(sizes) + choice, branches, operand)


def solution(mesh):
    n_row = mesh.shape["row"]
    n_col = mesh.shape["col"]

    def body(tiles, coords, counts, restrict, prolong, row_partner, col_partner):
        tile_order = tiles.shape[1]
        block_rows = restrict.shape[0] * n_col // tile_order
        block_cols = prolong.shape[0] * n_row // tile_order
        half_rows, half_cols = block_rows // 2, block_cols // 2
        row = lax.axis_index("row").astype(jnp.int32)
        col = lax.axis_index("col").astype(jnp.int32)
        me = jnp.stack([row, col])

        q_rows = lax.all_gather(restrict, "col", axis=0, tiled=True)
        shards, shard_places = gather_prolong(prolong, "row", n_row)

        slot_ids = jnp.arange(tiles.shape[0], dtype=jnp.int32)
        place_ids = jnp.arange(block_rows * block_cols, dtype=jnp.int32)
        named = (coords[:, 0] * block_cols + coords[:, 1])[None, :] == place_ids[:, None]
        hit = named & (slot_ids < counts[0])[None, :]
        slots = jnp.max(jnp.where(hit, slot_ids[None, :], -1), axis=1)

        def half_grid(given):
            w = left_products(given, me, slots, row_partner, tiles, q_rows, half_rows, block_cols)
            return right_products(
                given, me, slots, row_partner, col_partner, w, shards, shard_places, half_rows
            )

        def swap(mask, _, chunk):
            return flip(chunk, "row", n_row, mask)

        def swap_first(mask, _, chunk):
            return flip(chunk, "row", n_row, mask), half_grid(False)

        def swap_some(mask, count, singles):
            return [
                flip(single, "row", n_row, mask) if index < count else single
                for index, single in enumerate(singles)
            ]

        def swap_section(mask, _, section):
            return flip(section, "col", n_col, mask)

        row_mate = row_partner[col, row]
        col_mate = col_partner[row, col]

        mate_slots = pair_switch(row, row_mate, n_row, swap, slots)
        upper = place_ids >= half_rows * block_cols
        mine = (slots >= 0) & (upper == (row < row_mate))
        mates = (mate_slots >= 0) & (upper == (row > row_mate))
        most = jnp.maximum(mine.astype(jnp.int32).sum(), mates.astype(jnp.int32).sum())
        extra = jnp.maximum(most - (half_rows * block_cols) // 2, 0)

        packed, *singles = half_grid(True)

        packed, extra = lax.optimization_barrier((packed, extra))
        packed, kept = pair_switch(row, row_mate, n_row, swap_first, packed)
        counts = tuple(range(len(singles) + 1))
        singles, packed = lax.optimization_barrier((singles, packed))
        singles = pair_switch(row, row_mate, n_row, swap_some, singles, counts, extra)
        tables = (me, mate_slots, row_partner, col_partner)
        source = PackedSource(half_rows, block_cols)
        section = sum_blocks(False, tables, source, kept[0], packed, singles)
        section = pair_switch(col, col_mate, n_col, swap_section, section)
        return sum_blocks(True, tables, source, kept[1], packed, singles, section)

    in_specs = (
        P(("row", "col"), None, None),
        P(("row", "col"), None),
        P(("row", "col")),
        P(("row", "col"), None),
        P(("col", "row"), None),
        P(),
        P(),
    )
    return jax.shard_map(
        body, mesh=mesh, in_specs=in_specs, out_specs=P("row", "col"), check_vma=False
    )
```

```python
import functools

import jax
import jax.numpy as jnp
from jax import lax
from jax.experimental import pallas as pl
from jax.experimental.pallas import tpu as pltpu
from jax.sharding import PartitionSpec as P

F32 = jnp.float32
BF16 = jnp.bfloat16
VMEM_BYTES = 48 * 1024 * 1024
PARAMS = pltpu.CompilerParams(vmem_limit_bytes=VMEM_BYTES)


def split(value):
    high = value.astype(BF16)
    low = (value - high.astype(F32)).astype(BF16)
    return high, low


def dot(left, right):
    return jnp.dot(left, right, preferred_element_type=F32)


def product(left_both, right_high, right_low):
    half = left_both.shape[0] // 2
    total = dot(left_both[half:], right_high)
    total = total + dot(left_both[:half], right_low)
    return total + dot(left_both[:half], right_high)


def div(value, by):
    return lax.div(value, jnp.int32(by))


def rem(value, by):
    return lax.rem(value, jnp.int32(by))


def half_of(given, me, row_partner):
    mate = row_partner[me[1], me[0]]
    return ((mate > me[0]) if given else (me[0] > mate)).astype(jnp.int32)


def left_kernel(given, half_rows, block_cols, per_step, *refs):
    me, slots, row_partner, q_ref = refs[:4]
    tile_refs = refs[4 : 4 + per_step]
    out, q_both = refs[4 + per_step :]
    group, step = pl.program_id(0), pl.program_id(1)
    width = q_both.shape[0] // 2

    @pl.when(step == 0)
    def _():
        high, low = split(q_ref[...].T)
        q_both[:width] = high
        q_both[width:] = low

    block_row = half_of(given, me, row_partner) * half_rows + group
    for index, tile_ref in enumerate(tile_refs):
        live = slots[block_row * block_cols + step * per_step + index] >= 0
        high, low = split(tile_ref[0])
        total = jnp.where(live, product(q_both[...], high, low), 0.0)
        out[index, 0], out[index, 1] = split(total)


def left_products(given, me, slots, row_partner, tiles, q_rows, half_rows, block_cols):
    _, tile_order, _ = tiles.shape
    width = q_rows.shape[1]
    per_step = 2 if block_cols % 2 == 0 else 1

    def row_of(g, me, row_partner):
        return half_of(given, me, row_partner) * half_rows + g

    def tile_spec(index):
        def tile_at(g, b, me, slots, row_partner):
            place = row_of(g, me, row_partner) * block_cols + b * per_step + index
            return jnp.maximum(slots[place], 0), 0, 0

        return pl.BlockSpec((1, tile_order, tile_order), tile_at)

    return pl.pallas_call(
        functools.partial(left_kernel, given, half_rows, block_cols, per_step),
        grid_spec=pltpu.PrefetchScalarGridSpec(
            num_scalar_prefetch=3,
            grid=(half_rows, block_cols // per_step),
            in_specs=[
                pl.BlockSpec(
                    (tile_order, width),
                    lambda g, b, me, slots, row_partner: (row_of(g, me, row_partner), 0),
                )
            ]
            + [tile_spec(index) for index in range(per_step)],
            out_specs=pl.BlockSpec(
                (per_step, 2, width, tile_order), lambda g, b, *_: (b, 0, g, 0)
            ),
            scratch_shapes=[pltpu.VMEM((2 * width, tile_order), BF16)],
        ),
        out_shape=jax.ShapeDtypeStruct((block_cols, 2, half_rows * width, tile_order), BF16),
        compiler_params=PARAMS,
        cost_estimate=pl.CostEstimate(
            flops=12 * half_rows * block_cols * width * tile_order * tile_order,
            bytes_accessed=4 * half_rows * block_cols * tile_order * (tile_order + width),
            transcendentals=0,
        ),
        name="left_products",
    )(me, slots, row_partner, q_rows, *[tiles] * per_step)


def column_of(given, block_cols, step, me, row_partner, col_partner):
    row, col = me[0], me[1]
    holder = row_partner[col, row] if given else row
    keeps = col > col_partner[holder, col]
    half_cols = block_cols // 2
    later = div(step, half_cols)
    return jnp.where(keeps, later, 1 - later) * half_cols + rem(step, half_cols)


def live_blocks(given, half_rows, block_cols, me, table, row_partner, col_partner):
    first = half_of(given, me, row_partner) * half_rows
    flags = []
    for step in range(block_cols):
        column = column_of(given, block_cols, jnp.int32(step), me, row_partner, col_partner)
        for block_row in range(half_rows):
            slot = table((first + block_row) * block_cols + column)
            flags.append((slot >= 0).astype(jnp.int32))
    return flags


def packed_place(flags, block):
    before = here = jnp.int32(0)
    for index, flag in enumerate(flags):
        before = before + jnp.where(index < block, flag, 0)
        here = here + jnp.where(index == block, flag, 0)
    return jnp.where(here == 1, before, sum(flags) + block - before), here


def right_kernel(given, block_cols, half_rows, shard_places, groups, *refs):
    me, slots, row_partner, col_partner, w_ref = refs[:5]
    pieces = refs[5 : 5 + sum(groups)]
    p_high, p_low = refs[-2:]
    step = pl.program_id(0)
    tile_order = w_ref.shape[3]
    depth, width = pieces[0].shape

    @pl.when(step == 0)
    def _():
        at = 0
        for place, count in zip(shard_places(me), groups):
            value = pieces[at][...]
            for other in range(1, count):
                value = value + pieces[at + other][...]
            at += count
            rows = pl.ds(pl.multiple_of(place * depth, depth), depth)
            p_high[rows, :], p_low[rows, :] = split(value)

    column = column_of(given, block_cols, step, me, row_partner, col_partner)
    rows = pl.ds(pl.multiple_of(column * tile_order, tile_order), tile_order)
    both = w_ref[0].reshape(2 * w_ref.shape[2], tile_order)
    block = product(both, p_high[rows, :], p_low[rows, :])
    if not given:
        first, second = refs[5 + sum(groups) : -2]
        half_cols = block_cols // 2

        @pl.when(step < half_cols)
        def _():
            first[...] = block

        @pl.when(step >= half_cols)
        def _():
            second[...] = block

        return
    outs = refs[5 + sum(groups) : -3]
    packed = refs[-3]
    flags = live_blocks(
        given, half_rows, block_cols, me, lambda place: slots[place], row_partner, col_partner
    )
    for block_row in range(half_rows):
        place, _ = packed_place(flags, step * half_rows + block_row)
        packed[place] = block[block_row * width : (block_row + 1) * width]

    @pl.when(step == block_cols - 1)
    def _():
        count = outs[0].shape[0]
        outs[0][...] = packed[:count]
        for index, out in enumerate(outs[1:]):
            out[...] = packed[count + index]


def right_products(given, me, slots, row_partner, col_partner, w, shards, shard_places, half_rows):
    block_cols, _, height, tile_order = w.shape
    half_cols = block_cols // 2
    depth, width = shards[0][0].shape
    groups = [len(shard) for shard in shards]
    blocks = half_rows * block_cols

    def w_at(i, me, slots, row_partner, col_partner):
        return column_of(given, block_cols, i, me, row_partner, col_partner), 0, 0, 0

    def out_spec(first):
        return pl.BlockSpec(
            (height, width), lambda i, *_: (0, jnp.clip(i - first, 0, half_cols - 1))
        )

    scratch = [pltpu.VMEM((len(shards) * depth, width), BF16)] * 2
    if given:
        shapes = [(blocks // 2, width, width)] + [(width, width)] * (blocks - blocks // 2)
        out_specs = [pl.BlockSpec(shape, lambda i, *_, n=len(shape): (0,) * n) for shape in shapes]
        scratch = [pltpu.VMEM((blocks, width, width), F32)] + scratch
    else:
        shapes = [(height, half_cols * width)] * 2
        out_specs = [out_spec(0), out_spec(half_cols)]
    whole = pl.BlockSpec(memory_space=pltpu.VMEM)
    return pl.pallas_call(
        functools.partial(right_kernel, given, block_cols, half_rows, shard_places, groups),
        grid_spec=pltpu.PrefetchScalarGridSpec(
            num_scalar_prefetch=4,
            grid=(block_cols,),
            in_specs=[pl.BlockSpec((1, 2, height, tile_order), w_at)] + [whole] * sum(groups),
            out_specs=out_specs,
            scratch_shapes=scratch,
        ),
        out_shape=[jax.ShapeDtypeStruct(shape, F32) for shape in shapes],
        compiler_params=PARAMS,
        cost_estimate=pl.CostEstimate(
            flops=6 * block_cols * height * width * tile_order,
            bytes_accessed=4 * block_cols * height * (tile_order + width),
            transcendentals=0,
        ),
        name="right_products",
    )(me, slots, row_partner, col_partner, w, *[piece for shard in shards for piece in shard])


def sum_kernel(source, first, singles, *refs):
    tables, kept_ref, packed_ref = refs[:4], refs[4], refs[5]
    singles, sections, out = refs[6 : 6 + singles], refs[6 + singles : -1], refs[-1]
    place, live = source.place(first + pl.program_id(0), *tables)
    total = kept_ref[...]
    for section in sections:
        total = total + section[...]
    out[...] = total + jnp.where((live == 1) & (place < source.packed), packed_ref[0], 0.0)
    for index, single in enumerate(singles):

        @pl.when((live == 1) & (place == source.packed + index))
        def _():
            out[...] = total + single[...]


class PackedSource:
    def __init__(self, half_rows, block_cols):
        self.half_rows = half_rows
        self.block_cols = block_cols
        self.packed = half_rows * block_cols // 2

    def place(self, block, me, mate_slots, row_partner, col_partner):
        flags = live_blocks(
            False,
            self.half_rows,
            self.block_cols,
            me,
            lambda place: mate_slots[place],
            row_partner,
            col_partner,
        )
        return packed_place(flags, block)


def sum_blocks(second, tables, source, kept, packed, singles, section=None):
    height, both = kept.shape
    width = packed.shape[1]
    half_rows, half_cols = source.half_rows, source.block_cols // 2
    first = half_rows * half_cols if second else 0

    def packed_at(i, *tables):
        place, _ = source.place(first + i, *tables)
        return jnp.minimum(place, source.packed - 1), 0, 0

    block = pl.BlockSpec(
        (width, width), lambda i, *_: (rem(i, half_rows), div(i, half_rows))
    )
    sections = [] if section is None else [section]
    return pl.pallas_call(
        functools.partial(sum_kernel, source, first, len(singles)),
        grid_spec=pltpu.PrefetchScalarGridSpec(
            num_scalar_prefetch=4,
            grid=(half_rows * half_cols,),
            in_specs=[block, pl.BlockSpec((1, width, width), packed_at)]
            + [pl.BlockSpec(memory_space=pltpu.VMEM)] * len(singles)
            + [block] * len(sections),
            out_specs=block,
        ),
        out_shape=jax.ShapeDtypeStruct((height, both), F32),
        compiler_params=PARAMS,
        name="sum_blocks",
    )(*tables, kept, packed, *singles, *sections)


def flip(value, axis, size, mask):
    return lax.ppermute(value, axis, [(i, i ^ mask) for i in range(size)])


def gather_prolong(shard, axis, size):
    if size != 4:
        gathered = lax.all_gather(shard, axis)
        return [[gathered[i]] for i in range(size)], lambda me: list(range(size))
    by_two = flip(shard, axis, size, 2)
    by_one = flip(shard, axis, size, 1)
    middle = lax.ppermute(shard, axis, [(1, 2), (2, 1)])
    handed = lax.ppermute(by_two, axis, [(1, 0), (2, 3)])
    return [[shard], [by_one], [by_two], [middle, handed]], lambda me: [me[0] ^ m for m in range(4)]


def pair_switch(mine, mate, size, branch, operand, sizes=(None,), choice=0):
    branches = [functools.partial(branch, mask, each) for mask in range(1, size) for each in sizes]
    if len(branches) == 1:
        return branches[0](operand)
    return lax.switch(((mine ^ mate) - 1) * len(sizes) + choice, branches, operand)


def solution(mesh):
    n_row = mesh.shape["row"]
    n_col = mesh.shape["col"]

    def body(tiles, coords, counts, restrict, prolong, row_partner, col_partner):
        tile_order = tiles.shape[1]
        block_rows = restrict.shape[0] * n_col // tile_order
        block_cols = prolong.shape[0] * n_row // tile_order
        half_rows, half_cols = block_rows // 2, block_cols // 2
        row = lax.axis_index("row").astype(jnp.int32)
        col = lax.axis_index("col").astype(jnp.int32)
        me = jnp.stack([row, col])

        q_rows = lax.all_gather(restrict, "col", axis=0, tiled=True)
        shards, shard_places = gather_prolong(prolong, "row", n_row)

        slot_ids = jnp.arange(tiles.shape[0], dtype=jnp.int32)
        place_ids = jnp.arange(block_rows * block_cols, dtype=jnp.int32)
        named = (coords[:, 0] * block_cols + coords[:, 1])[None, :] == place_ids[:, None]
        hit = named & (slot_ids < counts[0])[None, :]
        slots = jnp.max(jnp.where(hit, slot_ids[None, :], -1), axis=1)

        def half_grid(given):
            w = left_products(given, me, slots, row_partner, tiles, q_rows, half_rows, block_cols)
            return right_products(
                given, me, slots, row_partner, col_partner, w, shards, shard_places, half_rows
            )

        def swap_first(mask, _, operands):
            packed, slots = operands
            packed = flip(packed, "row", n_row, mask)
            mate_slots = flip(slots, "row", n_row, mask)
            upper = place_ids >= half_rows * block_cols
            mine = (slots >= 0) & (upper == (row < row_mate))
            mates = (mate_slots >= 0) & (upper == (row > row_mate))
            most = jnp.maximum(mine.astype(jnp.int32).sum(), mates.astype(jnp.int32).sum())
            return packed, mate_slots, jnp.maximum(most - packed.shape[0], 0), half_grid(False)

        def swap_some(mask, count, singles):
            return [
                flip(single, "row", n_row, mask) if index < count else single
                for index, single in enumerate(singles)
            ]

        def swap_section(mask, _, section):
            return flip(section, "col", n_col, mask)

        row_mate = row_partner[col, row]
        col_mate = col_partner[row, col]

        packed, *singles = half_grid(True)
        packed, mate_slots, extra, kept = pair_switch(
            row, row_mate, n_row, swap_first, (packed, slots)
        )
        tables = (me, mate_slots, row_partner, col_partner)
        source = PackedSource(half_rows, block_cols)
        section = sum_blocks(False, tables, source, kept[0], packed, [])
        section = pair_switch(col, col_mate, n_col, swap_section, section)
        singles, section = lax.optimization_barrier((singles, section))
        counts = tuple(range(len(singles) + 1))
        singles = pair_switch(row, row_mate, n_row, swap_some, singles, counts, extra)
        return sum_blocks(True, tables, source, kept[1], packed, singles, section)

    in_specs = (
        P(("row", "col"), None, None),
        P(("row", "col"), None),
        P(("row", "col")),
        P(("row", "col"), None),
        P(("col", "row"), None),
        P(),
        P(),
    )
    return jax.shard_map(
        body, mesh=mesh, in_specs=in_specs, out_specs=P("row", "col"), check_vma=False
    )
```

```python
import functools

import jax
import jax.numpy as jnp
from jax import lax
from jax.experimental import pallas as pl
from jax.experimental.pallas import tpu as pltpu
from jax.sharding import PartitionSpec as P

F32 = jnp.float32
BF16 = jnp.bfloat16
VMEM_BYTES = 48 * 1024 * 1024
PARAMS = pltpu.CompilerParams(vmem_limit_bytes=VMEM_BYTES)


def split(value):
    high = value.astype(BF16)
    low = (value - high.astype(F32)).astype(BF16)
    return high, low


def dot(left, right):
    return jnp.dot(left, right, preferred_element_type=F32)


def product(left_both, right_high, right_low):
    half = left_both.shape[0] // 2
    total = dot(left_both[half:], right_high)
    total = total + dot(left_both[:half], right_low)
    return total + dot(left_both[:half], right_high)


def div(value, by):
    return lax.div(value, jnp.int32(by))


def rem(value, by):
    return lax.rem(value, jnp.int32(by))


def half_of(given, me, row_partner):
    mate = row_partner[me[1], me[0]]
    return ((mate > me[0]) if given else (me[0] > mate)).astype(jnp.int32)


class ChipBlocks:
    def __init__(self, given, pieces):
        self.given = given
        self.operands = pieces
        self.specs = [pl.BlockSpec(memory_space=pltpu.VMEM)] * len(pieces)

    def near(self, me, row_partner):
        return half_of(self.given, me, row_partner) == div(me[1], 4)

    def row_of(self, group, me, row_partner):
        return div(me[1], 2) ^ (jnp.where(self.near(me, row_partner), 0, 2) + group)

    def load(self, group, me, row_partner, refs, put):
        near = self.near(me, row_partner)
        odd = rem(me[1], 2)
        first, second = refs
        for chip in range(first.shape[0]):
            depth = first.shape[1]
            wanted = (group == chip % 2) & (near == (chip < 2))
            for core in range(2):

                @pl.when(wanted & (odd == core))
                def _():
                    put(first[chip], core * depth)
                    put(second[chip], (1 - core) * depth)


class WholeBlocks:
    def __init__(self, given, rows, tile_order, half_rows):
        self.given = given
        self.half_rows = half_rows
        self.operands = [rows]
        self.specs = [
            pl.BlockSpec(
                (tile_order, rows.shape[1]),
                lambda g, b, me, slots, row_partner: (self.row_of(g, me, row_partner), 0),
            )
        ]

    def row_of(self, group, me, row_partner):
        return half_of(self.given, me, row_partner) * self.half_rows + group

    def load(self, group, me, row_partner, refs, put):
        put(refs[0][...], 0)


def left_kernel(blocks, block_cols, per_step, *refs):
    me, slots, row_partner = refs[:3]
    tile_refs = refs[3 : 3 + per_step]
    q_refs = refs[3 + per_step : -2]
    out, q_both = refs[-2:]
    group, step = pl.program_id(0), pl.program_id(1)
    width = q_both.shape[0] // 2

    @pl.when(step == 0)
    def _():
        def put(value, first):
            high, low = split(value.T)
            q_both[:width, first : first + value.shape[0]] = high
            q_both[width:, first : first + value.shape[0]] = low

        blocks.load(group, me, row_partner, q_refs, put)

    block_row = blocks.row_of(group, me, row_partner)
    for index, tile_ref in enumerate(tile_refs):
        live = slots[block_row * block_cols + step * per_step + index] >= 0
        high, low = split(tile_ref[0])
        total = jnp.where(live, product(q_both[...], high, low), 0.0)
        out[index, 0], out[index, 1] = split(total)


def left_products(me, slots, row_partner, tiles, blocks, half_rows, block_cols):
    _, tile_order, _ = tiles.shape
    width = blocks.operands[0].shape[-1]
    per_step = 2 if block_cols % 2 == 0 else 1

    def tile_spec(index):
        def tile_at(g, b, me, slots, row_partner):
            place = blocks.row_of(g, me, row_partner) * block_cols + b * per_step + index
            return jnp.maximum(slots[place], 0), 0, 0

        return pl.BlockSpec((1, tile_order, tile_order), tile_at)

    def out_at(g, b, me, slots, row_partner):
        return b, 0, rem(blocks.row_of(g, me, row_partner), half_rows), 0

    return pl.pallas_call(
        functools.partial(left_kernel, blocks, block_cols, per_step),
        grid_spec=pltpu.PrefetchScalarGridSpec(
            num_scalar_prefetch=3,
            grid=(half_rows, block_cols // per_step),
            in_specs=[tile_spec(index) for index in range(per_step)] + blocks.specs,
            out_specs=pl.BlockSpec((per_step, 2, width, tile_order), out_at),
            scratch_shapes=[pltpu.VMEM((2 * width, tile_order), BF16)],
        ),
        out_shape=jax.ShapeDtypeStruct((block_cols, 2, half_rows * width, tile_order), BF16),
        compiler_params=PARAMS,
        cost_estimate=pl.CostEstimate(
            flops=12 * half_rows * block_cols * width * tile_order * tile_order,
            bytes_accessed=4 * half_rows * block_cols * tile_order * (tile_order + width),
            transcendentals=0,
        ),
        name="left_products",
    )(me, slots, row_partner, *[tiles] * per_step, *blocks.operands)


class Columns:
    OWN, FAR, KEPT = range(3)

    def __init__(self, kind, n_row, block_cols):
        self.kind = kind
        self.n_row = n_row
        self.half_cols = block_cols // 2
        self.steps = block_cols if kind == self.KEPT else self.half_cols

    def side(self, row):
        return div(2 * row, self.n_row)

    def half(self, step, me, col_partner):
        if self.kind == self.KEPT:
            goes_on = (me[1] < col_partner[me[0], me[1]]).astype(jnp.int32)
            return goes_on ^ div(step, self.half_cols)
        return self.side(me[0]) ^ (1 if self.kind == self.FAR else 0)

    def column(self, step, me, col_partner):
        return self.half(step, me, col_partner) * self.half_cols + rem(step, self.half_cols)


def packed_place(slots, first_row, first_col, half_rows, half_cols, block_cols, block):
    before = here = count = jnp.int32(0)
    for index in range(half_rows * half_cols):
        place = (first_row + index % half_rows) * block_cols + first_col + index // half_rows
        flag = (slots[place] >= 0).astype(jnp.int32)
        before = before + jnp.where(index < block, flag, 0)
        here = here + jnp.where(index == block, flag, 0)
        count = count + flag
    return jnp.where(here == 1, before, count + block - before), here == 1


def right_kernel(columns, block_cols, half_rows, shard_places, groups, *refs):
    me, slots, row_partner, col_partner, w_ref = refs[:5]
    pieces = refs[5 : 5 + sum(groups)]
    step = pl.program_id(0)
    tile_order = w_ref.shape[3]
    depth, width = pieces[0].shape
    packs = columns.kind != Columns.KEPT
    outs = refs[5 + sum(groups) : -3 if packs else -2]
    p_high, p_low = refs[-2:]

    @pl.when(step == 0)
    def _():
        at = 0
        for place, count in zip(shard_places(me), groups):
            value = pieces[at][...]
            for other in range(1, count):
                value = value + pieces[at + other][...]
            at += count
            rows = pl.ds(pl.multiple_of(place * depth, depth), depth)
            p_high[rows, :], p_low[rows, :] = split(value)

    column = columns.column(step, me, col_partner)
    rows = pl.ds(pl.multiple_of(column * tile_order, tile_order), tile_order)
    both = w_ref[0].reshape(2 * w_ref.shape[2], tile_order)
    block = product(both, p_high[rows, :], p_low[rows, :])
    half_cols = columns.half_cols
    if not packs:
        first, second = outs

        @pl.when(step < half_cols)
        def _():
            first[...] = block

        @pl.when(step >= half_cols)
        def _():
            second[...] = block

        return
    packed = refs[-3]
    first_row = half_of(True, me, row_partner) * half_rows
    first_col = columns.half(step, me, col_partner) * half_cols
    for row in range(half_rows):
        place, _ = packed_place(
            slots, first_row, first_col, half_rows, half_cols, block_cols, step * half_rows + row
        )
        packed[place] = block[row * width : (row + 1) * width]

    @pl.when(step == half_cols - 1)
    def _():
        count = outs[0].shape[0]
        outs[0][...] = packed[:count]
        for index, out in enumerate(outs[1:]):
            out[...] = packed[count + index]


def right_products(kind, me, slots, row_partner, col_partner, w, shards, shard_places, n_row, half_rows):
    block_cols, _, height, tile_order = w.shape
    columns = Columns(kind, n_row, block_cols)
    half_cols = columns.half_cols
    depth, width = shards[0][0].shape
    groups = [len(shard) for shard in shards]
    blocks = half_rows * half_cols
    p_rows = block_cols * tile_order

    def w_at(i, me, slots, row_partner, col_partner):
        return columns.column(i, me, col_partner), 0, 0, 0

    def quarter(first):
        return pl.BlockSpec(
            (height, width), lambda i, *_: (0, jnp.clip(i - first, 0, half_cols - 1))
        )

    scratch = [pltpu.VMEM((p_rows, width), BF16)] * 2
    if kind == Columns.KEPT:
        shapes = [(height, half_cols * width)] * 2
        out_specs = [quarter(0), quarter(half_cols)]
    else:
        shapes = [(blocks // 2, width, width)] + [(width, width)] * (blocks - blocks // 2)
        out_specs = [pl.BlockSpec(shape, lambda i, *_, n=len(shape): (0,) * n) for shape in shapes]
        scratch = [pltpu.VMEM((blocks, width, width), F32)] + scratch
    return pl.pallas_call(
        functools.partial(right_kernel, columns, block_cols, half_rows, shard_places, groups),
        grid_spec=pltpu.PrefetchScalarGridSpec(
            num_scalar_prefetch=4,
            grid=(columns.steps,),
            in_specs=[pl.BlockSpec((1, 2, height, tile_order), w_at)]
            + [pl.BlockSpec(memory_space=pltpu.VMEM)] * sum(groups),
            out_specs=out_specs,
            scratch_shapes=scratch,
        ),
        out_shape=[jax.ShapeDtypeStruct(shape, F32) for shape in shapes],
        compiler_params=PARAMS,
        cost_estimate=pl.CostEstimate(
            flops=6 * columns.steps * height * width * tile_order,
            bytes_accessed=4 * columns.steps * height * (tile_order + width),
            transcendentals=0,
        ),
        name="right_products",
    )(me, slots, row_partner, col_partner, w, *[piece for shard in shards for piece in shard])


def sum_kernel(columns, second, half_rows, block_cols, arrays, *refs):
    me, mate_slots, row_partner, col_partner, kept_ref = refs[:5]
    chunks = refs[5 : 5 + arrays]
    sections, out = refs[5 + arrays : -1], refs[-1]
    half_cols = columns.half_cols
    first_row = half_of(False, me, row_partner) * half_rows
    half = columns.half(half_cols if second else 0, me, col_partner)
    chunk = columns.side(row_partner[me[1], me[0]]) ^ half
    place, live = packed_place(
        mate_slots, first_row, half * half_cols, half_rows, half_cols, block_cols, pl.program_id(0)
    )
    total = kept_ref[...]
    for section in sections:
        total = total + section[...]

    @pl.when(jnp.logical_not(live))
    def _():
        out[...] = total

    for which in range(2):
        first, *singles = chunks[which * arrays // 2 : (which + 1) * arrays // 2]
        count = first.shape[0]

        @pl.when(live & (chunk == which) & (place < count))
        def _():
            out[...] = total + first[place]

        for index, single in enumerate(singles):

            @pl.when(live & (chunk == which) & (place == count + index))
            def _():
                out[...] = total + single[...]


def sum_blocks(second, tables, n_row, half_rows, block_cols, kept, chunks, section=None):
    columns = Columns(Columns.KEPT, n_row, block_cols)
    half_cols = columns.half_cols
    height, both = kept.shape
    width = both // half_cols
    block = pl.BlockSpec((width, width), lambda i, *_: (rem(i, half_rows), div(i, half_rows)))
    sections = [] if section is None else [section]
    return pl.pallas_call(
        functools.partial(sum_kernel, columns, second, half_rows, block_cols, len(chunks)),
        grid_spec=pltpu.PrefetchScalarGridSpec(
            num_scalar_prefetch=4,
            grid=(half_rows * half_cols,),
            in_specs=[block]
            + [pl.BlockSpec(memory_space=pltpu.VMEM)] * len(chunks)
            + [block] * len(sections),
            out_specs=block,
        ),
        out_shape=jax.ShapeDtypeStruct((height, both), F32),
        compiler_params=PARAMS,
        name="sum_blocks",
    )(*tables, kept, *chunks, *sections)


def flip(value, axis, size, mask):
    return lax.ppermute(value, axis, [(i, i ^ mask) for i in range(size)])


def gather_prolong(shard, axis, size):
    if size != 4:
        gathered = lax.all_gather(shard, axis)
        every = [[gathered[i]] for i in range(size)], lambda me: list(range(size))
        return every, every, lambda shards, _: shards
    by_two = flip(shard, axis, size, 2)
    by_one = flip(shard, axis, size, 1)
    middle = lax.ppermute(shard, axis, [(1, 2), (2, 1)])

    def hand_out(shards, after):
        by_two, _ = lax.optimization_barrier((shards[0][0], after))
        handed = lax.ppermute(by_two, axis, [(1, 0), (2, 3)])
        return [[by_two], [*shards[1], handed]]

    own = [[shard], [by_one]], lambda me: [me[0], me[0] ^ 1]
    far = [[by_two], [middle]], lambda me: [me[0] ^ 2, me[0] ^ 3]
    return own, far, hand_out


def gather_restrict(shard, axis, size):
    over_x = flip(shard, axis, size, 2)
    over_y = flip(shard, axis, size, 4)
    over_both = flip(over_x, axis, size, 4)
    mine = jnp.stack([shard, over_x, over_y, over_both])
    return [mine, flip(mine, axis, size, 1)]


def pair_switch(mine, mate, size, branch, operand, sizes=(None,), choice=0):
    branches = [functools.partial(branch, mask, each) for mask in range(1, size) for each in sizes]
    if len(branches) == 1:
        return branches[0](operand)
    return lax.switch(((mine ^ mate) - 1) * len(sizes) + choice, branches, operand)


def solution(mesh):
    n_row = mesh.shape["row"]
    n_col = mesh.shape["col"]

    def body(tiles, coords, counts, restrict, prolong, row_partner, col_partner):
        tile_order = tiles.shape[1]
        block_rows = restrict.shape[0] * n_col // tile_order
        block_cols = prolong.shape[0] * n_row // tile_order
        half_rows, half_cols = block_rows // 2, block_cols // 2
        row = lax.axis_index("row").astype(jnp.int32)
        col = lax.axis_index("col").astype(jnp.int32)
        me = jnp.stack([row, col])

        row_mate = row_partner[col, row]
        col_mate = col_partner[row, col]

        def swap_tables(mask, _, tables):
            return [flip(table, "row", n_row, mask) for table in tables]

        mate_coords, mate_counts = pair_switch(row, row_mate, n_row, swap_tables, (coords, counts))
        prolong, mate_counts = lax.optimization_barrier((prolong, mate_counts))
        by_chip = n_col == 8 and block_rows == 4 and tile_order == 2 * restrict.shape[0]
        if by_chip:
            q_pieces = gather_restrict(restrict, "col", n_col)
        else:
            q_rows = lax.all_gather(restrict, "col", axis=0, tiled=True)
        own_shards, far_shards, last_step = gather_prolong(prolong, "row", n_row)

        slot_ids = jnp.arange(tiles.shape[0], dtype=jnp.int32)
        place_ids = jnp.arange(block_rows * block_cols, dtype=jnp.int32)

        def slots_of(coords, counts):
            named = (coords[:, 0] * block_cols + coords[:, 1])[None, :] == place_ids[:, None]
            hit = named & (slot_ids < counts[0])[None, :]
            return jnp.max(jnp.where(hit, slot_ids[None, :], -1), axis=1)

        slots = slots_of(coords, counts)
        mate_slots = slots_of(mate_coords, mate_counts)

        def chunk_size(chunk):
            upper_row = place_ids // block_cols >= half_rows
            upper_col = place_ids % block_cols >= half_cols
            far = chunk == 1
            mine = (upper_row == (row < row_mate)) & (upper_col == ((2 * row >= n_row) ^ far))
            mates = (upper_row == (row > row_mate)) & (upper_col == ((2 * row_mate >= n_row) ^ far))
            mine = (mine & (slots >= 0)).astype(jnp.int32).sum()
            return jnp.maximum(mine, (mates & (mate_slots >= 0)).astype(jnp.int32).sum())

        def left(given):
            if by_chip:
                blocks = ChipBlocks(given, q_pieces)
            else:
                blocks = WholeBlocks(given, q_rows, tile_order, half_rows)
            return left_products(me, slots, row_partner, tiles, blocks, half_rows, block_cols)

        def right(kind, w, shards, places):
            return right_products(
                kind, me, slots, row_partner, col_partner, w, shards, places, n_row, half_rows
            )

        def swap_chunk(beside, mask, extra, chunk):
            received = [
                flip(array, "row", n_row, mask) if index <= extra else array
                for index, array in enumerate(chunk)
            ]
            return received, beside()

        def swap_section(mask, _, section):
            return flip(section, "col", n_col, mask)

        def exchange(size, chunk, beside):
            choice = jnp.clip(size - chunk[0].shape[0], 0, len(chunk) - 1)
            branch = functools.partial(swap_chunk, beside)
            return pair_switch(row, row_mate, n_row, branch, chunk, tuple(range(len(chunk))), choice)

        slots, sizes = lax.optimization_barrier((slots, (chunk_size(0), chunk_size(1))))
        w = left(True)
        far_shards = last_step(far_shards[0], w), far_shards[1]
        own = right(Columns.OWN, w, *own_shards)
        own, w_kept = exchange(sizes[0], own, lambda: left(False))
        far_pieces, w, own = lax.optimization_barrier((far_shards[0], w, own))
        far = right(Columns.FAR, w, far_pieces, far_shards[1])
        if n_row == 4:
            every = own_shards[0] + far_pieces, lambda me: own_shards[1](me) + far_shards[1](me)
        else:
            every = own_shards
        far, kept = exchange(sizes[1], far, lambda: right(Columns.KEPT, w_kept, *every))
        chunks = list(own) + list(far)
        add = functools.partial(sum_blocks, n_row=n_row, half_rows=half_rows, block_cols=block_cols)
        tables = (me, mate_slots, row_partner, col_partner)
        section = add(False, tables, kept=kept[0], chunks=chunks)
        section = pair_switch(col, col_mate, n_col, swap_section, section)
        return add(True, tables, kept=kept[1], chunks=chunks, section=section)

    in_specs = (
        P(("row", "col"), None, None),
        P(("row", "col"), None),
        P(("row", "col")),
        P(("row", "col"), None),
        P(("col", "row"), None),
        P(),
        P(),
    )
    return jax.shard_map(
        body, mesh=mesh, in_specs=in_specs, out_specs=P("row", "col"), check_vma=False
    )
```

```python
import functools

import jax
import jax.numpy as jnp
from jax import lax
from jax.experimental import pallas as pl
from jax.experimental.pallas import tpu as pltpu
from jax.sharding import PartitionSpec as P

F32 = jnp.float32
BF16 = jnp.bfloat16
VMEM_BYTES = 48 * 1024 * 1024
PARAMS = pltpu.CompilerParams(vmem_limit_bytes=VMEM_BYTES)


def split(value):
    high = value.astype(BF16)
    low = (value - high.astype(F32)).astype(BF16)
    return high, low


def dot(left, right):
    return jnp.dot(left, right, preferred_element_type=F32)


def product(left_both, right_high, right_low):
    half = left_both.shape[0] // 2
    total = dot(left_both[half:], right_high)
    total = total + dot(left_both[:half], right_low)
    return total + dot(left_both[:half], right_high)


def div(value, by):
    return lax.div(value, jnp.int32(by))


def rem(value, by):
    return lax.rem(value, jnp.int32(by))


def half_of(given, me, row_partner):
    mate = row_partner[me[1], me[0]]
    return ((mate > me[0]) if given else (me[0] > mate)).astype(jnp.int32)


def tables_kernel(n_row, half_rows, block_cols, me, live, row_partner, slots, mate_slots, sizes):
    columns = Columns(Columns.OWN, n_row, block_cols)
    mate = row_partner[me[1], me[0]]
    places = slots.shape[0]
    per_device = live.shape[0] // n_row
    for table, row in ((slots, me[0]), (mate_slots, mate)):
        for place in range(places):
            table[place] = jnp.int32(-1)
        for slot in range(per_device):
            block_row = live[row * per_device + slot, 0]

            @pl.when(block_row >= 0)
            def _():
                table[block_row * block_cols + live[row * per_device + slot, 1]] = jnp.int32(slot)

    half_cols = columns.half_cols
    for chunk in range(2):
        counts = []
        for table, row, given in ((slots, me[0], True), (mate_slots, mate, False)):
            first_row = half_of(given, me, row_partner) * half_rows
            first_col = (columns.side(row) ^ chunk) * half_cols
            count = jnp.int32(0)
            for index in range(half_rows * half_cols):
                place = (first_row + index % half_rows) * block_cols + first_col + index // half_rows
                count = count + (table[place] >= 0).astype(jnp.int32)
            counts.append(count)
        sizes[chunk] = jnp.maximum(*counts)


def make_tables(me, live, row_partner, n_row, half_rows, block_cols):
    smem = pl.BlockSpec(memory_space=pltpu.SMEM)
    places = 2 * half_rows * block_cols
    return pl.pallas_call(
        functools.partial(tables_kernel, n_row, half_rows, block_cols),
        in_specs=[smem] * 3,
        out_specs=[smem] * 3,
        out_shape=[jax.ShapeDtypeStruct((n,), jnp.int32) for n in (places, places, 2)],
        name="make_tables",
    )(me, live, row_partner)


class ChipBlocks:
    def __init__(self, given, pieces):
        self.given = given
        self.operands = pieces
        self.specs = [pl.BlockSpec(memory_space=pltpu.VMEM)] * len(pieces)

    def near(self, me, row_partner):
        return half_of(self.given, me, row_partner) == div(me[1], 4)

    def row_of(self, group, me, row_partner):
        return div(me[1], 2) ^ (jnp.where(self.near(me, row_partner), 0, 2) + group)

    def load(self, group, me, row_partner, refs, put):
        near = self.near(me, row_partner)
        odd = rem(me[1], 2)
        first, second = refs
        for chip in range(first.shape[0]):
            depth = first.shape[1]
            wanted = (group == chip % 2) & (near == (chip < 2))
            for core in range(2):

                @pl.when(wanted & (odd == core))
                def _():
                    put(first[chip], core * depth)
                    put(second[chip], (1 - core) * depth)


class WholeBlocks:
    def __init__(self, given, rows, tile_order, half_rows):
        self.given = given
        self.half_rows = half_rows
        self.operands = [rows]
        self.specs = [
            pl.BlockSpec(
                (tile_order, rows.shape[1]),
                lambda g, b, me, slots, row_partner: (self.row_of(g, me, row_partner), 0),
            )
        ]

    def row_of(self, group, me, row_partner):
        return half_of(self.given, me, row_partner) * self.half_rows + group

    def load(self, group, me, row_partner, refs, put):
        put(refs[0][...], 0)


def left_kernel(blocks, block_cols, per_step, *refs):
    me, slots, row_partner = refs[:3]
    tile_refs = refs[3 : 3 + per_step]
    q_refs = refs[3 + per_step : -2]
    out, q_both = refs[-2:]
    group, step = pl.program_id(0), pl.program_id(1)
    width = q_both.shape[0] // 2

    @pl.when(step == 0)
    def _():
        def put(value, first):
            high, low = split(value.T)
            q_both[:width, first : first + value.shape[0]] = high
            q_both[width:, first : first + value.shape[0]] = low

        blocks.load(group, me, row_partner, q_refs, put)

    block_row = blocks.row_of(group, me, row_partner)
    for index, tile_ref in enumerate(tile_refs):
        live = slots[block_row * block_cols + step * per_step + index] >= 0
        high, low = split(tile_ref[0])
        total = jnp.where(live, product(q_both[...], high, low), 0.0)
        out[index, 0], out[index, 1] = split(total)


def left_products(me, slots, row_partner, tiles, blocks, half_rows, block_cols):
    _, tile_order, _ = tiles.shape
    width = blocks.operands[0].shape[-1]
    per_step = 2 if block_cols % 2 == 0 else 1

    def tile_spec(index):
        def tile_at(g, b, me, slots, row_partner):
            place = blocks.row_of(g, me, row_partner) * block_cols + b * per_step + index
            return jnp.maximum(slots[place], 0), 0, 0

        return pl.BlockSpec((1, tile_order, tile_order), tile_at)

    def out_at(g, b, me, slots, row_partner):
        return b, 0, rem(blocks.row_of(g, me, row_partner), half_rows), 0

    return pl.pallas_call(
        functools.partial(left_kernel, blocks, block_cols, per_step),
        grid_spec=pltpu.PrefetchScalarGridSpec(
            num_scalar_prefetch=3,
            grid=(half_rows, block_cols // per_step),
            in_specs=[tile_spec(index) for index in range(per_step)] + blocks.specs,
            out_specs=pl.BlockSpec((per_step, 2, width, tile_order), out_at),
            scratch_shapes=[pltpu.VMEM((2 * width, tile_order), BF16)],
        ),
        out_shape=jax.ShapeDtypeStruct((block_cols, 2, half_rows * width, tile_order), BF16),
        compiler_params=PARAMS,
        cost_estimate=pl.CostEstimate(
            flops=12 * half_rows * block_cols * width * tile_order * tile_order,
            bytes_accessed=4 * half_rows * block_cols * tile_order * (tile_order + width),
            transcendentals=0,
        ),
        name="left_products",
    )(me, slots, row_partner, *[tiles] * per_step, *blocks.operands)


class Columns:
    OWN, FAR, KEPT = range(3)

    def __init__(self, kind, n_row, block_cols):
        self.kind = kind
        self.n_row = n_row
        self.half_cols = block_cols // 2
        self.steps = block_cols if kind == self.KEPT else self.half_cols

    def side(self, row):
        return div(2 * row, self.n_row)

    def half(self, step, me, col_partner):
        if self.kind == self.KEPT:
            goes_on = (me[1] < col_partner[me[0], me[1]]).astype(jnp.int32)
            return goes_on ^ div(step, self.half_cols)
        return self.side(me[0]) ^ (1 if self.kind == self.FAR else 0)

    def column(self, step, me, col_partner):
        return self.half(step, me, col_partner) * self.half_cols + rem(step, self.half_cols)


def packed_place(slots, first_row, first_col, half_rows, half_cols, block_cols, block):
    before = here = count = jnp.int32(0)
    for index in range(half_rows * half_cols):
        place = (first_row + index % half_rows) * block_cols + first_col + index // half_rows
        flag = (slots[place] >= 0).astype(jnp.int32)
        before = before + jnp.where(index < block, flag, 0)
        here = here + jnp.where(index == block, flag, 0)
        count = count + flag
    return jnp.where(here == 1, before, count + block - before), here == 1


def right_kernel(columns, block_cols, half_rows, shard_places, groups, *refs):
    me, slots, row_partner, col_partner, w_ref = refs[:5]
    pieces = refs[5 : 5 + sum(groups)]
    step = pl.program_id(0)
    tile_order = w_ref.shape[3]
    depth, width = pieces[0].shape
    packs = columns.kind != Columns.KEPT
    outs = refs[5 + sum(groups) : -3 if packs else -2]
    p_high, p_low = refs[-2:]

    @pl.when(step == 0)
    def _():
        at = 0
        for place, count in zip(shard_places(me), groups):
            value = pieces[at][...]
            for other in range(1, count):
                value = value + pieces[at + other][...]
            at += count
            rows = pl.ds(pl.multiple_of(place * depth, depth), depth)
            p_high[rows, :], p_low[rows, :] = split(value)

    column = columns.column(step, me, col_partner)
    rows = pl.ds(pl.multiple_of(column * tile_order, tile_order), tile_order)
    both = w_ref[0].reshape(2 * w_ref.shape[2], tile_order)
    block = product(both, p_high[rows, :], p_low[rows, :])
    half_cols = columns.half_cols
    if not packs:
        first, second = outs

        @pl.when(step < half_cols)
        def _():
            first[...] = block

        @pl.when(step >= half_cols)
        def _():
            second[...] = block

        return
    packed = refs[-3]
    first_row = half_of(True, me, row_partner) * half_rows
    first_col = columns.half(step, me, col_partner) * half_cols
    for row in range(half_rows):
        place, _ = packed_place(
            slots, first_row, first_col, half_rows, half_cols, block_cols, step * half_rows + row
        )
        packed[place] = block[row * width : (row + 1) * width]

    @pl.when(step == half_cols - 1)
    def _():
        count = outs[0].shape[0]
        outs[0][...] = packed[:count]
        for index, out in enumerate(outs[1:]):
            out[...] = packed[count + index]


def right_products(kind, me, slots, row_partner, col_partner, w, shards, shard_places, n_row, half_rows):
    block_cols, _, height, tile_order = w.shape
    columns = Columns(kind, n_row, block_cols)
    half_cols = columns.half_cols
    depth, width = shards[0][0].shape
    groups = [len(shard) for shard in shards]
    blocks = half_rows * half_cols
    p_rows = block_cols * tile_order

    def w_at(i, me, slots, row_partner, col_partner):
        return columns.column(i, me, col_partner), 0, 0, 0

    def quarter(first):
        return pl.BlockSpec(
            (height, width), lambda i, *_: (0, jnp.clip(i - first, 0, half_cols - 1))
        )

    scratch = [pltpu.VMEM((p_rows, width), BF16)] * 2
    if kind == Columns.KEPT:
        shapes = [(height, half_cols * width)] * 2
        out_specs = [quarter(0), quarter(half_cols)]
    else:
        most = max(1, blocks * 3 // 4)
        shapes = [(most, width, width)] + [(width, width)] * (blocks - most)
        out_specs = [pl.BlockSpec(shape, lambda i, *_, n=len(shape): (0,) * n) for shape in shapes]
        scratch = [pltpu.VMEM((blocks, width, width), F32)] + scratch
    return pl.pallas_call(
        functools.partial(right_kernel, columns, block_cols, half_rows, shard_places, groups),
        grid_spec=pltpu.PrefetchScalarGridSpec(
            num_scalar_prefetch=4,
            grid=(columns.steps,),
            in_specs=[pl.BlockSpec((1, 2, height, tile_order), w_at)]
            + [pl.BlockSpec(memory_space=pltpu.VMEM)] * sum(groups),
            out_specs=out_specs,
            scratch_shapes=scratch,
        ),
        out_shape=[jax.ShapeDtypeStruct(shape, F32) for shape in shapes],
        compiler_params=PARAMS,
        cost_estimate=pl.CostEstimate(
            flops=6 * columns.steps * height * width * tile_order,
            bytes_accessed=4 * columns.steps * height * (tile_order + width),
            transcendentals=0,
        ),
        name="right_products",
    )(me, slots, row_partner, col_partner, w, *[piece for shard in shards for piece in shard])


def sum_kernel(columns, second, half_rows, block_cols, arrays, *refs):
    me, mate_slots, row_partner, col_partner, kept_ref = refs[:5]
    chunks = refs[5 : 5 + arrays]
    sections, out = refs[5 + arrays : -1], refs[-1]
    half_cols = columns.half_cols
    first_row = half_of(False, me, row_partner) * half_rows
    half = columns.half(half_cols if second else 0, me, col_partner)
    chunk = columns.side(row_partner[me[1], me[0]]) ^ half
    place, live = packed_place(
        mate_slots, first_row, half * half_cols, half_rows, half_cols, block_cols, pl.program_id(0)
    )
    total = kept_ref[...]
    for section in sections:
        total = total + section[...]

    @pl.when(jnp.logical_not(live))
    def _():
        out[...] = total

    for which in range(2):
        first, *singles = chunks[which * arrays // 2 : (which + 1) * arrays // 2]
        count = first.shape[0]

        @pl.when(live & (chunk == which) & (place < count))
        def _():
            out[...] = total + first[place]

        for index, single in enumerate(singles):

            @pl.when(live & (chunk == which) & (place == count + index))
            def _():
                out[...] = total + single[...]


def sum_blocks(second, tables, n_row, half_rows, block_cols, kept, chunks, section=None):
    columns = Columns(Columns.KEPT, n_row, block_cols)
    half_cols = columns.half_cols
    height, both = kept.shape
    width = both // half_cols
    block = pl.BlockSpec((width, width), lambda i, *_: (rem(i, half_rows), div(i, half_rows)))
    sections = [] if section is None else [section]
    return pl.pallas_call(
        functools.partial(sum_kernel, columns, second, half_rows, block_cols, len(chunks)),
        grid_spec=pltpu.PrefetchScalarGridSpec(
            num_scalar_prefetch=4,
            grid=(half_rows * half_cols,),
            in_specs=[block]
            + [pl.BlockSpec(memory_space=pltpu.VMEM)] * len(chunks)
            + [block] * len(sections),
            out_specs=block,
        ),
        out_shape=jax.ShapeDtypeStruct((height, both), F32),
        compiler_params=PARAMS,
        name="sum_blocks",
    )(*tables, kept, *chunks, *sections)


def flip(value, axis, size, mask):
    return lax.ppermute(value, axis, [(i, i ^ mask) for i in range(size)])


def near_prolong(shard, axis, size):
    if size != 4:
        return []
    return [flip(shard, axis, size, 1), lax.ppermute(shard, axis, [(1, 2), (2, 1)])]


def gather_prolong(shard, near, axis, size):
    if size != 4:
        gathered = lax.all_gather(shard, axis)
        every = [[gathered[i]] for i in range(size)], lambda me: list(range(size))
        return every, every
    mate, over = near
    mate_over = lax.ppermute(mate, axis, [(1, 2), (2, 1)])
    handed = lax.ppermute(over, axis, [(1, 0), (2, 3)])
    mate_handed = lax.ppermute(mate, axis, [(2, 0), (1, 3)])

    def far_places(me):
        return [jnp.where(me[0] < 2, 2, 1), jnp.where(me[0] < 2, 3, 0)]

    own = [[shard], [mate]], lambda me: [me[0], me[0] ^ 1]
    return own, ([[over, handed], [mate_over, mate_handed]], far_places)


def chip_restrict(shard, axis, size):
    over_x = flip(shard, axis, size, 2)
    over_y = flip(shard, axis, size, 4)
    return [shard, over_x, over_y, flip(over_x, axis, size, 4)]


def pair_switch(mine, mate, size, branch, operand, sizes=(None,), choice=0):
    branches = [functools.partial(branch, mask, each) for mask in range(1, size) for each in sizes]
    if len(branches) == 1:
        return branches[0](operand)
    return lax.switch(((mine ^ mate) - 1) * len(sizes) + choice, branches, operand)


def solution(mesh):
    n_row = mesh.shape["row"]
    n_col = mesh.shape["col"]

    def body(tiles, coords, counts, restrict, prolong, row_partner, col_partner):
        tile_order = tiles.shape[1]
        block_rows = restrict.shape[0] * n_col // tile_order
        block_cols = prolong.shape[0] * n_row // tile_order
        half_rows, half_cols = block_rows // 2, block_cols // 2
        row = lax.axis_index("row").astype(jnp.int32)
        col = lax.axis_index("col").astype(jnp.int32)
        me = jnp.stack([row, col])

        row_mate = row_partner[col, row]
        col_mate = col_partner[row, col]

        slot_ids = jnp.arange(tiles.shape[0], dtype=jnp.int32)
        live = lax.all_gather(
            jnp.where(slot_ids[:, None] < counts[0], coords, -1), "row", axis=0, tiled=True
        )
        near = near_prolong(prolong, "row", n_row)
        slots, mate_slots, sizes = make_tables(me, live, row_partner, n_row, half_rows, block_cols)
        by_chip = n_col == 8 and block_rows == 4 and tile_order == 2 * restrict.shape[0]
        if by_chip:
            pieces = chip_restrict(restrict, "col", n_col)
            pieces, near, slots = lax.optimization_barrier((pieces, near, slots))
            mine = jnp.stack(pieces)
            q_pieces = [mine, flip(mine, "col", n_col, 1)]
        else:
            q_rows = lax.all_gather(restrict, "col", axis=0, tiled=True)
        own_shards, far_shards = gather_prolong(prolong, near, "row", n_row)

        def left(given):
            if by_chip:
                blocks = ChipBlocks(given, q_pieces)
            else:
                blocks = WholeBlocks(given, q_rows, tile_order, half_rows)
            return left_products(me, slots, row_partner, tiles, blocks, half_rows, block_cols)

        def right(kind, w, shards, places):
            return right_products(
                kind, me, slots, row_partner, col_partner, w, shards, places, n_row, half_rows
            )

        def swap_chunk(beside, mask, extra, chunk):
            received = [
                flip(array, "row", n_row, mask) if index <= extra else array
                for index, array in enumerate(chunk)
            ]
            return received, beside()

        def swap_section(mask, _, section):
            return flip(section, "col", n_col, mask)

        def exchange(size, chunk, beside):
            choice = jnp.clip(size - chunk[0].shape[0], 0, len(chunk) - 1)
            branch = functools.partial(swap_chunk, beside)
            return pair_switch(row, row_mate, n_row, branch, chunk, tuple(range(len(chunk))), choice)

        w = left(True)
        own = right(Columns.OWN, w, *own_shards)
        own, w_kept = exchange(sizes[0], own, lambda: left(False))
        far_pieces, own = lax.optimization_barrier((far_shards[0], own))
        far = right(Columns.FAR, w, far_pieces, far_shards[1])
        if n_row == 4:
            every = own_shards[0] + far_pieces, lambda me: own_shards[1](me) + far_shards[1](me)
        else:
            every = own_shards
        far, kept = exchange(sizes[1], far, lambda: right(Columns.KEPT, w_kept, *every))
        chunks = list(own) + list(far)
        add = functools.partial(sum_blocks, n_row=n_row, half_rows=half_rows, block_cols=block_cols)
        tables = (me, mate_slots, row_partner, col_partner)
        section = add(False, tables, kept=kept[0], chunks=chunks)
        section = pair_switch(col, col_mate, n_col, swap_section, section)
        return add(True, tables, kept=kept[1], chunks=chunks, section=section)

    in_specs = (
        P(("row", "col"), None, None),
        P(("row", "col"), None),
        P(("row", "col")),
        P(("row", "col"), None),
        P(("col", "row"), None),
        P(),
        P(),
    )
    return jax.shard_map(
        body, mesh=mesh, in_specs=in_specs, out_specs=P("row", "col"), check_vma=False
    )
```

```python
import functools

import jax
import jax.numpy as jnp
from jax import lax
from jax.experimental import pallas as pl
from jax.experimental.pallas import tpu as pltpu
from jax.sharding import PartitionSpec as P

F32 = jnp.float32
BF16 = jnp.bfloat16
VMEM_BYTES = 60 * 1024 * 1024
SHORT = pl.CostEstimate(flops=0, bytes_accessed=0, transcendentals=0)
PARAMS = pltpu.CompilerParams(vmem_limit_bytes=VMEM_BYTES)


def split(value):
    high = value.astype(BF16)
    low = (value - high.astype(F32)).astype(BF16)
    return high, low


def dot(left, right):
    return jnp.dot(left, right, preferred_element_type=F32)


def product(left_both, right_high, right_low):
    half = left_both.shape[0] // 2
    total = dot(left_both[half:], right_high)
    total = total + dot(left_both[:half], right_low)
    return total + dot(left_both[:half], right_high)


def div(value, by):
    return lax.div(value, jnp.int32(by))


def rem(value, by):
    return lax.rem(value, jnp.int32(by))


def half_of(given, me, row_partner):
    mate = row_partner[me[1], me[0]]
    return ((mate > me[0]) if given else (me[0] > mate)).astype(jnp.int32)


def tables_kernel(n_row, half_rows, block_cols, packed, choices, *refs):
    me, row_partner, col_partner, live = refs[:4]
    others = refs[4:-5]
    slots, mate_slots, first, second, across = refs[-5:]
    columns = Columns(Columns.OWN, n_row, block_cols)
    mate = row_partner[me[1], me[0]]
    distance = me[0] ^ mate
    per_device = live.shape[0]

    def fill(table, source, start):
        for slot in range(per_device):
            block_row = source[start + slot, 0]

            @pl.when(block_row >= 0)
            def _():
                table[block_row * block_cols + source[start + slot, 1]] = jnp.int32(slot)

    for place in range(slots.shape[0]):
        slots[place] = jnp.int32(-1)
        mate_slots[place] = jnp.int32(-1)
    fill(slots, live, 0)
    if len(others) == 1:
        fill(mate_slots, others[0], mate * per_device)
    else:
        for index, other in enumerate(others):
            pl.when(distance == index + 1)(functools.partial(fill, mate_slots, other, 0))

    half_cols = columns.half_cols
    for chunk, branch in enumerate((first, second)):
        counts = []
        for table, row, given in ((slots, me[0], True), (mate_slots, mate, False)):
            first_row = half_of(given, me, row_partner) * half_rows
            first_col = (columns.side(row) ^ chunk) * half_cols
            count = jnp.int32(0)
            for index in range(half_rows * half_cols):
                place = (first_row + index % half_rows) * block_cols + first_col + index // half_rows
                count = count + (table[place] >= 0).astype(jnp.int32)
            counts.append(count)
        choice = jnp.clip(jnp.maximum(*counts) - packed, 0, choices - 1)
        branch[0] = (distance - 1) * choices + choice
    across[0] = (me[1] ^ col_partner[me[0], me[1]]) - 1


def make_tables(me, row_partner, col_partner, live, others, n_row, half_rows, block_cols, packed, choices):
    smem = pl.BlockSpec(memory_space=pltpu.SMEM)
    places = 2 * half_rows * block_cols
    return pl.pallas_call(
        functools.partial(tables_kernel, n_row, half_rows, block_cols, packed, choices),
        in_specs=[smem] * (4 + len(others)),
        out_specs=[smem] * 5,
        out_shape=[jax.ShapeDtypeStruct((n,), jnp.int32) for n in (places, places, 1, 1, 1)],
        cost_estimate=SHORT,
        name="make_tables",
    )(me, row_partner, col_partner, live, *others)


class ChipBlocks:
    def __init__(self, given, pieces):
        self.given = given
        self.operands = pieces
        self.specs = [pl.BlockSpec(memory_space=pltpu.VMEM)] * len(pieces)

    def near(self, me, row_partner):
        return half_of(self.given, me, row_partner) == div(me[1], 4)

    def row_of(self, group, me, row_partner):
        return div(me[1], 2) ^ (jnp.where(self.near(me, row_partner), 0, 2) + group)

    def load(self, group, me, row_partner, refs, put):
        near = self.near(me, row_partner)
        odd = rem(me[1], 2)
        first, second = refs
        for chip in range(first.shape[0]):
            depth = first.shape[1]
            wanted = (group == chip % 2) & (near == (chip < 2))
            for core in range(2):

                @pl.when(wanted & (odd == core))
                def _():
                    put(first[chip], core * depth)
                    put(second[chip], (1 - core) * depth)


class WholeBlocks:
    def __init__(self, given, rows, tile_order, half_rows):
        self.given = given
        self.half_rows = half_rows
        self.operands = [rows]
        self.specs = [
            pl.BlockSpec(
                (tile_order, rows.shape[1]),
                lambda g, b, me, slots, row_partner: (self.row_of(g, me, row_partner), 0),
            )
        ]

    def row_of(self, group, me, row_partner):
        return half_of(self.given, me, row_partner) * self.half_rows + group

    def load(self, group, me, row_partner, refs, put):
        put(refs[0][...], 0)


def left_kernel(blocks, block_cols, per_step, *refs):
    me, slots, row_partner = refs[:3]
    tile_refs = refs[3 : 3 + per_step]
    q_refs = refs[3 + per_step : -2]
    out, q_both = refs[-2:]
    group, step = pl.program_id(0), pl.program_id(1)
    width = q_both.shape[0] // 2

    @pl.when(step == 0)
    def _():
        def put(value, first):
            high, low = split(value.T)
            q_both[:width, first : first + value.shape[0]] = high
            q_both[width:, first : first + value.shape[0]] = low

        blocks.load(group, me, row_partner, q_refs, put)

    block_row = blocks.row_of(group, me, row_partner)
    for index, tile_ref in enumerate(tile_refs):
        live = slots[block_row * block_cols + step * per_step + index] >= 0
        high, low = split(tile_ref[0])
        total = jnp.where(live, product(q_both[...], high, low), 0.0)
        out[index, 0], out[index, 1] = split(total)


def left_products(me, slots, row_partner, tiles, blocks, half_rows, block_cols):
    _, tile_order, _ = tiles.shape
    width = blocks.operands[0].shape[-1]
    per_step = 2 if block_cols % 2 == 0 else 1

    def tile_spec(index):
        def tile_at(g, b, me, slots, row_partner):
            place = blocks.row_of(g, me, row_partner) * block_cols + b * per_step + index
            return jnp.maximum(slots[place], 0), 0, 0

        return pl.BlockSpec((1, tile_order, tile_order), tile_at)

    def out_at(g, b, me, slots, row_partner):
        return b, 0, rem(blocks.row_of(g, me, row_partner), half_rows), 0

    return pl.pallas_call(
        functools.partial(left_kernel, blocks, block_cols, per_step),
        grid_spec=pltpu.PrefetchScalarGridSpec(
            num_scalar_prefetch=3,
            grid=(half_rows, block_cols // per_step),
            in_specs=[tile_spec(index) for index in range(per_step)] + blocks.specs,
            out_specs=pl.BlockSpec((per_step, 2, width, tile_order), out_at),
            scratch_shapes=[pltpu.VMEM((2 * width, tile_order), BF16)],
        ),
        out_shape=jax.ShapeDtypeStruct((block_cols, 2, half_rows * width, tile_order), BF16),
        compiler_params=PARAMS,
        cost_estimate=SHORT,
        name="left_products",
    )(me, slots, row_partner, *[tiles] * per_step, *blocks.operands)


class Columns:
    OWN, FAR, KEPT = range(3)

    def __init__(self, kind, n_row, block_cols):
        self.kind = kind
        self.n_row = n_row
        self.half_cols = block_cols // 2
        self.steps = block_cols if kind == self.KEPT else self.half_cols

    def side(self, row):
        return div(2 * row, self.n_row)

    def half(self, step, me, col_partner):
        if self.kind == self.KEPT:
            goes_on = (me[1] < col_partner[me[0], me[1]]).astype(jnp.int32)
            return goes_on ^ div(step, self.half_cols)
        return self.side(me[0]) ^ (1 if self.kind == self.FAR else 0)

    def column(self, step, me, col_partner):
        return self.half(step, me, col_partner) * self.half_cols + rem(step, self.half_cols)


def packed_first(blocks):
    return max(1, blocks * 3 // 4)


def packed_place(slots, first_row, first_col, half_rows, half_cols, block_cols, block):
    before = here = count = jnp.int32(0)
    for index in range(half_rows * half_cols):
        place = (first_row + index % half_rows) * block_cols + first_col + index // half_rows
        flag = (slots[place] >= 0).astype(jnp.int32)
        before = before + jnp.where(index < block, flag, 0)
        here = here + jnp.where(index == block, flag, 0)
        count = count + flag
    return jnp.where(here == 1, before, count + block - before), here == 1


def right_kernel(columns, block_cols, half_rows, places, *refs):
    me, slots, row_partner, col_partner, w_ref = refs[:5]
    pieces = refs[5 : 5 + len(places)]
    step = pl.program_id(0)
    tile_order = w_ref.shape[3]
    depth, width = pieces[0].shape[-2:]
    packs = columns.kind != Columns.KEPT
    outs = refs[5 + len(places) : -3 if packs else -2]
    p_high, p_low = refs[-2:]

    @pl.when(step == 0)
    def _():
        for place, piece in zip(places, pieces):
            rows = pl.ds(pl.multiple_of(place(me) * depth, depth), depth)
            p_high[rows, :], p_low[rows, :] = split(piece[...].reshape(depth, width))

    column = columns.column(step, me, col_partner)
    rows = pl.ds(pl.multiple_of(column * tile_order, tile_order), tile_order)
    both = w_ref[0].reshape(2 * w_ref.shape[2], tile_order)
    block = product(both, p_high[rows, :], p_low[rows, :])
    half_cols = columns.half_cols
    if not packs:
        first, second = outs

        @pl.when(step < half_cols)
        def _():
            first[...] = block

        @pl.when(step >= half_cols)
        def _():
            second[...] = block

        return
    packed = refs[-3]
    first_row = half_of(True, me, row_partner) * half_rows
    first_col = columns.half(step, me, col_partner) * half_cols
    for row in range(half_rows):
        place, _ = packed_place(
            slots, first_row, first_col, half_rows, half_cols, block_cols, step * half_rows + row
        )
        packed[place] = block[row * width : (row + 1) * width]

    @pl.when(step == half_cols - 1)
    def _():
        count = outs[0].shape[0]
        outs[0][...] = packed[:count]
        for index, out in enumerate(outs[1:]):
            out[...] = packed[count + index]


def right_products(kind, me, slots, row_partner, col_partner, w, shards, n_row, half_rows):
    block_cols, _, height, tile_order = w.shape
    columns = Columns(kind, n_row, block_cols)
    half_cols = columns.half_cols
    depth, width = shards[0][0].shape[-2:]
    blocks = half_rows * half_cols
    p_rows = block_cols * tile_order

    def w_at(i, me, slots, row_partner, col_partner):
        return columns.column(i, me, col_partner), 0, 0, 0

    def quarter(first):
        return pl.BlockSpec(
            (height, width), lambda i, *_: (0, jnp.clip(i - first, 0, half_cols - 1))
        )

    def shard_spec(array, place):
        if array.ndim == 2:
            return pl.BlockSpec((depth, width), lambda i, *_: (0, 0))
        return pl.BlockSpec((1, depth, width), lambda i, me, *_: (place(me), 0, 0))

    scratch = [pltpu.VMEM((p_rows, width), BF16)] * 2
    if kind == Columns.KEPT:
        shapes = [(height, half_cols * width)] * 2
        out_specs = [quarter(0), quarter(half_cols)]
    else:
        most = packed_first(blocks)
        shapes = [(most, width, width)] + [(width, width)] * (blocks - most)
        out_specs = [pl.BlockSpec(shape, lambda i, *_, n=len(shape): (0,) * n) for shape in shapes]
        scratch = [pltpu.VMEM((blocks, width, width), F32)] + scratch
    return pl.pallas_call(
        functools.partial(
            right_kernel, columns, block_cols, half_rows, [place for _, place in shards]
        ),
        grid_spec=pltpu.PrefetchScalarGridSpec(
            num_scalar_prefetch=4,
            grid=(columns.steps,),
            in_specs=[pl.BlockSpec((1, 2, height, tile_order), w_at)]
            + [shard_spec(array, place) for array, place in shards],
            out_specs=out_specs,
            scratch_shapes=scratch,
        ),
        out_shape=[jax.ShapeDtypeStruct(shape, F32) for shape in shapes],
        compiler_params=PARAMS,
        cost_estimate=SHORT,
        name="right_products",
    )(me, slots, row_partner, col_partner, w, *[array for array, _ in shards])


def sum_kernel(columns, second, half_rows, block_cols, arrays, *refs):
    me, mate_slots, row_partner, col_partner, kept_ref = refs[:5]
    chunks = refs[5 : 5 + arrays]
    sections, out = refs[5 + arrays : -1], refs[-1]
    half_cols = columns.half_cols
    first_row = half_of(False, me, row_partner) * half_rows
    half = columns.half(half_cols if second else 0, me, col_partner)
    chunk = columns.side(row_partner[me[1], me[0]]) ^ half
    place, live = packed_place(
        mate_slots, first_row, half * half_cols, half_rows, half_cols, block_cols, pl.program_id(0)
    )
    total = kept_ref[...]
    for section in sections:
        total = total + section[...]

    @pl.when(jnp.logical_not(live))
    def _():
        out[...] = total

    for which in range(2):
        first, *singles = chunks[which * arrays // 2 : (which + 1) * arrays // 2]
        count = first.shape[0]

        @pl.when(live & (chunk == which) & (place < count))
        def _():
            out[...] = total + first[place]

        for index, single in enumerate(singles):

            @pl.when(live & (chunk == which) & (place == count + index))
            def _():
                out[...] = total + single[...]


def sum_blocks(second, tables, n_row, half_rows, block_cols, kept, chunks, section=None):
    columns = Columns(Columns.KEPT, n_row, block_cols)
    half_cols = columns.half_cols
    height, both = kept.shape
    width = both // half_cols
    block = pl.BlockSpec((width, width), lambda i, *_: (rem(i, half_rows), div(i, half_rows)))
    sections = [] if section is None else [section]
    return pl.pallas_call(
        functools.partial(sum_kernel, columns, second, half_rows, block_cols, len(chunks)),
        grid_spec=pltpu.PrefetchScalarGridSpec(
            num_scalar_prefetch=4,
            grid=(half_rows * half_cols,),
            in_specs=[block]
            + [pl.BlockSpec(memory_space=pltpu.VMEM)] * len(chunks)
            + [block] * len(sections),
            out_specs=block,
        ),
        out_shape=jax.ShapeDtypeStruct((height, both), F32),
        compiler_params=PARAMS,
        name="sum_blocks",
    )(*tables, kept, *chunks, *sections)


def flip(value, axis, size, mask):
    return lax.ppermute(value, axis, [(i, i ^ mask) for i in range(size)])


def gather_prolong(shard, mate, axis, size):
    gathered = lax.all_gather(shard, axis)

    def at(place):
        return gathered, place

    def side(other, index):
        return at(lambda me: (div(2 * me[0], size) ^ other) * (size // 2) + index)

    own = [side(0, index) for index in range(size // 2)]
    if mate is not None:
        own = [(shard, lambda me: me[0]), (mate, lambda me: me[0] ^ 1)]
    far = [side(1, index) for index in range(size // 2)]
    return own, far, [at(lambda me, index=index: jnp.int32(index)) for index in range(size)]


def chip_restrict(shard, axis, size):
    over_x = flip(shard, axis, size, 2)
    over_y = flip(shard, axis, size, 4)
    return [shard, over_x, over_y, flip(over_x, axis, size, 4)]


def pair_switch(index, size, branch, operand, choices=1):
    branches = [
        functools.partial(branch, mask, choice) for mask in range(1, size) for choice in range(choices)
    ]
    return lax.switch(index[0], branches, operand)


def solution(mesh):
    n_row = mesh.shape["row"]
    n_col = mesh.shape["col"]

    def body(tiles, coords, counts, restrict, prolong, row_partner, col_partner):
        tile_order = tiles.shape[1]
        block_rows = restrict.shape[0] * n_col // tile_order
        block_cols = prolong.shape[0] * n_row // tile_order
        half_rows, half_cols = block_rows // 2, block_cols // 2
        row = lax.axis_index("row").astype(jnp.int32)
        col = lax.axis_index("col").astype(jnp.int32)
        me = jnp.stack([row, col])

        slot_ids = jnp.arange(tiles.shape[0], dtype=jnp.int32)
        live = jnp.where(slot_ids[:, None] < counts[0], coords, -1)
        if n_row == 4:
            others = [flip(live, "row", n_row, mask) for mask in range(1, n_row)]
        else:
            others = [lax.all_gather(live, "row", axis=0, tiled=True)]
        mate_prolong = flip(prolong, "row", n_row, 1) if n_row == 4 else None
        prolong, others = lax.optimization_barrier((prolong, others))
        packed = packed_first(half_rows * half_cols)
        choices = half_rows * half_cols - packed + 1
        slots, mate_slots, first, second, across = make_tables(
            me, row_partner, col_partner, live, others, n_row, half_rows, block_cols, packed, choices
        )
        by_chip = n_col == 8 and block_rows == 4 and tile_order == 2 * restrict.shape[0]
        if by_chip:
            pieces = chip_restrict(restrict, "col", n_col)
            pieces, slots, mate_prolong = lax.optimization_barrier((pieces, slots, mate_prolong))
            mine = jnp.stack(pieces)
            q_pieces = [mine, flip(mine, "col", n_col, 1)]
        else:
            q_rows = lax.all_gather(restrict, "col", axis=0, tiled=True)

        own_shards, far_shards, all_shards = gather_prolong(prolong, mate_prolong, "row", n_row)

        def left(given):
            if by_chip:
                blocks = ChipBlocks(given, q_pieces)
            else:
                blocks = WholeBlocks(given, q_rows, tile_order, half_rows)
            return left_products(me, slots, row_partner, tiles, blocks, half_rows, block_cols)

        def right(kind, w, shards):
            return right_products(
                kind, me, slots, row_partner, col_partner, w, shards, n_row, half_rows
            )

        def swap_chunk(beside, mask, extra, chunk):
            received = [
                flip(array, "row", n_row, mask) if index <= extra else array
                for index, array in enumerate(chunk)
            ]
            return received, beside()

        def swap_section(mask, _, section):
            return flip(section, "col", n_col, mask)

        def exchange(index, chunk, beside):
            branch = functools.partial(swap_chunk, beside)
            return pair_switch(index, n_row, branch, chunk, choices)

        w = left(True)
        own = right(Columns.OWN, w, own_shards)
        own, w_kept = exchange(first, own, lambda: left(False))
        far = right(Columns.FAR, w, far_shards)
        far, kept = exchange(second, far, lambda: right(Columns.KEPT, w_kept, all_shards))
        chunks = list(own) + list(far)
        add = functools.partial(sum_blocks, n_row=n_row, half_rows=half_rows, block_cols=block_cols)
        tables = (me, mate_slots, row_partner, col_partner)
        section = add(False, tables, kept=kept[0], chunks=chunks)
        section = pair_switch(across, n_col, swap_section, section)
        return add(True, tables, kept=kept[1], chunks=chunks, section=section)

    in_specs = (
        P(("row", "col"), None, None),
        P(("row", "col"), None),
        P(("row", "col")),
        P(("row", "col"), None),
        P(("col", "row"), None),
        P(),
        P(),
    )
    return jax.shard_map(
        body, mesh=mesh, in_specs=in_specs, out_specs=P("row", "col"), check_vma=False
    )
```

```python
import functools

import jax
import jax.numpy as jnp
from jax import lax
from jax.experimental import pallas as pl
from jax.experimental.pallas import tpu as pltpu
from jax.sharding import PartitionSpec as P

F32 = jnp.float32
BF16 = jnp.bfloat16
VMEM_BYTES = 60 * 1024 * 1024
SHORT = pl.CostEstimate(flops=0, bytes_accessed=0, transcendentals=0)
PARAMS = pltpu.CompilerParams(vmem_limit_bytes=VMEM_BYTES)


def split(value):
    high = value.astype(BF16)
    low = (value - high.astype(F32)).astype(BF16)
    return high, low


def dot(left, right):
    return jnp.dot(left, right, preferred_element_type=F32)


def product(left_both, right_high, right_low):
    half = left_both.shape[0] // 2
    total = dot(left_both[half:], right_high)
    total = total + dot(left_both[:half], right_low)
    return total + dot(left_both[:half], right_high)


def div(value, by):
    return lax.div(value, jnp.int32(by))


def rem(value, by):
    return lax.rem(value, jnp.int32(by))


def half_of(given, me, row_partner):
    mate = row_partner[me[1], me[0]]
    return ((mate > me[0]) if given else (me[0] > mate)).astype(jnp.int32)


def tables_kernel(block_cols, me, row_partner, col_partner, coords, counts, slots, first, across):
    for place in range(slots.shape[0]):
        slots[place] = jnp.int32(-1)
    for slot in range(coords.shape[0]):

        @pl.when(slot < counts[0])
        def _():
            slots[coords[slot, 0] * block_cols + coords[slot, 1]] = jnp.int32(slot)

    first[0] = (me[0] ^ row_partner[me[1], me[0]]) - 1
    across[0] = (me[1] ^ col_partner[me[0], me[1]]) - 1


def make_tables(me, row_partner, col_partner, coords, counts, places, block_cols):
    smem = pl.BlockSpec(memory_space=pltpu.SMEM)
    return pl.pallas_call(
        functools.partial(tables_kernel, block_cols),
        in_specs=[smem] * 5,
        out_specs=[smem] * 3,
        out_shape=[jax.ShapeDtypeStruct((n,), jnp.int32) for n in (places, 1, 1)],
        cost_estimate=SHORT,
        name="make_tables",
    )(me, row_partner, col_partner, coords, counts)


class ChipBlocks:
    def __init__(self, given, pieces):
        self.given = given
        self.operands = pieces
        self.specs = [pl.BlockSpec(memory_space=pltpu.VMEM)] * len(pieces)

    def near(self, me, row_partner):
        return half_of(self.given, me, row_partner) == div(me[1], 4)

    def row_of(self, group, me, row_partner):
        return div(me[1], 2) ^ (jnp.where(self.near(me, row_partner), 0, 2) + group)

    def load(self, group, me, row_partner, refs, put):
        near = self.near(me, row_partner)
        odd = rem(me[1], 2)
        first, second = refs
        for chip in range(first.shape[0]):
            depth = first.shape[1]
            wanted = (group == chip % 2) & (near == (chip < 2))
            for core in range(2):

                @pl.when(wanted & (odd == core))
                def _():
                    put(first[chip], core * depth)
                    put(second[chip], (1 - core) * depth)


class WholeBlocks:
    def __init__(self, given, rows, tile_order, half_rows):
        self.given = given
        self.half_rows = half_rows
        self.operands = [rows]
        self.specs = [
            pl.BlockSpec(
                (tile_order, rows.shape[1]),
                lambda g, b, me, slots, row_partner: (self.row_of(g, me, row_partner), 0),
            )
        ]

    def row_of(self, group, me, row_partner):
        return half_of(self.given, me, row_partner) * self.half_rows + group

    def load(self, group, me, row_partner, refs, put):
        put(refs[0][...], 0)


def left_kernel(blocks, block_cols, per_step, *refs):
    me, slots, row_partner = refs[:3]
    tile_refs = refs[3 : 3 + per_step]
    q_refs = refs[3 + per_step : -2]
    out, q_both = refs[-2:]
    group, step = pl.program_id(0), pl.program_id(1)
    width = q_both.shape[0] // 2

    @pl.when(step == 0)
    def _():
        def put(value, first):
            high, low = split(value.T)
            q_both[:width, first : first + value.shape[0]] = high
            q_both[width:, first : first + value.shape[0]] = low

        blocks.load(group, me, row_partner, q_refs, put)

    block_row = blocks.row_of(group, me, row_partner)
    for index, tile_ref in enumerate(tile_refs):
        live = slots[block_row * block_cols + step * per_step + index] >= 0
        high, low = split(tile_ref[0])
        total = jnp.where(live, product(q_both[...], high, low), 0.0)
        out[index, 0], out[index, 1] = split(total)


def left_products(me, slots, row_partner, tiles, blocks, half_rows, block_cols):
    _, tile_order, _ = tiles.shape
    width = blocks.operands[0].shape[-1]
    per_step = 2 if block_cols % 2 == 0 else 1

    def tile_spec(index):
        def tile_at(g, b, me, slots, row_partner):
            place = blocks.row_of(g, me, row_partner) * block_cols + b * per_step + index
            return jnp.maximum(slots[place], 0), 0, 0

        return pl.BlockSpec((1, tile_order, tile_order), tile_at)

    def out_at(g, b, me, slots, row_partner):
        return b, 0, rem(blocks.row_of(g, me, row_partner), half_rows), 0

    return pl.pallas_call(
        functools.partial(left_kernel, blocks, block_cols, per_step),
        grid_spec=pltpu.PrefetchScalarGridSpec(
            num_scalar_prefetch=3,
            grid=(half_rows, block_cols // per_step),
            in_specs=[tile_spec(index) for index in range(per_step)] + blocks.specs,
            out_specs=pl.BlockSpec((per_step, 2, width, tile_order), out_at),
            scratch_shapes=[pltpu.VMEM((2 * width, tile_order), BF16)],
        ),
        out_shape=jax.ShapeDtypeStruct((block_cols, 2, half_rows * width, tile_order), BF16),
        compiler_params=PARAMS,
        cost_estimate=SHORT,
        name="left_products",
    )(me, slots, row_partner, *[tiles] * per_step, *blocks.operands)


class Columns:
    OWN, FAR, KEPT = range(3)

    def __init__(self, kind, n_row, block_cols):
        self.kind = kind
        self.n_row = n_row
        self.half_cols = block_cols // 2
        self.steps = block_cols if kind == self.KEPT else self.half_cols

    def side(self, row):
        return div(2 * row, self.n_row)

    def half(self, step, me, col_partner):
        if self.kind == self.KEPT:
            goes_on = (me[1] < col_partner[me[0], me[1]]).astype(jnp.int32)
            return goes_on ^ div(step, self.half_cols)
        return self.side(me[0]) ^ (1 if self.kind == self.FAR else 0)

    def column(self, step, me, col_partner):
        return self.half(step, me, col_partner) * self.half_cols + rem(step, self.half_cols)


def packed_first(blocks):
    return max(1, blocks // 2)


def packed_place(slots, first_row, first_col, half_rows, half_cols, block_cols, block):
    before = here = count = jnp.int32(0)
    for index in range(half_rows * half_cols):
        place = (first_row + index % half_rows) * block_cols + first_col + index // half_rows
        flag = (slots[place] >= 0).astype(jnp.int32)
        before = before + jnp.where(index < block, flag, 0)
        here = here + jnp.where(index == block, flag, 0)
        count = count + flag
    return jnp.where(here == 1, before, count + block - before), here == 1


def quarter_live(table, first_row, first_col, half_rows, half_cols, block_cols):
    count = jnp.int32(0)
    for index in range(half_rows * half_cols):
        place = (first_row + index % half_rows) * block_cols + first_col + index // half_rows
        count = count + (table[place] >= 0).astype(jnp.int32)
    return count


def right_kernel(columns, block_cols, half_rows, places, *refs):
    me, slots, mate_slots, row_partner, col_partner, w_ref = refs[:6]
    pieces = refs[6 : 6 + len(places)]
    step = pl.program_id(0)
    tile_order = w_ref.shape[3]
    depth, width = pieces[0].shape[-2:]
    packs = columns.kind == Columns.FAR
    outs = refs[6 + len(places) : -3 if packs else -2]
    p_high, p_low = refs[-2:]

    @pl.when(step == 0)
    def _():
        for place, piece in zip(places, pieces):
            rows = pl.ds(pl.multiple_of(place(me) * depth, depth), depth)
            p_high[rows, :], p_low[rows, :] = split(piece[...].reshape(depth, width))

    column = columns.column(step, me, col_partner)
    rows = pl.ds(pl.multiple_of(column * tile_order, tile_order), tile_order)
    both = w_ref[0].reshape(2 * w_ref.shape[2], tile_order)
    block = product(both, p_high[rows, :], p_low[rows, :])
    half_cols = columns.half_cols
    if not packs:
        for index, out in enumerate(outs):

            @pl.when(div(step, half_cols) == index)
            def _():
                out[...] = block

        return
    branch, *outs = outs
    packed = refs[-3]
    first_row = half_of(True, me, row_partner) * half_rows
    first_col = columns.half(step, me, col_partner) * half_cols
    for row in range(half_rows):
        place, _ = packed_place(
            slots, first_row, first_col, half_rows, half_cols, block_cols, step * half_rows + row
        )
        packed[place] = block[row * width : (row + 1) * width]

    @pl.when(step == half_cols - 1)
    def _():
        count = outs[0].shape[0]
        outs[0][...] = packed[:count]
        for index, out in enumerate(outs[1:]):
            out[...] = packed[count + index]
        mate = row_partner[me[1], me[0]]
        mate_col = (columns.side(mate) ^ 1) * half_cols
        mate_row = half_of(False, me, row_partner) * half_rows
        quarter = half_rows, half_cols, block_cols
        most = jnp.maximum(
            quarter_live(slots, first_row, first_col, *quarter),
            quarter_live(mate_slots, mate_row, mate_col, *quarter),
        )
        choice = jnp.clip(most - count, 0, len(outs) - 1)
        branch[0] = ((me[0] ^ mate) - 1) * len(outs) + choice


def right_products(kind, tables, w, shards, n_row, half_rows):
    block_cols, _, height, tile_order = w.shape
    columns = Columns(kind, n_row, block_cols)
    half_cols = columns.half_cols
    depth, width = shards[0][0].shape[-2:]
    blocks = half_rows * half_cols

    def w_at(i, me, slots, mate_slots, row_partner, col_partner):
        return columns.column(i, me, col_partner), 0, 0, 0

    def quarter(first):
        return pl.BlockSpec(
            (height, width), lambda i, *_: (0, jnp.clip(i - first, 0, half_cols - 1))
        )

    def shard_spec(array, place):
        if array.ndim == 2:
            return pl.BlockSpec((depth, width), lambda i, *_: (0, 0))
        return pl.BlockSpec((1, depth, width), lambda i, me, *_: (place(me), 0, 0))

    scratch = [pltpu.VMEM((block_cols * tile_order, width), BF16)] * 2
    if kind == Columns.FAR:
        most = packed_first(blocks)
        shapes = [(most, width, width)] + [(width, width)] * (blocks - most)
        out_specs = [pl.BlockSpec(shape, lambda i, *_, n=len(shape): (0,) * n) for shape in shapes]
        out_specs = [pl.BlockSpec(memory_space=pltpu.SMEM)] + out_specs
        scratch = [pltpu.VMEM((blocks, width, width), F32)] + scratch
    else:
        shapes = [(height, half_cols * width)] * (columns.steps // half_cols)
        out_specs = [quarter(index * half_cols) for index in range(len(shapes))]
    out_shape = [jax.ShapeDtypeStruct(shape, F32) for shape in shapes]
    if kind == Columns.FAR:
        out_shape = [jax.ShapeDtypeStruct((1,), jnp.int32)] + out_shape
    return pl.pallas_call(
        functools.partial(
            right_kernel, columns, block_cols, half_rows, [place for _, place in shards]
        ),
        grid_spec=pltpu.PrefetchScalarGridSpec(
            num_scalar_prefetch=5,
            grid=(columns.steps,),
            in_specs=[pl.BlockSpec((1, 2, height, tile_order), w_at)]
            + [shard_spec(array, place) for array, place in shards],
            out_specs=out_specs,
            scratch_shapes=scratch,
        ),
        out_shape=out_shape,
        compiler_params=PARAMS,
        cost_estimate=SHORT,
        name="right_products",
    )(*tables, w, *[array for array, _ in shards])


def sum_kernel(columns, second, half_rows, block_cols, singles, *refs):
    me, _, mate_slots, row_partner, col_partner, kept_ref, own_ref, packed_ref = refs[:8]
    singles, sections, out = refs[8 : 8 + singles], refs[8 + singles : -1], refs[-1]
    half_cols = columns.half_cols
    first_row = half_of(False, me, row_partner) * half_rows
    half = columns.half(half_cols if second else 0, me, col_partner)
    far = (columns.side(row_partner[me[1], me[0]]) ^ half) == 1
    place, live = packed_place(
        mate_slots, first_row, half * half_cols, half_rows, half_cols, block_cols, pl.program_id(0)
    )
    count = packed_ref.shape[0]
    total = kept_ref[...]
    for section in sections:
        total = total + section[...]

    @pl.when(jnp.logical_not(far))
    def _():
        out[...] = total + own_ref[...]

    @pl.when(far & jnp.logical_not(live))
    def _():
        out[...] = total

    @pl.when(far & live & (place < count))
    def _():
        out[...] = total + packed_ref[place]

    for index, single in enumerate(singles):

        @pl.when(far & live & (place == count + index))
        def _():
            out[...] = total + single[...]


def sum_blocks(second, tables, n_row, half_rows, block_cols, kept, own, far, section=None):
    columns = Columns(Columns.KEPT, n_row, block_cols)
    half_cols = columns.half_cols
    height, both = kept.shape
    width = both // half_cols
    block = pl.BlockSpec((width, width), lambda i, *_: (rem(i, half_rows), div(i, half_rows)))
    sections = [] if section is None else [section]
    return pl.pallas_call(
        functools.partial(sum_kernel, columns, second, half_rows, block_cols, len(far) - 1),
        grid_spec=pltpu.PrefetchScalarGridSpec(
            num_scalar_prefetch=5,
            grid=(half_rows * half_cols,),
            in_specs=[block, block]
            + [pl.BlockSpec(memory_space=pltpu.VMEM)] * len(far)
            + [block] * len(sections),
            out_specs=block,
        ),
        out_shape=jax.ShapeDtypeStruct((height, both), F32),
        compiler_params=PARAMS,
        name="sum_blocks",
    )(*tables, kept, own, *far, *sections)


def flip(value, axis, size, mask):
    return lax.ppermute(value, axis, [(i, i ^ mask) for i in range(size)])


def gather_prolong(shard, mate, axis, size):
    gathered = lax.all_gather(shard, axis)

    def at(place):
        return gathered, place

    def side(other, index):
        return at(lambda me: (div(2 * me[0], size) ^ other) * (size // 2) + index)

    own = [side(0, index) for index in range(size // 2)]
    if mate is not None:
        own = [(shard, lambda me: me[0]), (mate, lambda me: me[0] ^ 1)]
    far = [side(1, index) for index in range(size // 2)]
    return own, far, [at(lambda me, index=index: jnp.int32(index)) for index in range(size)]


def chip_restrict(shard, axis, size):
    over_x = flip(shard, axis, size, 2)
    over_y = flip(shard, axis, size, 4)
    return [shard, over_x, over_y, flip(over_x, axis, size, 4)]


def pair_switch(index, size, branch, operand, choices=1):
    branches = [
        functools.partial(branch, mask, choice) for mask in range(1, size) for choice in range(choices)
    ]
    return lax.switch(index[0], branches, operand)


def solution(mesh):
    n_row = mesh.shape["row"]
    n_col = mesh.shape["col"]

    def body(tiles, coords, counts, restrict, prolong, row_partner, col_partner):
        tile_order = tiles.shape[1]
        block_rows = restrict.shape[0] * n_col // tile_order
        block_cols = prolong.shape[0] * n_row // tile_order
        half_rows, half_cols = block_rows // 2, block_cols // 2
        row = lax.axis_index("row").astype(jnp.int32)
        col = lax.axis_index("col").astype(jnp.int32)
        me = jnp.stack([row, col])

        places = block_rows * block_cols
        slots, first, across = make_tables(
            me, row_partner, col_partner, coords, counts, places, block_cols
        )
        by_chip = n_col == 8 and block_rows == 4 and tile_order == 2 * restrict.shape[0]
        if by_chip:
            pieces = chip_restrict(restrict, "col", n_col)
        else:
            pieces = []
        mate_prolong = None
        if n_row == 4:
            mate_prolong = flip(prolong, "row", n_row, 1)
            prolong, mate_prolong, pieces = lax.optimization_barrier((prolong, mate_prolong, pieces))
        own_shards, far_shards, all_shards = gather_prolong(prolong, mate_prolong, "row", n_row)
        if by_chip:
            pieces, slots = lax.optimization_barrier((pieces, slots))
            mine = jnp.stack(pieces)
            q_pieces = [mine, flip(mine, "col", n_col, 1)]
        else:
            q_rows = lax.all_gather(restrict, "col", axis=0, tiled=True)

        def left(given):
            if by_chip:
                blocks = ChipBlocks(given, q_pieces)
            else:
                blocks = WholeBlocks(given, q_rows, tile_order, half_rows)
            return left_products(me, slots, row_partner, tiles, blocks, half_rows, block_cols)

        def right(kind, mate_slots, w, shards):
            tables = (me, slots, mate_slots, row_partner, col_partner)
            return right_products(kind, tables, w, shards, n_row, half_rows)

        def swap_own(mask, _, own):
            return flip(own, "row", n_row, mask), flip(slots, "row", n_row, mask), left(False)

        def swap_far(mask, extra, far):
            received = [
                flip(array, "row", n_row, mask) if index <= extra else array
                for index, array in enumerate(far)
            ]
            return received, right(Columns.KEPT, slots, w_kept, all_shards)

        def swap_section(mask, _, section):
            return flip(section, "col", n_col, mask)

        w = left(True)
        (own,) = right(Columns.OWN, slots, w, own_shards)
        own, mate_slots, w_kept = pair_switch(first, n_row, swap_own, own)
        second, *far = right(Columns.FAR, mate_slots, w, far_shards)
        far, kept = pair_switch(second, n_row, swap_far, far, len(far))
        add = functools.partial(sum_blocks, n_row=n_row, half_rows=half_rows, block_cols=block_cols)
        tables = (me, slots, mate_slots, row_partner, col_partner)
        section = add(False, tables, kept=kept[0], own=own, far=far)
        section = pair_switch(across, n_col, swap_section, section)
        return add(True, tables, kept=kept[1], own=own, far=far, section=section)

    in_specs = (
        P(("row", "col"), None, None),
        P(("row", "col"), None),
        P(("row", "col")),
        P(("row", "col"), None),
        P(("col", "row"), None),
        P(),
        P(),
    )
    return jax.shard_map(
        body, mesh=mesh, in_specs=in_specs, out_specs=P("row", "col"), check_vma=False
    )
```

```python
import functools

import jax
import jax.numpy as jnp
from jax import lax
from jax.experimental import pallas as pl
from jax.experimental.pallas import tpu as pltpu
from jax.sharding import PartitionSpec as P

F32 = jnp.float32
BF16 = jnp.bfloat16
VMEM_BYTES = 48 * 1024 * 1024
PARAMS = pltpu.CompilerParams(vmem_limit_bytes=VMEM_BYTES)


def cost(flops):
    return pl.CostEstimate(flops=flops, bytes_accessed=0, transcendentals=0)


def split(value):
    high = value.astype(BF16)
    low = (value - high.astype(F32)).astype(BF16)
    return high, low


def dot(left, right):
    return jnp.dot(left, right, preferred_element_type=F32)


def product(left_both, right_high, right_low):
    half = left_both.shape[0] // 2
    total = dot(left_both[half:], right_high)
    total = total + dot(left_both[:half], right_low)
    return total + dot(left_both[:half], right_high)


def div(value, by):
    return lax.div(value, jnp.int32(by))


def rem(value, by):
    return lax.rem(value, jnp.int32(by))


def half_of(given, me, row_partner):
    mate = row_partner[me[1], me[0]]
    return ((mate > me[0]) if given else (me[0] > mate)).astype(jnp.int32)


def tables_kernel(block_cols, me, row_partner, col_partner, coords, counts, slots, first, across):
    for place in range(slots.shape[0]):
        slots[place] = jnp.int32(-1)
    for slot in range(coords.shape[0]):

        @pl.when(slot < counts[0])
        def _():
            slots[coords[slot, 0] * block_cols + coords[slot, 1]] = jnp.int32(slot)

    first[0] = (me[0] ^ row_partner[me[1], me[0]]) - 1
    across[0] = (me[1] ^ col_partner[me[0], me[1]]) - 1


def make_tables(me, row_partner, col_partner, coords, counts, places, block_cols):
    smem = pl.BlockSpec(memory_space=pltpu.SMEM)
    return pl.pallas_call(
        functools.partial(tables_kernel, block_cols),
        in_specs=[smem] * 5,
        out_specs=[smem] * 3,
        out_shape=[jax.ShapeDtypeStruct((n,), jnp.int32) for n in (places, 1, 1)],
        cost_estimate=cost(0),
        name="make_tables",
    )(me, row_partner, col_partner, coords, counts)


class WholeBlocks:
    def __init__(self, given, rows, tile_order, half_rows):
        self.given = given
        self.half_rows = half_rows
        self.operands = [rows]
        self.specs = [
            pl.BlockSpec(
                (tile_order, rows.shape[1]),
                lambda g, b, me, slots, row_partner: (self.row_of(g, me, row_partner), 0),
            )
        ]

    def row_of(self, group, me, row_partner):
        return half_of(self.given, me, row_partner) * self.half_rows + group

    def load(self, group, me, row_partner, refs, put):
        put(refs[0][...], 0)


def left_kernel(blocks, block_cols, per_step, *refs):
    me, slots, row_partner = refs[:3]
    tile_refs = refs[3 : 3 + per_step]
    q_refs = refs[3 + per_step : -2]
    out, q_both = refs[-2:]
    group, step = pl.program_id(0), pl.program_id(1)
    width = q_both.shape[0] // 2

    @pl.when(step == 0)
    def _():
        def put(value, first):
            high, low = split(value.T)
            q_both[:width, first : first + value.shape[0]] = high
            q_both[width:, first : first + value.shape[0]] = low

        blocks.load(group, me, row_partner, q_refs, put)

    block_row = blocks.row_of(group, me, row_partner)
    for index, tile_ref in enumerate(tile_refs):
        live = slots[block_row * block_cols + step * per_step + index] >= 0
        high, low = split(tile_ref[0])
        total = jnp.where(live, product(q_both[...], high, low), 0.0)
        out[index, 0], out[index, 1] = split(total)


def left_products(me, slots, row_partner, tiles, blocks, half_rows, block_cols):
    _, tile_order, _ = tiles.shape
    width = blocks.operands[0].shape[-1]
    per_step = 2 if block_cols % 2 == 0 else 1

    def tile_spec(index):
        def tile_at(g, b, me, slots, row_partner):
            place = blocks.row_of(g, me, row_partner) * block_cols + b * per_step + index
            return jnp.maximum(slots[place], 0), 0, 0

        return pl.BlockSpec((1, tile_order, tile_order), tile_at)

    def out_at(g, b, me, slots, row_partner):
        return b, 0, rem(blocks.row_of(g, me, row_partner), half_rows), 0

    return pl.pallas_call(
        functools.partial(left_kernel, blocks, block_cols, per_step),
        grid_spec=pltpu.PrefetchScalarGridSpec(
            num_scalar_prefetch=3,
            grid=(half_rows, block_cols // per_step),
            in_specs=[tile_spec(index) for index in range(per_step)] + blocks.specs,
            out_specs=pl.BlockSpec((per_step, 2, width, tile_order), out_at),
            scratch_shapes=[pltpu.VMEM((2 * width, tile_order), BF16)],
        ),
        out_shape=jax.ShapeDtypeStruct((block_cols, 2, half_rows * width, tile_order), BF16),
        compiler_params=PARAMS,
        cost_estimate=cost(12 * half_rows * block_cols * width * tile_order * tile_order),
        name="left_products",
    )(me, slots, row_partner, *[tiles] * per_step, *blocks.operands)


class Columns:
    ON, REST, KEPT = range(3)

    def __init__(self, kind, block_cols):
        self.kind = kind
        self.half_cols = block_cols // 2
        self.steps = block_cols if kind == self.KEPT else self.half_cols

    def half(self, step, me, row_partner, col_partner):
        if self.kind == self.KEPT:
            goes_on = (me[1] < col_partner[me[0], me[1]]).astype(jnp.int32)
            return goes_on ^ div(step, self.half_cols)
        goes_on = (me[1] < col_partner[row_partner[me[1], me[0]], me[1]]).astype(jnp.int32)
        return goes_on ^ (1 if self.kind == self.REST else 0)

    def column(self, step, me, row_partner, col_partner):
        half = self.half(step, me, row_partner, col_partner)
        return half * self.half_cols + rem(step, self.half_cols)


def packed_first(blocks):
    return max(1, blocks // 2)


def packed_place(slots, first_row, first_col, half_rows, half_cols, block_cols, block):
    before = here = count = jnp.int32(0)
    for index in range(half_rows * half_cols):
        place = (first_row + index % half_rows) * block_cols + first_col + index // half_rows
        flag = (slots[place] >= 0).astype(jnp.int32)
        before = before + jnp.where(index < block, flag, 0)
        here = here + jnp.where(index == block, flag, 0)
        count = count + flag
    return jnp.where(here == 1, before, count + block - before), here == 1


def quarter_live(table, first_row, first_col, half_rows, half_cols, block_cols):
    count = jnp.int32(0)
    for index in range(half_rows * half_cols):
        place = (first_row + index % half_rows) * block_cols + first_col + index // half_rows
        count = count + (table[place] >= 0).astype(jnp.int32)
    return count


def right_kernel(columns, block_cols, half_rows, shard_places, groups, *refs):
    me, slots, mate_slots, row_partner, col_partner, w_ref = refs[:6]
    pieces = refs[6 : 6 + sum(groups)]
    step = pl.program_id(0)
    tile_order = w_ref.shape[3]
    depth, width = pieces[0].shape
    packs = columns.kind == Columns.REST
    outs = refs[6 + sum(groups) : -3 if packs else -2]
    p_high, p_low = refs[-2:]

    @pl.when(step == 0)
    def _():
        at = 0
        for place, count in zip(shard_places(me), groups):
            value = pieces[at][...]
            for other in range(1, count):
                value = value + pieces[at + other][...]
            at += count
            rows = pl.ds(pl.multiple_of(place * depth, depth), depth)
            p_high[rows, :], p_low[rows, :] = split(value)

    column = columns.column(step, me, row_partner, col_partner)
    rows = pl.ds(pl.multiple_of(column * tile_order, tile_order), tile_order)
    both = w_ref[0].reshape(2 * w_ref.shape[2], tile_order)
    block = product(both, p_high[rows, :], p_low[rows, :])
    half_cols = columns.half_cols
    if not packs:
        for index, out in enumerate(outs):

            @pl.when(jnp.minimum(step, half_cols) == index)
            def _():
                out[...] = block

        return
    branch, *outs = outs
    packed = refs[-3]
    first_row = half_of(True, me, row_partner) * half_rows
    first_col = columns.half(step, me, row_partner, col_partner) * half_cols
    for row in range(half_rows):
        place, _ = packed_place(
            slots, first_row, first_col, half_rows, half_cols, block_cols, step * half_rows + row
        )
        packed[place] = block[row * width : (row + 1) * width]

    @pl.when(step == half_cols - 1)
    def _():
        count = outs[0].shape[0]
        outs[0][...] = packed[:count]
        for index, out in enumerate(outs[1:]):
            out[...] = packed[count + index]
        keeps = (me[1] > col_partner[me[0], me[1]]).astype(jnp.int32)
        mate_row = half_of(False, me, row_partner) * half_rows
        quarter = half_rows, half_cols, block_cols
        most = jnp.maximum(
            quarter_live(slots, first_row, first_col, *quarter),
            quarter_live(mate_slots, mate_row, keeps * half_cols, *quarter),
        )
        choice = jnp.clip(most - count, 0, len(outs) - 1)
        branch[0] = ((me[0] ^ row_partner[me[1], me[0]]) - 1) * len(outs) + choice


def right_products(kind, tables, w, shards, shard_places, half_rows):
    block_cols, _, height, tile_order = w.shape
    columns = Columns(kind, block_cols)
    half_cols = columns.half_cols
    depth, width = shards[0][0].shape
    groups = [len(shard) for shard in shards]
    blocks = half_rows * half_cols

    def w_at(i, me, slots, mate_slots, row_partner, col_partner):
        return columns.column(i, me, row_partner, col_partner), 0, 0, 0

    scratch = [pltpu.VMEM((len(shards) * depth, width), BF16)] * 2
    if kind == Columns.REST:
        most = packed_first(blocks)
        shapes = [(most, width, width)] + [(width, width)] * (blocks - most)
        out_specs = [pl.BlockSpec(memory_space=pltpu.SMEM)]
        out_specs += [pl.BlockSpec(shape, lambda i, *_, n=len(shape): (0,) * n) for shape in shapes]
        scratch = [pltpu.VMEM((blocks, width, width), F32)] + scratch
    else:
        shapes = [(height, width)] * half_cols
        out_specs = [pl.BlockSpec((height, width), lambda i, *_: (0, 0))] * half_cols
        if kind == Columns.KEPT:
            shapes += [(height, half_cols * width)]
            out_specs += [
                pl.BlockSpec((height, width), lambda i, *_: (0, jnp.maximum(i - half_cols, 0)))
            ]
    out_shape = [jax.ShapeDtypeStruct(shape, F32) for shape in shapes]
    if kind == Columns.REST:
        out_shape = [jax.ShapeDtypeStruct((1,), jnp.int32)] + out_shape
    return pl.pallas_call(
        functools.partial(right_kernel, columns, block_cols, half_rows, shard_places, groups),
        grid_spec=pltpu.PrefetchScalarGridSpec(
            num_scalar_prefetch=5,
            grid=(columns.steps,),
            in_specs=[pl.BlockSpec((1, 2, height, tile_order), w_at)]
            + [pl.BlockSpec(memory_space=pltpu.VMEM)] * sum(groups),
            out_specs=out_specs,
            scratch_shapes=scratch,
        ),
        out_shape=out_shape,
        compiler_params=PARAMS,
        cost_estimate=cost(6 * columns.steps * height * width * tile_order),
        name="right_products",
    )(*tables, w, *[piece for shard in shards for piece in shard])


def sum_kernel(half_rows, block_cols, singles, sections, *refs):
    me, _, mate_slots, row_partner, col_partner, kept_ref, packed_ref = refs[:7]
    single_refs, section_refs, out = refs[7 : 7 + singles], refs[7 + singles : -1], refs[-1]
    half_cols = block_cols // 2
    step = pl.program_id(0)
    keeps = (me[1] > col_partner[me[0], me[1]]).astype(jnp.int32)
    first_row = half_of(False, me, row_partner) * half_rows
    place, live = packed_place(
        mate_slots, first_row, keeps * half_cols, half_rows, half_cols, block_cols, step
    )
    count = packed_ref.shape[0]
    distance = me[1] ^ col_partner[me[0], me[1]]
    at = 0
    for index, kind in enumerate(sections):
        for which in range(kind):
            section = section_refs[at + which]
            wanted = div(step, half_rows) == index
            if kind > 1:
                core = rem(distance, 2) == 1
                wanted &= core if which == 0 else jnp.logical_not(core) & (div(distance, 2) == which - 1)

            @pl.when(wanted)
            def _():
                out[...] = kept_ref[...] + section[...].reshape(out.shape)

        at += kind

    @pl.when(live & (place < count))
    def _():
        out[...] += packed_ref[jnp.minimum(place, count - 1)]

    for index, single in enumerate(single_refs):

        @pl.when(live & (place == count + index))
        def _():
            out[...] += single[...]


def sum_blocks(tables, half_rows, block_cols, kept, packed, singles, sections):
    half_cols = block_cols // 2
    height, both = kept.shape
    width = both // half_cols
    block = pl.BlockSpec((width, width), lambda i, *_: (rem(i, half_rows), div(i, half_rows)))

    def section_spec(index, section):
        def section_at(i, me, slots, mate_slots, row_partner, col_partner):
            here = jnp.clip(i - index * half_rows, 0, half_rows - 1)
            return (col_partner[me[0], me[1]], here, 0) if section.ndim == 3 else (here, 0)

        return pl.BlockSpec((1,) * (section.ndim - 2) + (width, width), section_at)

    return pl.pallas_call(
        functools.partial(
            sum_kernel, half_rows, block_cols, len(singles), [len(each) for each in sections]
        ),
        grid_spec=pltpu.PrefetchScalarGridSpec(
            num_scalar_prefetch=5,
            grid=(half_rows * half_cols,),
            in_specs=[block]
            + [pl.BlockSpec(memory_space=pltpu.VMEM)] * (1 + len(singles))
            + [section_spec(index, each) for index, group in enumerate(sections) for each in group],
            out_specs=block,
        ),
        out_shape=jax.ShapeDtypeStruct((height, both), F32),
        compiler_params=PARAMS,
        name="sum_blocks",
    )(*tables, kept, packed, *singles, *[each for group in sections for each in group])


def flip(value, axis, size, mask):
    return lax.ppermute(value, axis, [(i, i ^ mask) for i in range(size)])


def gather_prolong(shard, axis, size):
    if size != 4:
        gathered = lax.all_gather(shard, axis)
        return [[gathered[i]] for i in range(size)], lambda me: list(range(size))
    by_two = flip(shard, axis, size, 2)
    by_one = flip(shard, axis, size, 1)
    middle = lax.ppermute(shard, axis, [(1, 2), (2, 1)])
    handed = lax.ppermute(by_two, axis, [(1, 0), (2, 3)])
    return [[shard], [by_one], [by_two], [middle, handed]], lambda me: [me[0] ^ m for m in range(4)]


def pair_switch(index, size, branch, operand, choices=1):
    branches = [
        functools.partial(branch, mask, choice) for mask in range(1, size) for choice in range(choices)
    ]
    return lax.switch(index[0], branches, operand)


def solution(mesh):
    n_row = mesh.shape["row"]
    n_col = mesh.shape["col"]

    def body(tiles, coords, counts, restrict, prolong, row_partner, col_partner):
        tile_order = tiles.shape[1]
        block_rows = restrict.shape[0] * n_col // tile_order
        block_cols = prolong.shape[0] * n_row // tile_order
        half_rows, half_cols = block_rows // 2, block_cols // 2
        row = lax.axis_index("row").astype(jnp.int32)
        col = lax.axis_index("col").astype(jnp.int32)
        me = jnp.stack([row, col])

        places = block_rows * block_cols
        slots, first, across = make_tables(
            me, row_partner, col_partner, coords, counts, places, block_cols
        )
        q_rows = lax.all_gather(restrict, "col", axis=0, tiled=True)
        shards, shard_places = gather_prolong(prolong, "row", n_row)

        def left(given):
            blocks = WholeBlocks(given, q_rows, tile_order, half_rows)
            return left_products(me, slots, row_partner, tiles, blocks, half_rows, block_cols)

        def right(kind, w, mate_slots):
            tables = (me, slots, mate_slots, row_partner, col_partner)
            return right_products(kind, tables, w, shards, shard_places, half_rows)

        def swap_first(mask, _, chunk):
            received = flip(chunk, "row", n_row, mask)
            return received, flip(slots, "row", n_row, mask), right(Columns.KEPT, left(False), slots)

        def swap_next(mask, _, operands):
            chunk, mate_slots = operands
            return flip(chunk, "row", n_row, mask), right(Columns.REST, w, mate_slots)

        def swap_more(mask, _, operands):
            return flip(operands[0], "row", n_row, mask), operands[1:]

        def swap_rest(mask, extra, rest):
            return [
                flip(array, "row", n_row, mask) if index <= extra else array
                for index, array in enumerate(rest)
            ]

        w = left(True)
        given = right(Columns.ON, w, slots)
        received, mate_slots, kept = pair_switch(first, n_row, swap_first, given[0])
        sections, rest = [], None
        for index in range(half_cols):
            section = kept[index] + received
            over = None
            if index == 0 and n_col == 8 and half_cols > 1:
                over = [section] + [flip(section, "col", n_col, 2 * chip) for chip in range(1, 4)]
            else:
                sections.append([lax.all_gather(section, "col")])
            if index + 1 == half_cols:
                break
            chunk, section = lax.optimization_barrier((given[index + 1], section))
            if index == 0:
                received, rest = pair_switch(first, n_row, swap_next, (chunk, mate_slots))
            else:
                received, *_ = pair_switch(first, n_row, swap_more, (chunk,))
            if over is not None:
                over, received = lax.optimization_barrier((over, received))
                chip = (col ^ 1 ^ col_partner[row, col ^ 1]) >> 1
                wanted = jnp.where(
                    chip < 2,
                    jnp.where(chip == 0, over[0], over[1]),
                    jnp.where(chip == 2, over[2], over[3]),
                )
                sections.append([flip(wanted, "col", n_col, 1)] + over)
        if rest is None:
            rest = right(Columns.REST, w, mate_slots)
        second, *rest = rest
        rest, section = lax.optimization_barrier((rest, section))
        packed, *singles = pair_switch(second, n_row, swap_rest, rest, len(rest))
        tables = (me, slots, mate_slots, row_partner, col_partner)
        return sum_blocks(tables, half_rows, block_cols, kept[-1], packed, singles, sections)

    in_specs = (
        P(("row", "col"), None, None),
        P(("row", "col"), None),
        P(("row", "col")),
        P(("row", "col"), None),
        P(("col", "row"), None),
        P(),
        P(),
    )
    return jax.shard_map(
        body, mesh=mesh, in_specs=in_specs, out_specs=P("row", "col"), check_vma=False
    )
```

```python
import functools

import jax
import jax.numpy as jnp
from jax import lax
from jax.experimental import pallas as pl
from jax.experimental.pallas import tpu as pltpu
from jax.sharding import PartitionSpec as P

F32 = jnp.float32
BF16 = jnp.bfloat16
VMEM_BYTES = 48 * 1024 * 1024
PARAMS = pltpu.CompilerParams(vmem_limit_bytes=VMEM_BYTES)


def cost(flops):
    return pl.CostEstimate(flops=flops, bytes_accessed=0, transcendentals=0)


def split(value):
    high = value.astype(BF16)
    low = (value - high.astype(F32)).astype(BF16)
    return high, low


def dot(left, right):
    return jnp.dot(left, right, preferred_element_type=F32)


def product(left_both, right_high, right_low):
    half = left_both.shape[0] // 2
    total = dot(left_both[half:], right_high)
    total = total + dot(left_both[:half], right_low)
    return total + dot(left_both[:half], right_high)


def div(value, by):
    return lax.div(value, jnp.int32(by))


def rem(value, by):
    return lax.rem(value, jnp.int32(by))


def half_of(given, me, row_partner):
    mate = row_partner[me[0], me[1]]
    return ((mate > me[0]) if given else (me[0] > mate)).astype(jnp.int32)


def tables_kernel(block_cols, me, row_partner, col_partner, coords, counts, slots, first, wish):
    for place in range(slots.shape[0]):
        slots[place] = jnp.int32(-1)
    for slot in range(coords.shape[1]):

        @pl.when(slot < counts[0])
        def _():
            slots[coords[0, slot] * block_cols + coords[1, slot]] = jnp.int32(slot)

    first[0] = (me[0] ^ row_partner[me[0], me[1]]) - 1
    other = me[1] ^ 1
    wish[0] = div(other ^ col_partner[me[0], other], 2)


def make_tables(me, row_partner, col_partner, coords, counts, places, block_cols):
    smem = pl.BlockSpec(memory_space=pltpu.SMEM)
    return pl.pallas_call(
        functools.partial(tables_kernel, block_cols),
        in_specs=[smem] * 5,
        out_specs=[smem] * 3,
        out_shape=[jax.ShapeDtypeStruct((n,), jnp.int32) for n in (places, 1, 1)],
        cost_estimate=cost(0),
        name="make_tables",
    )(me, row_partner, col_partner, coords, counts)


class Columns:
    ON, REST, KEPT = range(3)

    def __init__(self, kind, block_cols):
        self.kind = kind
        self.given = kind != self.KEPT
        self.half_cols = block_cols // 2
        self.steps = block_cols if kind == self.KEPT else self.half_cols

    def half(self, step, me, row_partner, col_partner):
        if self.kind == self.KEPT:
            goes_on = (me[1] < col_partner[me[0], me[1]]).astype(jnp.int32)
            return goes_on ^ div(step, self.half_cols)
        goes_on = (me[1] < col_partner[row_partner[me[0], me[1]], me[1]]).astype(jnp.int32)
        return goes_on ^ (1 if self.kind == self.REST else 0)

    def column(self, step, me, row_partner, col_partner):
        half = self.half(step, me, row_partner, col_partner)
        return half * self.half_cols + rem(step, self.half_cols)


def left_kernel(columns, block_cols, half_rows, per_step, *refs):
    me, slots, row_partner, col_partner = refs[:4]
    q_ref, tile_refs, out, q_both = refs[4], refs[5:-2], refs[-2], refs[-1]
    group, step = pl.program_id(0), pl.program_id(1)
    width = q_both.shape[0] // 2

    @pl.when(step == 0)
    def _():
        high, low = split(q_ref[...].T)
        q_both[:width] = high
        q_both[width:] = low

    block_row = half_of(columns.given, me, row_partner) * half_rows + group
    for index, tile_ref in enumerate(tile_refs):
        column = columns.column(step * per_step + index, me, row_partner, col_partner)
        live = slots[block_row * block_cols + column] >= 0
        high, low = split(tile_ref[0])
        total = jnp.where(live, product(q_both[...], high, low), 0.0)
        out[index, 0], out[index, 1] = split(total)


def left_products(kind, tables, tiles, q_rows, half_rows, block_cols):
    _, tile_order, _ = tiles.shape
    width = q_rows.shape[1]
    columns = Columns(kind, block_cols)
    per_step = 2 if columns.steps % 2 == 0 else 1

    def row_of(g, me, row_partner):
        return half_of(columns.given, me, row_partner) * half_rows + g

    def tile_spec(index):
        def tile_at(g, b, me, slots, row_partner, col_partner):
            column = columns.column(b * per_step + index, me, row_partner, col_partner)
            return jnp.maximum(slots[row_of(g, me, row_partner) * block_cols + column], 0), 0, 0

        return pl.BlockSpec((1, tile_order, tile_order), tile_at)

    return pl.pallas_call(
        functools.partial(left_kernel, columns, block_cols, half_rows, per_step),
        grid_spec=pltpu.PrefetchScalarGridSpec(
            num_scalar_prefetch=4,
            grid=(half_rows, columns.steps // per_step),
            in_specs=[
                pl.BlockSpec(
                    (tile_order, width),
                    lambda g, b, me, slots, row_partner, _: (row_of(g, me, row_partner), 0),
                )
            ]
            + [tile_spec(index) for index in range(per_step)],
            out_specs=pl.BlockSpec(
                (per_step, 2, width, tile_order), lambda g, b, *_: (b, 0, g, 0)
            ),
            scratch_shapes=[pltpu.VMEM((2 * width, tile_order), BF16)],
        ),
        out_shape=jax.ShapeDtypeStruct((columns.steps, 2, half_rows * width, tile_order), BF16),
        compiler_params=PARAMS,
        cost_estimate=cost(12 * half_rows * columns.steps * width * tile_order * tile_order),
        name="left_products",
    )(*tables, q_rows, *[tiles] * per_step)


def packed_first(blocks):
    return max(1, blocks // 2)


def packed_place(slots, first_row, first_col, half_rows, half_cols, block_cols, block):
    before = here = count = jnp.int32(0)
    for index in range(half_rows * half_cols):
        place = (first_row + index % half_rows) * block_cols + first_col + index // half_rows
        flag = (slots[place] >= 0).astype(jnp.int32)
        before = before + jnp.where(index < block, flag, 0)
        here = here + jnp.where(index == block, flag, 0)
        count = count + flag
    return jnp.where(here == 1, before, count + block - before), here == 1


def quarter_live(table, first_row, first_col, half_rows, half_cols, block_cols):
    count = jnp.int32(0)
    for index in range(half_rows * half_cols):
        place = (first_row + index % half_rows) * block_cols + first_col + index // half_rows
        count = count + (table[place] >= 0).astype(jnp.int32)
    return count


def right_kernel(columns, block_cols, half_rows, shard_places, groups, *refs):
    me, slots, mate_slots, row_partner, col_partner, w_ref = refs[:6]
    pieces = refs[6 : 6 + sum(groups)]
    step = pl.program_id(0)
    tile_order = w_ref.shape[3]
    depth, width = pieces[0].shape
    packs = columns.kind == Columns.REST
    outs = refs[6 + sum(groups) : -3 if packs else -2]
    p_high, p_low = refs[-2:]

    @pl.when(step == 0)
    def _():
        at = 0
        half = columns.half(step, me, row_partner, col_partner)
        for place, count in zip(shard_places(me), groups):
            wanted = div(place * depth, columns.half_cols * tile_order) == half
            if columns.kind == Columns.KEPT:
                wanted = place >= 0

            @pl.when(wanted)
            def _():
                value = pieces[at][...]
                for other in range(1, count):
                    value = value + pieces[at + other][...]
                rows = pl.ds(pl.multiple_of(place * depth, depth), depth)
                p_high[rows, :], p_low[rows, :] = split(value)

            at += count

    column = columns.column(step, me, row_partner, col_partner)
    rows = pl.ds(pl.multiple_of(column * tile_order, tile_order), tile_order)
    both = w_ref[0].reshape(2 * w_ref.shape[2], tile_order)
    block = product(both, p_high[rows, :], p_low[rows, :])
    half_cols = columns.half_cols
    if not packs:
        for index, out in enumerate(outs):

            @pl.when(jnp.minimum(step, half_cols) == index)
            def _():
                out[...] = block

        return
    branch, *outs = outs
    packed = refs[-3]
    first_row = half_of(True, me, row_partner) * half_rows
    first_col = columns.half(step, me, row_partner, col_partner) * half_cols
    for row in range(half_rows):
        place, _ = packed_place(
            slots, first_row, first_col, half_rows, half_cols, block_cols, step * half_rows + row
        )
        packed[place] = block[row * width : (row + 1) * width]

    @pl.when(step == half_cols - 1)
    def _():
        count = outs[0].shape[0]
        outs[0][...] = packed[:count]
        for index, out in enumerate(outs[1:]):
            out[...] = packed[count + index]
        keeps = (me[1] > col_partner[me[0], me[1]]).astype(jnp.int32)
        mate_row = half_of(False, me, row_partner) * half_rows
        quarter = half_rows, half_cols, block_cols
        most = jnp.maximum(
            quarter_live(slots, first_row, first_col, *quarter),
            quarter_live(mate_slots, mate_row, keeps * half_cols, *quarter),
        )
        choice = jnp.clip(most - count, 0, len(outs) - 1)
        branch[0] = ((me[0] ^ row_partner[me[0], me[1]]) - 1) * len(outs) + choice


def right_products(kind, tables, w, shards, shard_places, half_rows, block_cols):
    _, _, height, tile_order = w.shape
    columns = Columns(kind, block_cols)
    half_cols = columns.half_cols
    depth, width = shards[0][0].shape
    groups = [len(shard) for shard in shards]
    blocks = half_rows * half_cols

    scratch = [pltpu.VMEM((len(shards) * depth, width), BF16)] * 2
    if kind == Columns.REST:
        most = packed_first(blocks)
        shapes = [(most, width, width)] + [(width, width)] * (blocks - most)
        out_specs = [pl.BlockSpec(memory_space=pltpu.SMEM)]
        out_specs += [pl.BlockSpec(shape, lambda i, *_, n=len(shape): (0,) * n) for shape in shapes]
        scratch = [pltpu.VMEM((blocks, width, width), F32)] + scratch
    else:
        shapes = [(height, width)] * half_cols
        out_specs = [pl.BlockSpec((height, width), lambda i, *_: (0, 0))] * half_cols
        if kind == Columns.KEPT:
            shapes += [(height, half_cols * width)]
            out_specs += [
                pl.BlockSpec((height, width), lambda i, *_: (0, jnp.maximum(i - half_cols, 0)))
            ]
    out_shape = [jax.ShapeDtypeStruct(shape, F32) for shape in shapes]
    if kind == Columns.REST:
        out_shape = [jax.ShapeDtypeStruct((1,), jnp.int32)] + out_shape
    return pl.pallas_call(
        functools.partial(right_kernel, columns, block_cols, half_rows, shard_places, groups),
        grid_spec=pltpu.PrefetchScalarGridSpec(
            num_scalar_prefetch=5,
            grid=(columns.steps,),
            in_specs=[pl.BlockSpec((1, 2, height, tile_order), lambda i, *_: (i, 0, 0, 0))]
            + [pl.BlockSpec(memory_space=pltpu.VMEM)] * sum(groups),
            out_specs=out_specs,
            scratch_shapes=scratch,
        ),
        out_shape=out_shape,
        compiler_params=PARAMS,
        cost_estimate=cost(6 * columns.steps * height * width * tile_order),
        name="right_products",
    )(*tables, w, *[piece for shard in shards for piece in shard])


def sum_kernel(half_rows, block_cols, singles, sections, *refs):
    me, _, mate_slots, row_partner, col_partner, kept_ref, packed_ref = refs[:7]
    single_refs, section_refs, out = refs[7 : 7 + singles], refs[7 + singles : -1], refs[-1]
    half_cols = block_cols // 2
    step = pl.program_id(0)
    keeps = (me[1] > col_partner[me[0], me[1]]).astype(jnp.int32)
    first_row = half_of(False, me, row_partner) * half_rows
    place, live = packed_place(
        mate_slots, first_row, keeps * half_cols, half_rows, half_cols, block_cols, step
    )
    count = packed_ref.shape[0]
    distance = me[1] ^ col_partner[me[0], me[1]]
    at = 0
    for index, kind in enumerate(sections):
        for which in range(kind):
            section = section_refs[at + which]
            wanted = div(step, half_rows) == index
            if kind > 1:
                core = rem(distance, 2) == 1
                wanted &= core if which == 0 else jnp.logical_not(core) & (div(distance, 2) == which - 1)

            @pl.when(wanted)
            def _():
                out[...] = kept_ref[...] + section[...].reshape(out.shape)

        at += kind

    @pl.when(live & (place < count))
    def _():
        out[...] += packed_ref[jnp.minimum(place, count - 1)]

    for index, single in enumerate(single_refs):

        @pl.when(live & (place == count + index))
        def _():
            out[...] += single[...]


def sum_blocks(tables, half_rows, block_cols, kept, packed, singles, sections):
    half_cols = block_cols // 2
    height, both = kept.shape
    width = both // half_cols
    block = pl.BlockSpec((width, width), lambda i, *_: (rem(i, half_rows), div(i, half_rows)))

    def section_spec(index, section):
        def section_at(i, me, slots, mate_slots, row_partner, col_partner):
            here = jnp.clip(i - index * half_rows, 0, half_rows - 1)
            return (col_partner[me[0], me[1]], here, 0) if section.ndim == 3 else (here, 0)

        return pl.BlockSpec((1,) * (section.ndim - 2) + (width, width), section_at)

    return pl.pallas_call(
        functools.partial(
            sum_kernel, half_rows, block_cols, len(singles), [len(each) for each in sections]
        ),
        grid_spec=pltpu.PrefetchScalarGridSpec(
            num_scalar_prefetch=5,
            grid=(half_rows * half_cols,),
            in_specs=[block]
            + [pl.BlockSpec(memory_space=pltpu.VMEM)] * (1 + len(singles))
            + [section_spec(index, each) for index, group in enumerate(sections) for each in group],
            out_specs=block,
        ),
        out_shape=jax.ShapeDtypeStruct((height, both), F32),
        compiler_params=PARAMS,
        name="sum_blocks",
    )(*tables, kept, packed, *singles, *[each for group in sections for each in group])


def flip(value, axis, size, mask):
    return lax.ppermute(value, axis, [(i, i ^ mask) for i in range(size)])


def gather_prolong(shard, axis, size):
    if size != 4:
        gathered = lax.all_gather(shard, axis)
        return [[gathered[i]] for i in range(size)], lambda me: list(range(size))
    by_two = flip(shard, axis, size, 2)
    by_one = flip(shard, axis, size, 1)
    after, by_two = lax.optimization_barrier((shard, by_two))
    handed = lax.ppermute(by_two, axis, [(1, 0), (2, 3)])
    middle = lax.ppermute(after, axis, [(1, 2), (2, 1)])
    return [[shard], [by_one], [by_two], [middle, handed]], lambda me: [me[0] ^ m for m in range(4)]


def pair_switch(index, size, branch, operand, choices=1):
    branches = [
        functools.partial(branch, mask, choice) for mask in range(1, size) for choice in range(choices)
    ]
    return lax.switch(index[0], branches, operand)


def solution(mesh):
    n_row = mesh.shape["row"]
    n_col = mesh.shape["col"]

    def body(tiles, coords, counts, restrict, prolong, row_partner, col_partner):
        tile_order = tiles.shape[1]
        block_rows = restrict.shape[0] * n_col // tile_order
        block_cols = prolong.shape[0] * n_row // tile_order
        half_rows, half_cols = block_rows // 2, block_cols // 2
        row = lax.axis_index("row").astype(jnp.int32)
        col = lax.axis_index("col").astype(jnp.int32)
        me = jnp.stack([row, col])

        row_partner, coords = row_partner.T, coords.T
        places = block_rows * block_cols
        slots, first, wish = make_tables(
            me, row_partner, col_partner, coords, counts, places, block_cols
        )
        shards, shard_places = gather_prolong(prolong, "row", n_row)
        q_rows = lax.all_gather(restrict, "col", axis=0, tiled=True)

        def products(kind, mate_slots):
            tables = (me, slots, row_partner, col_partner)
            w = left_products(kind, tables, tiles, q_rows, half_rows, block_cols)
            tables = (me, slots, mate_slots, row_partner, col_partner)
            return right_products(kind, tables, w, shards, shard_places, half_rows, block_cols)

        def swap_first(mask, _, chunk):
            received = flip(chunk, "row", n_row, mask)
            return received, flip(slots, "row", n_row, mask), products(Columns.KEPT, slots)

        def swap_next(mask, _, operands):
            chunk, mate_slots = operands
            return flip(chunk, "row", n_row, mask), products(Columns.REST, mate_slots)

        def swap_more(mask, _, operands):
            return flip(operands[0], "row", n_row, mask), operands[1:]

        def swap_rest(mask, extra, rest):
            return [
                flip(array, "row", n_row, mask) if index <= extra else array
                for index, array in enumerate(rest)
            ]

        given = products(Columns.ON, slots)
        received, mate_slots, kept = pair_switch(first, n_row, swap_first, given[0])
        sections, rest = [], None
        for index in range(half_cols):
            section = kept[index] + received
            over = None
            if index == 0 and n_col == 8 and half_cols > 1:
                over = [section] + [flip(section, "col", n_col, 2 * chip) for chip in range(1, 4)]
            else:
                sections.append([lax.all_gather(section, "col")])
            if index + 1 == half_cols:
                break
            chunk, section = lax.optimization_barrier((given[index + 1], section))
            if index == 0:
                received, rest = pair_switch(first, n_row, swap_next, (chunk, mate_slots))
            else:
                received, *_ = pair_switch(first, n_row, swap_more, (chunk,))
            if over is not None:
                over, received = lax.optimization_barrier((over, received))
                chip = wish[0]
                wanted = jnp.where(
                    chip < 2,
                    jnp.where(chip == 0, over[0], over[1]),
                    jnp.where(chip == 2, over[2], over[3]),
                )
                sections.append([flip(wanted, "col", n_col, 1)] + over)
        if rest is None:
            rest = products(Columns.REST, mate_slots)
        second, *rest = rest
        rest, section = lax.optimization_barrier((rest, section))
        packed, *singles = pair_switch(second, n_row, swap_rest, rest, len(rest))
        tables = (me, slots, mate_slots, row_partner, col_partner)
        return sum_blocks(tables, half_rows, block_cols, kept[-1], packed, singles, sections)

    in_specs = (
        P(("row", "col"), None, None),
        P(("row", "col"), None),
        P(("row", "col")),
        P(("row", "col"), None),
        P(("col", "row"), None),
        P(),
        P(),
    )
    return jax.shard_map(
        body, mesh=mesh, in_specs=in_specs, out_specs=P("row", "col"), check_vma=False
    )
```

```python
import functools

import jax
import jax.numpy as jnp
from jax import lax
from jax.experimental import pallas as pl
from jax.experimental.pallas import tpu as pltpu
from jax.sharding import PartitionSpec as P

F32 = jnp.float32
BF16 = jnp.bfloat16
VMEM_BYTES = 48 * 1024 * 1024
PARAMS = pltpu.CompilerParams(vmem_limit_bytes=VMEM_BYTES)


def cost(flops):
    return pl.CostEstimate(flops=flops, bytes_accessed=0, transcendentals=0)


def split(value):
    high = value.astype(BF16)
    low = (value - high.astype(F32)).astype(BF16)
    return high, low


def dot(left, right):
    return jnp.dot(left, right, preferred_element_type=F32)


def product(left_both, right_high, right_low):
    half = left_both.shape[0] // 2
    total = dot(left_both[half:], right_high)
    total = total + dot(left_both[:half], right_low)
    return total + dot(left_both[:half], right_high)


def div(value, by):
    return lax.div(value, jnp.int32(by))


def rem(value, by):
    return lax.rem(value, jnp.int32(by))


def half_of(given, me, row_partner):
    mate = row_partner[me[0], me[1]]
    return ((mate > me[0]) if given else (me[0] > mate)).astype(jnp.int32)


def tables_kernel(block_cols, me, row_partner, col_partner, coords, counts, slots, first, wish):
    for place in range(slots.shape[0]):
        slots[place] = jnp.int32(-1)
    for slot in range(coords.shape[1]):

        @pl.when(slot < counts[0])
        def _():
            slots[coords[0, slot] * block_cols + coords[1, slot]] = jnp.int32(slot)

    first[0] = (me[0] ^ row_partner[me[0], me[1]]) - 1
    other = me[1] ^ 1
    wish[0] = div(other ^ col_partner[me[0], other], 2)


def make_tables(me, row_partner, col_partner, coords, counts, places, block_cols):
    smem = pl.BlockSpec(memory_space=pltpu.SMEM)
    return pl.pallas_call(
        functools.partial(tables_kernel, block_cols),
        in_specs=[smem] * 5,
        out_specs=[smem] * 3,
        out_shape=[jax.ShapeDtypeStruct((n,), jnp.int32) for n in (places, 1, 1)],
        cost_estimate=cost(0),
        name="make_tables",
    )(me, row_partner, col_partner, coords, counts)


class Columns:
    ON, REST, KEPT = range(3)

    def __init__(self, kind, block_cols):
        self.kind = kind
        self.given = kind != self.KEPT
        self.half_cols = block_cols // 2
        self.steps = block_cols if kind == self.KEPT else self.half_cols

    def half(self, step, me, row_partner, col_partner):
        if self.kind == self.KEPT:
            goes_on = (me[1] < col_partner[me[0], me[1]]).astype(jnp.int32)
            return goes_on ^ div(step, self.half_cols)
        goes_on = (me[1] < col_partner[row_partner[me[0], me[1]], me[1]]).astype(jnp.int32)
        return goes_on ^ (1 if self.kind == self.REST else 0)

    def column(self, step, me, row_partner, col_partner):
        half = self.half(step, me, row_partner, col_partner)
        return half * self.half_cols + rem(step, self.half_cols)


def left_kernel(columns, block_cols, half_rows, per_step, *refs):
    me, slots, row_partner, col_partner = refs[:4]
    q_ref, tile_refs, out, q_both = refs[4], refs[5:-2], refs[-2], refs[-1]
    group, step = pl.program_id(0), pl.program_id(1)
    width = q_both.shape[0] // 2

    @pl.when(step == 0)
    def _():
        high, low = split(q_ref[...].T)
        q_both[:width] = high
        q_both[width:] = low

    block_row = half_of(columns.given, me, row_partner) * half_rows + group
    for index, tile_ref in enumerate(tile_refs):
        column = columns.column(step * per_step + index, me, row_partner, col_partner)
        live = slots[block_row * block_cols + column] >= 0
        high, low = split(tile_ref[0])
        total = jnp.where(live, product(q_both[...], high, low), 0.0)
        out[index, 0], out[index, 1] = split(total)


def left_products(kind, tables, tiles, q_rows, half_rows, block_cols):
    _, tile_order, _ = tiles.shape
    width = q_rows.shape[1]
    columns = Columns(kind, block_cols)
    per_step = 2 if columns.steps % 2 == 0 else 1

    def row_of(g, me, row_partner):
        return half_of(columns.given, me, row_partner) * half_rows + g

    def tile_spec(index):
        def tile_at(g, b, me, slots, row_partner, col_partner):
            column = columns.column(b * per_step + index, me, row_partner, col_partner)
            return jnp.maximum(slots[row_of(g, me, row_partner) * block_cols + column], 0), 0, 0

        return pl.BlockSpec((1, tile_order, tile_order), tile_at)

    return pl.pallas_call(
        functools.partial(left_kernel, columns, block_cols, half_rows, per_step),
        grid_spec=pltpu.PrefetchScalarGridSpec(
            num_scalar_prefetch=4,
            grid=(half_rows, columns.steps // per_step),
            in_specs=[
                pl.BlockSpec(
                    (tile_order, width),
                    lambda g, b, me, slots, row_partner, _: (row_of(g, me, row_partner), 0),
                )
            ]
            + [tile_spec(index) for index in range(per_step)],
            out_specs=pl.BlockSpec(
                (per_step, 2, width, tile_order), lambda g, b, *_: (b, 0, g, 0)
            ),
            scratch_shapes=[pltpu.VMEM((2 * width, tile_order), BF16)],
        ),
        out_shape=jax.ShapeDtypeStruct((columns.steps, 2, half_rows * width, tile_order), BF16),
        compiler_params=PARAMS,
        cost_estimate=cost(12 * half_rows * columns.steps * width * tile_order * tile_order),
        name="left_products",
    )(*tables, q_rows, *[tiles] * per_step)


def packed_first(blocks):
    return max(1, blocks // 2)


def packed_place(slots, first_row, first_col, half_rows, half_cols, block_cols, block):
    before = here = count = jnp.int32(0)
    for index in range(half_rows * half_cols):
        place = (first_row + index % half_rows) * block_cols + first_col + index // half_rows
        flag = (slots[place] >= 0).astype(jnp.int32)
        before = before + jnp.where(index < block, flag, 0)
        here = here + jnp.where(index == block, flag, 0)
        count = count + flag
    return jnp.where(here == 1, before, count + block - before), here == 1


def quarter_live(table, first_row, first_col, half_rows, half_cols, block_cols):
    count = jnp.int32(0)
    for index in range(half_rows * half_cols):
        place = (first_row + index % half_rows) * block_cols + first_col + index // half_rows
        count = count + (table[place] >= 0).astype(jnp.int32)
    return count


def right_kernel(columns, block_cols, half_rows, starts, *refs):
    me, slots, mate_slots, row_partner, col_partner, w_ref = refs[:6]
    pieces = refs[6 : 6 + len(starts)]
    step = pl.program_id(0)
    tile_order = w_ref.shape[3]
    width = pieces[0].shape[1]
    packs = columns.kind == Columns.REST
    outs = refs[6 + len(starts) : -3 if packs else -2]
    p_high, p_low = refs[-2:]

    @pl.when(step == 0)
    def _():
        half = columns.half(step, me, row_partner, col_partner)
        for (start, filled), piece in zip(starts, pieces):
            wanted = start(me) >= 0
            if columns.given:
                wanted = div(start(me), columns.half_cols * tile_order) == half
            if filled is not None:
                wanted &= filled(me)

            @pl.when(wanted)
            def _():
                depth = piece.shape[0]
                rows = pl.ds(pl.multiple_of(start(me), depth), depth)
                p_high[rows, :], p_low[rows, :] = split(piece[...])

    column = columns.column(step, me, row_partner, col_partner)
    rows = pl.ds(pl.multiple_of(column * tile_order, tile_order), tile_order)
    both = w_ref[0].reshape(2 * w_ref.shape[2], tile_order)
    block = product(both, p_high[rows, :], p_low[rows, :])
    half_cols = columns.half_cols
    if not packs:
        for index, out in enumerate(outs):

            @pl.when(jnp.minimum(step, half_cols) == index)
            def _():
                out[...] = block

        return
    branch, *outs = outs
    packed = refs[-3]
    first_row = half_of(True, me, row_partner) * half_rows
    first_col = columns.half(step, me, row_partner, col_partner) * half_cols
    for row in range(half_rows):
        place, _ = packed_place(
            slots, first_row, first_col, half_rows, half_cols, block_cols, step * half_rows + row
        )
        packed[place] = block[row * width : (row + 1) * width]

    @pl.when(step == half_cols - 1)
    def _():
        count = outs[0].shape[0]
        outs[0][...] = packed[:count]
        for index, out in enumerate(outs[1:]):
            out[...] = packed[count + index]
        keeps = (me[1] > col_partner[me[0], me[1]]).astype(jnp.int32)
        mate_row = half_of(False, me, row_partner) * half_rows
        quarter = half_rows, half_cols, block_cols
        most = jnp.maximum(
            quarter_live(slots, first_row, first_col, *quarter),
            quarter_live(mate_slots, mate_row, keeps * half_cols, *quarter),
        )
        choice = jnp.clip(most - count, 0, len(outs) - 1)
        branch[0] = ((me[0] ^ row_partner[me[0], me[1]]) - 1) * len(outs) + choice


def right_products(kind, tables, w, shards, half_rows, block_cols):
    _, _, height, tile_order = w.shape
    columns = Columns(kind, block_cols)
    half_cols = columns.half_cols
    width = shards[0][0].shape[1]
    blocks = half_rows * half_cols

    scratch = [pltpu.VMEM((block_cols * tile_order, width), BF16)] * 2
    if kind == Columns.REST:
        most = packed_first(blocks)
        shapes = [(most, width, width)] + [(width, width)] * (blocks - most)
        out_specs = [pl.BlockSpec(memory_space=pltpu.SMEM)]
        out_specs += [pl.BlockSpec(shape, lambda i, *_, n=len(shape): (0,) * n) for shape in shapes]
        scratch = [pltpu.VMEM((blocks, width, width), F32)] + scratch
    else:
        shapes = [(height, width)] * half_cols
        out_specs = [pl.BlockSpec((height, width), lambda i, *_: (0, 0))] * half_cols
        if kind == Columns.KEPT:
            shapes += [(height, half_cols * width)]
            out_specs += [
                pl.BlockSpec((height, width), lambda i, *_: (0, jnp.maximum(i - half_cols, 0)))
            ]
    out_shape = [jax.ShapeDtypeStruct(shape, F32) for shape in shapes]
    if kind == Columns.REST:
        out_shape = [jax.ShapeDtypeStruct((1,), jnp.int32)] + out_shape
    return pl.pallas_call(
        functools.partial(
            right_kernel, columns, block_cols, half_rows, [shard[1:] for shard in shards]
        ),
        grid_spec=pltpu.PrefetchScalarGridSpec(
            num_scalar_prefetch=5,
            grid=(columns.steps,),
            in_specs=[pl.BlockSpec((1, 2, height, tile_order), lambda i, *_: (i, 0, 0, 0))]
            + [pl.BlockSpec(memory_space=pltpu.VMEM)] * len(shards),
            out_specs=out_specs,
            scratch_shapes=scratch,
        ),
        out_shape=out_shape,
        compiler_params=PARAMS,
        cost_estimate=cost(6 * columns.steps * height * width * tile_order),
        name="right_products",
    )(*tables, w, *[shard[0] for shard in shards])


def sum_kernel(half_rows, block_cols, singles, sections, *refs):
    me, _, mate_slots, row_partner, col_partner, kept_ref, packed_ref = refs[:7]
    single_refs, section_refs, out = refs[7 : 7 + singles], refs[7 + singles : -1], refs[-1]
    half_cols = block_cols // 2
    step = pl.program_id(0)
    keeps = (me[1] > col_partner[me[0], me[1]]).astype(jnp.int32)
    first_row = half_of(False, me, row_partner) * half_rows
    place, live = packed_place(
        mate_slots, first_row, keeps * half_cols, half_rows, half_cols, block_cols, step
    )
    count = packed_ref.shape[0]
    distance = me[1] ^ col_partner[me[0], me[1]]
    at = 0
    for index, kind in enumerate(sections):
        for which in range(kind):
            section = section_refs[at + which]
            wanted = div(step, half_rows) == index
            if kind > 1:
                core = rem(distance, 2) == 1
                wanted &= core if which == 0 else jnp.logical_not(core) & (div(distance, 2) == which - 1)

            @pl.when(wanted)
            def _():
                out[...] = kept_ref[...] + section[...].reshape(out.shape)

        at += kind

    @pl.when(live & (place < count))
    def _():
        out[...] += packed_ref[jnp.minimum(place, count - 1)]

    for index, single in enumerate(single_refs):

        @pl.when(live & (place == count + index))
        def _():
            out[...] += single[...]


def sum_blocks(tables, half_rows, block_cols, kept, packed, singles, sections):
    half_cols = block_cols // 2
    height, both = kept.shape
    width = both // half_cols
    block = pl.BlockSpec((width, width), lambda i, *_: (rem(i, half_rows), div(i, half_rows)))

    def section_spec(index, section):
        def section_at(i, me, slots, mate_slots, row_partner, col_partner):
            here = jnp.clip(i - index * half_rows, 0, half_rows - 1)
            return (col_partner[me[0], me[1]], here, 0) if section.ndim == 3 else (here, 0)

        return pl.BlockSpec((1,) * (section.ndim - 2) + (width, width), section_at)

    return pl.pallas_call(
        functools.partial(
            sum_kernel, half_rows, block_cols, len(singles), [len(each) for each in sections]
        ),
        grid_spec=pltpu.PrefetchScalarGridSpec(
            num_scalar_prefetch=5,
            grid=(half_rows * half_cols,),
            in_specs=[block]
            + [pl.BlockSpec(memory_space=pltpu.VMEM)] * (1 + len(singles))
            + [section_spec(index, each) for index, group in enumerate(sections) for each in group],
            out_specs=block,
        ),
        out_shape=jax.ShapeDtypeStruct((height, both), F32),
        compiler_params=PARAMS,
        name="sum_blocks",
    )(*tables, kept, packed, *singles, *[each for group in sections for each in group])


def flip(value, axis, size, mask):
    return lax.ppermute(value, axis, [(i, i ^ mask) for i in range(size)])


def gather_prolong(shard, axis, size):
    depth = shard.shape[0]
    if size != 4:
        gathered = lax.all_gather(shard, axis)
        return [(gathered[i], lambda me, i=i: jnp.int32(i * depth), None) for i in range(size)]
    part = depth // 2
    parts = [shard[:part], shard[part:]]
    by_two = [flip(each, axis, size, 2) for each in parts]
    by_one = flip(shard, axis, size, 1)
    middle = lax.ppermute(shard, axis, [(1, 2), (2, 1)])
    handed = [lax.ppermute(each, axis, [(1, 0), (2, 3)]) for each in by_two]

    def at(mask, first=0):
        return lambda me: (me[0] ^ mask) * depth + first

    def inner(me):
        return (me[0] == 1) | (me[0] == 2)

    pieces = [(shard, at(0), None), (by_one, at(1), None), (middle, at(3), inner)]
    for index in range(2):
        pieces.append((by_two[index], at(2, index * part), None))
        pieces.append((handed[index], at(3, index * part), lambda me: jnp.logical_not(inner(me))))
    return pieces


def pair_switch(index, size, branch, operand, choices=1):
    branches = [
        functools.partial(branch, mask, choice) for mask in range(1, size) for choice in range(choices)
    ]
    return lax.switch(index[0], branches, operand)


def solution(mesh):
    n_row = mesh.shape["row"]
    n_col = mesh.shape["col"]

    def body(tiles, coords, counts, restrict, prolong, row_partner, col_partner):
        tile_order = tiles.shape[1]
        block_rows = restrict.shape[0] * n_col // tile_order
        block_cols = prolong.shape[0] * n_row // tile_order
        half_rows, half_cols = block_rows // 2, block_cols // 2
        row = lax.axis_index("row").astype(jnp.int32)
        col = lax.axis_index("col").astype(jnp.int32)
        me = jnp.stack([row, col])

        row_partner, coords = row_partner.T, coords.T
        places = block_rows * block_cols
        slots, first, wish = make_tables(
            me, row_partner, col_partner, coords, counts, places, block_cols
        )
        shards = gather_prolong(prolong, "row", n_row)
        q_rows = lax.all_gather(restrict, "col", axis=0, tiled=True)

        def products(kind, mate_slots):
            tables = (me, slots, row_partner, col_partner)
            w = left_products(kind, tables, tiles, q_rows, half_rows, block_cols)
            tables = (me, slots, mate_slots, row_partner, col_partner)
            return right_products(kind, tables, w, shards, half_rows, block_cols)

        def swap_first(mask, _, chunk):
            received = flip(chunk, "row", n_row, mask)
            return received, flip(slots, "row", n_row, mask), products(Columns.KEPT, slots)

        def swap_next(mask, _, operands):
            chunk, mate_slots = operands
            return flip(chunk, "row", n_row, mask), products(Columns.REST, mate_slots)

        def swap_more(mask, _, operands):
            return flip(operands[0], "row", n_row, mask), operands[1:]

        def swap_rest(mask, extra, rest):
            return [
                flip(array, "row", n_row, mask) if index <= extra else array
                for index, array in enumerate(rest)
            ]

        given = products(Columns.ON, slots)
        received, mate_slots, kept = pair_switch(first, n_row, swap_first, given[0])
        sections, rest = [], None
        for index in range(half_cols):
            section = kept[index] + received
            over = None
            if index == 0 and n_col == 8 and half_cols > 1:
                over = [section] + [flip(section, "col", n_col, 2 * chip) for chip in range(1, 4)]
            else:
                sections.append([lax.all_gather(section, "col")])
            if index + 1 == half_cols:
                break
            chunk, section = lax.optimization_barrier((given[index + 1], section))
            if index == 0:
                received, rest = pair_switch(first, n_row, swap_next, (chunk, mate_slots))
            else:
                received, *_ = pair_switch(first, n_row, swap_more, (chunk,))
            if over is not None:
                over, received = lax.optimization_barrier((over, received))
                chip = wish[0]
                wanted = jnp.where(
                    chip < 2,
                    jnp.where(chip == 0, over[0], over[1]),
                    jnp.where(chip == 2, over[2], over[3]),
                )
                sections.append([flip(wanted, "col", n_col, 1)] + over)
        if rest is None:
            rest = products(Columns.REST, mate_slots)
        second, *rest = rest
        rest, section = lax.optimization_barrier((rest, section))
        packed, *singles = pair_switch(second, n_row, swap_rest, rest, len(rest))
        tables = (me, slots, mate_slots, row_partner, col_partner)
        return sum_blocks(tables, half_rows, block_cols, kept[-1], packed, singles, sections)

    in_specs = (
        P(("row", "col"), None, None),
        P(("row", "col"), None),
        P(("row", "col")),
        P(("row", "col"), None),
        P(("col", "row"), None),
        P(),
        P(),
    )
    return jax.shard_map(
        body, mesh=mesh, in_specs=in_specs, out_specs=P("row", "col"), check_vma=False
    )
```

```python
import functools

import jax
import jax.numpy as jnp
from jax import lax
from jax.experimental import pallas as pl
from jax.experimental.pallas import tpu as pltpu
from jax.sharding import PartitionSpec as P

F32 = jnp.float32
BF16 = jnp.bfloat16
VMEM_BYTES = 48 * 1024 * 1024
PARAMS = pltpu.CompilerParams(vmem_limit_bytes=VMEM_BYTES)


def cost(flops):
    return pl.CostEstimate(flops=flops, bytes_accessed=0, transcendentals=0)


def split(value):
    high = value.astype(BF16)
    low = (value - high.astype(F32)).astype(BF16)
    return high, low


def dot(left, right):
    return jnp.dot(left, right, preferred_element_type=F32)


def product(left_both, right_high, right_low):
    half = left_both.shape[0] // 2
    total = dot(left_both[half:], right_high)
    total = total + dot(left_both[:half], right_low)
    return total + dot(left_both[:half], right_high)


def div(value, by):
    return lax.div(value, jnp.int32(by))


def rem(value, by):
    return lax.rem(value, jnp.int32(by))


def half_of(given, me, row_partner):
    mate = row_partner[me[0], me[1]]
    return ((mate > me[0]) if given else (me[0] > mate)).astype(jnp.int32)


def tables_kernel(block_cols, me, row_partner, col_partner, coords, counts, slots, first, wish):
    for place in range(slots.shape[0]):
        slots[place] = jnp.int32(-1)
    for slot in range(coords.shape[1]):

        @pl.when(slot < counts[0])
        def _():
            slots[coords[0, slot] * block_cols + coords[1, slot]] = jnp.int32(slot)

    first[0] = (me[0] ^ row_partner[me[0], me[1]]) - 1
    other = me[1] ^ 1
    wish[0] = div(other ^ col_partner[me[0], other], 2)


def make_tables(me, row_partner, col_partner, coords, counts, places, block_cols):
    smem = pl.BlockSpec(memory_space=pltpu.SMEM)
    return pl.pallas_call(
        functools.partial(tables_kernel, block_cols),
        in_specs=[smem] * 5,
        out_specs=[smem] * 3,
        out_shape=[jax.ShapeDtypeStruct((n,), jnp.int32) for n in (places, 1, 1)],
        cost_estimate=cost(0),
        name="make_tables",
    )(me, row_partner, col_partner, coords, counts)


class Columns:
    ON, REST, KEPT = range(3)

    def __init__(self, kind, block_cols):
        self.kind = kind
        self.given = kind != self.KEPT
        self.half_cols = block_cols // 2
        self.steps = block_cols if kind == self.KEPT else self.half_cols

    def half(self, step, me, row_partner, col_partner):
        if self.kind == self.KEPT:
            goes_on = (me[1] < col_partner[me[0], me[1]]).astype(jnp.int32)
            return goes_on ^ div(step, self.half_cols)
        goes_on = (me[1] < col_partner[row_partner[me[0], me[1]], me[1]]).astype(jnp.int32)
        return goes_on ^ (1 if self.kind == self.REST else 0)

    def column(self, step, me, row_partner, col_partner):
        half = self.half(step, me, row_partner, col_partner)
        return half * self.half_cols + rem(step, self.half_cols)


def left_kernel(columns, block_cols, half_rows, per_step, *refs):
    me, slots, row_partner, col_partner = refs[:4]
    q_ref, tile_refs, out, q_both = refs[4], refs[5:-2], refs[-2], refs[-1]
    group, step = pl.program_id(0), pl.program_id(1)
    width = q_both.shape[0] // 2

    @pl.when(step == 0)
    def _():
        high, low = split(q_ref[...].T)
        q_both[:width] = high
        q_both[width:] = low

    block_row = half_of(columns.given, me, row_partner) * half_rows + group
    for index, tile_ref in enumerate(tile_refs):
        column = columns.column(step * per_step + index, me, row_partner, col_partner)
        live = slots[block_row * block_cols + column] >= 0
        high, low = split(tile_ref[0])
        total = jnp.where(live, product(q_both[...], high, low), 0.0)
        out[index, 0], out[index, 1] = split(total)


def left_products(kind, tables, tiles, q_rows, half_rows, block_cols):
    _, tile_order, _ = tiles.shape
    width = q_rows.shape[1]
    columns = Columns(kind, block_cols)
    per_step = 2 if columns.steps % 2 == 0 else 1

    def row_of(g, me, row_partner):
        return half_of(columns.given, me, row_partner) * half_rows + g

    def tile_spec(index):
        def tile_at(g, b, me, slots, row_partner, col_partner):
            column = columns.column(b * per_step + index, me, row_partner, col_partner)
            return jnp.maximum(slots[row_of(g, me, row_partner) * block_cols + column], 0), 0, 0

        return pl.BlockSpec((1, tile_order, tile_order), tile_at)

    return pl.pallas_call(
        functools.partial(left_kernel, columns, block_cols, half_rows, per_step),
        grid_spec=pltpu.PrefetchScalarGridSpec(
            num_scalar_prefetch=4,
            grid=(half_rows, columns.steps // per_step),
            in_specs=[
                pl.BlockSpec(
                    (tile_order, width),
                    lambda g, b, me, slots, row_partner, _: (row_of(g, me, row_partner), 0),
                )
            ]
            + [tile_spec(index) for index in range(per_step)],
            out_specs=pl.BlockSpec(
                (per_step, 2, width, tile_order), lambda g, b, *_: (b, 0, g, 0)
            ),
            scratch_shapes=[pltpu.VMEM((2 * width, tile_order), BF16)],
        ),
        out_shape=jax.ShapeDtypeStruct((columns.steps, 2, half_rows * width, tile_order), BF16),
        compiler_params=PARAMS,
        cost_estimate=cost(12 * half_rows * columns.steps * width * tile_order * tile_order),
        name="left_products",
    )(*tables, q_rows, *[tiles] * per_step)


def packed_first(blocks):
    return max(1, blocks // 2)


def packed_place(slots, first_row, first_col, half_rows, half_cols, block_cols, block):
    before = here = count = jnp.int32(0)
    for index in range(half_rows * half_cols):
        place = (first_row + index % half_rows) * block_cols + first_col + index // half_rows
        flag = (slots[place] >= 0).astype(jnp.int32)
        before = before + jnp.where(index < block, flag, 0)
        here = here + jnp.where(index == block, flag, 0)
        count = count + flag
    return jnp.where(here == 1, before, count + block - before), here == 1


def quarter_live(table, first_row, first_col, half_rows, half_cols, block_cols):
    count = jnp.int32(0)
    for index in range(half_rows * half_cols):
        place = (first_row + index % half_rows) * block_cols + first_col + index // half_rows
        count = count + (table[place] >= 0).astype(jnp.int32)
    return count


def right_kernel(columns, block_cols, half_rows, starts, *refs):
    me, slots, mate_slots, row_partner, col_partner, w_ref = refs[:6]
    pieces = refs[6 : 6 + len(starts)]
    step = pl.program_id(0)
    tile_order = w_ref.shape[3]
    width = pieces[0].shape[1]
    packs = columns.kind == Columns.REST
    outs = refs[6 + len(starts) : -3 if packs else -2]
    p_high, p_low = refs[-2:]

    @pl.when(step == 0)
    def _():
        half = columns.half(step, me, row_partner, col_partner)
        for (start, filled), piece in zip(starts, pieces):
            wanted = start(me) >= 0
            if columns.given:
                wanted = div(start(me), columns.half_cols * tile_order) == half
            if filled is not None:
                wanted &= filled(me)

            @pl.when(wanted)
            def _():
                depth = piece.shape[0]
                rows = pl.ds(pl.multiple_of(start(me), depth), depth)
                p_high[rows, :], p_low[rows, :] = split(piece[...])

    column = columns.column(step, me, row_partner, col_partner)
    rows = pl.ds(pl.multiple_of(column * tile_order, tile_order), tile_order)
    both = w_ref[step if columns.given else 0].reshape(2 * w_ref.shape[2], tile_order)
    block = product(both, p_high[rows, :], p_low[rows, :])
    half_cols = columns.half_cols
    if not packs:
        for index, out in enumerate(outs):

            @pl.when(jnp.minimum(step, half_cols) == index)
            def _():
                out[...] = block

        return
    branch, *outs = outs
    packed = refs[-3]
    first_row = half_of(True, me, row_partner) * half_rows
    first_col = columns.half(step, me, row_partner, col_partner) * half_cols
    for row in range(half_rows):
        place, _ = packed_place(
            slots, first_row, first_col, half_rows, half_cols, block_cols, step * half_rows + row
        )
        packed[place] = block[row * width : (row + 1) * width]

    @pl.when(step == half_cols - 1)
    def _():
        count = outs[0].shape[0]
        outs[0][...] = packed[:count]
        for index, out in enumerate(outs[1:]):
            out[...] = packed[count + index]
        keeps = (me[1] > col_partner[me[0], me[1]]).astype(jnp.int32)
        mate_row = half_of(False, me, row_partner) * half_rows
        quarter = half_rows, half_cols, block_cols
        most = jnp.maximum(
            quarter_live(slots, first_row, first_col, *quarter),
            quarter_live(mate_slots, mate_row, keeps * half_cols, *quarter),
        )
        choice = jnp.clip(most - count, 0, len(outs) - 1)
        branch[0] = ((me[0] ^ row_partner[me[0], me[1]]) - 1) * len(outs) + choice


def right_products(kind, tables, w, shards, half_rows, block_cols):
    _, _, height, tile_order = w.shape
    columns = Columns(kind, block_cols)
    half_cols = columns.half_cols
    width = shards[0][0].shape[1]
    blocks = half_rows * half_cols

    whole = pl.BlockSpec(memory_space=pltpu.VMEM)
    one_column = pl.BlockSpec((1, 2, height, tile_order), lambda i, *_: (i, 0, 0, 0))
    scratch = [pltpu.VMEM((block_cols * tile_order, width), BF16)] * 2
    if kind == Columns.REST:
        most = packed_first(blocks)
        shapes = [(most, width, width)] + [(width, width)] * (blocks - most)
        out_specs = [pl.BlockSpec(memory_space=pltpu.SMEM)]
        out_specs += [pl.BlockSpec(shape, lambda i, *_, n=len(shape): (0,) * n) for shape in shapes]
        scratch = [pltpu.VMEM((blocks, width, width), F32)] + scratch
    else:
        shapes = [(height, width)] * half_cols
        out_specs = [pl.BlockSpec((height, width), lambda i, *_: (0, 0))] * half_cols
        if kind == Columns.KEPT:
            shapes += [(height, half_cols * width)]
            out_specs += [
                pl.BlockSpec((height, width), lambda i, *_: (0, jnp.maximum(i - half_cols, 0)))
            ]
    out_shape = [jax.ShapeDtypeStruct(shape, F32) for shape in shapes]
    if kind == Columns.REST:
        out_shape = [jax.ShapeDtypeStruct((1,), jnp.int32)] + out_shape
    return pl.pallas_call(
        functools.partial(
            right_kernel, columns, block_cols, half_rows, [shard[1:] for shard in shards]
        ),
        grid_spec=pltpu.PrefetchScalarGridSpec(
            num_scalar_prefetch=5,
            grid=(columns.steps,),
            in_specs=[whole if columns.given else one_column] + [whole] * len(shards),
            out_specs=out_specs,
            scratch_shapes=scratch,
        ),
        out_shape=out_shape,
        compiler_params=PARAMS,
        cost_estimate=cost(6 * columns.steps * height * width * tile_order),
        name="right_products",
    )(*tables, w, *[shard[0] for shard in shards])


def comes_from(which, me, col_partner):
    distance = me[1] ^ col_partner[me[0], me[1]]
    core = rem(distance, 2) == 1
    return core if which == 0 else jnp.logical_not(core) & (div(distance, 2) == which - 1)


def sum_kernel(half_rows, block_cols, singles, sections, *refs):
    me, _, mate_slots, row_partner, col_partner, kept_ref, packed_ref = refs[:7]
    single_refs, section_refs, out = refs[7 : 7 + singles], refs[7 + singles : -1], refs[-1]
    half_cols = block_cols // 2
    step = pl.program_id(0)
    keeps = (me[1] > col_partner[me[0], me[1]]).astype(jnp.int32)
    first_row = half_of(False, me, row_partner) * half_rows
    place, live = packed_place(
        mate_slots, first_row, keeps * half_cols, half_rows, half_cols, block_cols, step
    )
    count = packed_ref.shape[0]
    at = 0
    for index, kind in enumerate(sections):
        for which in range(kind):
            section = section_refs[at + which]
            wanted = div(step, half_rows) == index
            if kind > 1:
                wanted &= comes_from(which, me, col_partner)

            @pl.when(wanted)
            def _():
                out[...] = kept_ref[...] + section[...].reshape(out.shape)

        at += kind

    @pl.when(live & (place < count))
    def _():
        out[...] += packed_ref[jnp.minimum(place, count - 1)]

    for index, single in enumerate(single_refs):

        @pl.when(live & (place == count + index))
        def _():
            out[...] += single[...]


def sum_blocks(tables, half_rows, block_cols, kept, packed, singles, sections):
    half_cols = block_cols // 2
    height, both = kept.shape
    width = both // half_cols
    block = pl.BlockSpec((width, width), lambda i, *_: (rem(i, half_rows), div(i, half_rows)))

    def section_spec(index, section, which=None):
        def section_at(i, me, slots, mate_slots, row_partner, col_partner):
            here = jnp.clip(i - index * half_rows, 0, half_rows - 1)
            if which is not None:
                here = jnp.where(comes_from(which, me, col_partner), here, 0)
            return (col_partner[me[0], me[1]], here, 0) if section.ndim == 3 else (here, 0)

        return pl.BlockSpec((1,) * (section.ndim - 2) + (width, width), section_at)

    return pl.pallas_call(
        functools.partial(
            sum_kernel, half_rows, block_cols, len(singles), [len(each) for each in sections]
        ),
        grid_spec=pltpu.PrefetchScalarGridSpec(
            num_scalar_prefetch=5,
            grid=(half_rows * half_cols,),
            in_specs=[block]
            + [pl.BlockSpec(memory_space=pltpu.VMEM)] * (1 + len(singles))
            + [
                section_spec(index, each, which if len(group) > 1 else None)
                for index, group in enumerate(sections)
                for which, each in enumerate(group)
            ],
            out_specs=block,
        ),
        out_shape=jax.ShapeDtypeStruct((height, both), F32),
        compiler_params=PARAMS,
        name="sum_blocks",
    )(*tables, kept, packed, *singles, *[each for group in sections for each in group])


def hand_over_kernel(wish, kept_ref, received_ref, *refs):
    out, wanted = refs[-2:]
    out[...] = kept_ref[...] + received_ref[...]
    for chip, section in enumerate(refs[:-2]):

        @pl.when(wish[0] == chip)
        def _():
            wanted[...] = section[...]


def hand_over(wish, kept, received, over):
    height, width = kept.shape
    steps = 2 if height % 16 == 0 else 1
    block = pl.BlockSpec((height // steps, width), lambda i, _: (i, 0))

    def chip_spec(chip):
        return pl.BlockSpec(
            (height // steps, width), lambda i, wish: (jnp.where(wish[0] == chip, i, 0), 0)
        )

    return pl.pallas_call(
        hand_over_kernel,
        grid_spec=pltpu.PrefetchScalarGridSpec(
            num_scalar_prefetch=1,
            grid=(steps,),
            in_specs=[block, block] + [chip_spec(chip) for chip in range(len(over))],
            out_specs=[block, block],
        ),
        out_shape=[jax.ShapeDtypeStruct(kept.shape, F32)] * 2,
        compiler_params=PARAMS,
        cost_estimate=cost(0),
        name="hand_over",
    )(wish, kept, received, *over)


def flip(value, axis, size, mask):
    return lax.ppermute(value, axis, [(i, i ^ mask) for i in range(size)])


def gather_prolong(shard, axis, size):
    depth = shard.shape[0]
    if size != 4:
        gathered = lax.all_gather(shard, axis)
        return [(gathered[i], lambda me, i=i: jnp.int32(i * depth), None) for i in range(size)]
    part = depth // 2
    parts = [shard[:part], shard[part:]]
    by_two = [flip(each, axis, size, 2) for each in parts]
    by_one = flip(shard, axis, size, 1)
    middle = lax.ppermute(shard, axis, [(1, 2), (2, 1)])
    handed = [lax.ppermute(each, axis, [(1, 0), (2, 3)]) for each in by_two]

    def at(mask, first=0):
        return lambda me: (me[0] ^ mask) * depth + first

    def inner(me):
        return (me[0] == 1) | (me[0] == 2)

    pieces = [(shard, at(0), None), (by_one, at(1), None), (middle, at(3), inner)]
    for index in range(2):
        pieces.append((by_two[index], at(2, index * part), None))
        pieces.append((handed[index], at(3, index * part), lambda me: jnp.logical_not(inner(me))))
    return pieces


def pair_switch(index, size, branch, operand, choices=1):
    branches = [
        functools.partial(branch, mask, choice) for mask in range(1, size) for choice in range(choices)
    ]
    return lax.switch(index[0], branches, operand)


def solution(mesh):
    n_row = mesh.shape["row"]
    n_col = mesh.shape["col"]

    def body(tiles, coords, counts, restrict, prolong, row_partner, col_partner):
        tile_order = tiles.shape[1]
        block_rows = restrict.shape[0] * n_col // tile_order
        block_cols = prolong.shape[0] * n_row // tile_order
        half_rows, half_cols = block_rows // 2, block_cols // 2
        row = lax.axis_index("row").astype(jnp.int32)
        col = lax.axis_index("col").astype(jnp.int32)
        me = jnp.stack([row, col])

        row_partner, coords = row_partner.T, coords.T
        places = block_rows * block_cols
        slots, first, wish = make_tables(
            me, row_partner, col_partner, coords, counts, places, block_cols
        )
        shards = gather_prolong(prolong, "row", n_row)
        q_rows = lax.all_gather(restrict, "col", axis=0, tiled=True)

        def products(kind, mate_slots):
            tables = (me, slots, row_partner, col_partner)
            w = left_products(kind, tables, tiles, q_rows, half_rows, block_cols)
            tables = (me, slots, mate_slots, row_partner, col_partner)
            return right_products(kind, tables, w, shards, half_rows, block_cols)

        def swap_first(mask, _, chunk):
            received = flip(chunk, "row", n_row, mask)
            return received, flip(slots, "row", n_row, mask), products(Columns.KEPT, slots)

        def swap_next(mask, _, operands):
            chunk, mate_slots = operands
            return flip(chunk, "row", n_row, mask), products(Columns.REST, mate_slots)

        def swap_more(mask, _, operands):
            return flip(operands[0], "row", n_row, mask), operands[1:]

        def swap_rest(mask, extra, rest):
            return [
                flip(array, "row", n_row, mask) if index <= extra else array
                for index, array in enumerate(rest)
            ]

        given = products(Columns.ON, slots)
        received, mate_slots, kept = pair_switch(first, n_row, swap_first, given[0])
        sections, rest, over = [], None, None
        for index in range(half_cols):
            if index == 1 and over is not None:
                over, received = lax.optimization_barrier((over, received))
                section, wanted = hand_over(wish, kept[index], received, over)
                sections.append([flip(wanted, "col", n_col, 1)] + over)
            else:
                section = kept[index] + received
            if index == 0 and n_col == 8 and half_cols > 1:
                over = [section] + [flip(section, "col", n_col, 2 * chip) for chip in range(1, 4)]
            else:
                sections.append([lax.all_gather(section, "col")])
            if index + 1 == half_cols:
                break
            chunk, section = lax.optimization_barrier((given[index + 1], section))
            if index == 0:
                received, rest = pair_switch(first, n_row, swap_next, (chunk, mate_slots))
            else:
                received, *_ = pair_switch(first, n_row, swap_more, (chunk,))
        if rest is None:
            rest = products(Columns.REST, mate_slots)
        second, *rest = rest
        rest, section = lax.optimization_barrier((rest, section))
        packed, *singles = pair_switch(second, n_row, swap_rest, rest, len(rest))
        tables = (me, slots, mate_slots, row_partner, col_partner)
        return sum_blocks(tables, half_rows, block_cols, kept[-1], packed, singles, sections)

    in_specs = (
        P(("row", "col"), None, None),
        P(("row", "col"), None),
        P(("row", "col")),
        P(("row", "col"), None),
        P(("col", "row"), None),
        P(),
        P(),
    )
    return jax.shard_map(
        body, mesh=mesh, in_specs=in_specs, out_specs=P("row", "col"), check_vma=False
    )
```

```python
import functools

import jax
import jax.numpy as jnp
from jax import lax
from jax.experimental import pallas as pl
from jax.experimental.pallas import tpu as pltpu
from jax.sharding import PartitionSpec as P

F32 = jnp.float32
BF16 = jnp.bfloat16
VMEM_BYTES = 48 * 1024 * 1024
PARAMS = pltpu.CompilerParams(vmem_limit_bytes=VMEM_BYTES)


def cost(flops):
    return pl.CostEstimate(flops=flops, bytes_accessed=0, transcendentals=0)


def split(value):
    high = value.astype(BF16)
    low = (value - high.astype(F32)).astype(BF16)
    return high, low


def dot(left, right):
    return jnp.dot(left, right, preferred_element_type=F32)


def product(left_both, right_high, right_low):
    half = left_both.shape[0] // 2
    total = dot(left_both[half:], right_high)
    total = total + dot(left_both[:half], right_low)
    return total + dot(left_both[:half], right_high)


def div(value, by):
    return lax.div(value, jnp.int32(by))


def rem(value, by):
    return lax.rem(value, jnp.int32(by))


def half_of(given, me, row_partner):
    mate = row_partner[me[0], me[1]]
    return ((mate > me[0]) if given else (me[0] > mate)).astype(jnp.int32)


def tables_kernel(block_cols, me, row_partner, col_partner, coords, counts, slots, first, wish):
    for place in range(slots.shape[0]):
        slots[place] = jnp.int32(-1)
    for slot in range(coords.shape[1]):

        @pl.when(slot < counts[0])
        def _():
            slots[coords[0, slot] * block_cols + coords[1, slot]] = jnp.int32(slot)

    first[0] = (me[0] ^ row_partner[me[0], me[1]]) - 1
    other = me[1] ^ 1
    wish[0] = div(other ^ col_partner[me[0], other], 2)


def make_tables(me, row_partner, col_partner, coords, counts, places, block_cols):
    smem = pl.BlockSpec(memory_space=pltpu.SMEM)
    return pl.pallas_call(
        functools.partial(tables_kernel, block_cols),
        in_specs=[smem] * 5,
        out_specs=[smem] * 3,
        out_shape=[jax.ShapeDtypeStruct((n,), jnp.int32) for n in (places, 1, 1)],
        cost_estimate=cost(0),
        name="make_tables",
    )(me, row_partner, col_partner, coords, counts)


class Columns:
    ON, REST, KEPT = range(3)

    def __init__(self, kind, block_cols):
        self.kind = kind
        self.given = kind != self.KEPT
        self.half_cols = block_cols // 2
        self.steps = block_cols if kind == self.KEPT else self.half_cols

    def half(self, step, me, row_partner, col_partner):
        if self.kind == self.KEPT:
            goes_on = (me[1] < col_partner[me[0], me[1]]).astype(jnp.int32)
            return goes_on ^ div(step, self.half_cols)
        goes_on = (me[1] < col_partner[row_partner[me[0], me[1]], me[1]]).astype(jnp.int32)
        return goes_on ^ (1 if self.kind == self.REST else 0)

    def column(self, step, me, row_partner, col_partner):
        half = self.half(step, me, row_partner, col_partner)
        return half * self.half_cols + rem(step, self.half_cols)


def left_kernel(columns, block_cols, half_rows, per_step, *refs):
    me, slots, row_partner, col_partner = refs[:4]
    tile_refs, q_refs, out, q_both = refs[4 : 4 + per_step], refs[4 + per_step : -2], refs[-2], refs[-1]
    group, step = pl.program_id(0), pl.program_id(1)
    width = q_both.shape[0] // 2

    block_row = half_of(columns.given, me, row_partner) * half_rows + group

    def put(value, first):
        high, low = split(value.T)
        q_both[:width, first : first + value.shape[0]] = high
        q_both[width:, first : first + value.shape[0]] = low

    if len(q_refs) == 1:

        @pl.when(step == 0)
        def _():
            put(q_refs[0][...], 0)

    else:
        distance = block_row ^ div(me[1], 2)
        for core in range(2):

            @pl.when((step == 0) & (rem(me[1], 2) == core))
            def _():
                depth = q_refs[0].shape[1]
                put(q_refs[0][distance], core * depth)
                put(q_refs[1][distance], (1 - core) * depth)

    for index, tile_ref in enumerate(tile_refs):
        column = columns.column(step * per_step + index, me, row_partner, col_partner)
        live = slots[block_row * block_cols + column] >= 0
        high, low = split(tile_ref[0])
        total = jnp.where(live, product(q_both[...], high, low), 0.0)
        out[index, 0], out[index, 1] = split(total)


def left_products(kind, tables, tiles, q_pieces, half_rows, block_cols):
    _, tile_order, _ = tiles.shape
    width = q_pieces[0].shape[-1]
    columns = Columns(kind, block_cols)
    per_step = 2 if columns.steps % 2 == 0 else 1

    def row_of(g, me, row_partner):
        return half_of(columns.given, me, row_partner) * half_rows + g

    def tile_spec(index):
        def tile_at(g, b, me, slots, row_partner, col_partner):
            column = columns.column(b * per_step + index, me, row_partner, col_partner)
            return jnp.maximum(slots[row_of(g, me, row_partner) * block_cols + column], 0), 0, 0

        return pl.BlockSpec((1, tile_order, tile_order), tile_at)

    if len(q_pieces) == 1:
        q_specs = [
            pl.BlockSpec(
                (tile_order, width),
                lambda g, b, me, slots, row_partner, _: (row_of(g, me, row_partner), 0),
            )
        ]
    else:
        q_specs = [pl.BlockSpec(memory_space=pltpu.VMEM)] * len(q_pieces)
    return pl.pallas_call(
        functools.partial(left_kernel, columns, block_cols, half_rows, per_step),
        grid_spec=pltpu.PrefetchScalarGridSpec(
            num_scalar_prefetch=4,
            grid=(half_rows, columns.steps // per_step),
            in_specs=[tile_spec(index) for index in range(per_step)] + q_specs,
            out_specs=pl.BlockSpec(
                (per_step, 2, width, tile_order), lambda g, b, *_: (b, 0, g, 0)
            ),
            scratch_shapes=[pltpu.VMEM((2 * width, tile_order), BF16)],
        ),
        out_shape=jax.ShapeDtypeStruct((columns.steps, 2, half_rows * width, tile_order), BF16),
        compiler_params=PARAMS,
        cost_estimate=cost(12 * half_rows * columns.steps * width * tile_order * tile_order),
        name="left_products",
    )(*tables, *[tiles] * per_step, *q_pieces)


def packed_first(blocks):
    return max(1, blocks * 3 // 4)


def packed_place(slots, first_row, first_col, half_rows, half_cols, block_cols, block):
    before = here = count = jnp.int32(0)
    for index in range(half_rows * half_cols):
        place = (first_row + index % half_rows) * block_cols + first_col + index // half_rows
        flag = (slots[place] >= 0).astype(jnp.int32)
        before = before + jnp.where(index < block, flag, 0)
        here = here + jnp.where(index == block, flag, 0)
        count = count + flag
    return jnp.where(here == 1, before, count + block - before), here == 1


def quarter_live(table, first_row, first_col, half_rows, half_cols, block_cols):
    count = jnp.int32(0)
    for index in range(half_rows * half_cols):
        place = (first_row + index % half_rows) * block_cols + first_col + index // half_rows
        count = count + (table[place] >= 0).astype(jnp.int32)
    return count


def right_kernel(columns, block_cols, half_rows, starts, *refs):
    me, slots, mate_slots, row_partner, col_partner, w_ref = refs[:6]
    pieces = refs[6 : 6 + len(starts)]
    step = pl.program_id(0)
    tile_order = w_ref.shape[3]
    width = pieces[0].shape[1]
    packs = columns.kind == Columns.REST
    outs = refs[6 + len(starts) : -3 if packs else -2]
    p_high, p_low = refs[-2:]

    @pl.when(step == 0)
    def _():
        half = columns.half(step, me, row_partner, col_partner)
        for (start, filled), piece in zip(starts, pieces):
            wanted = start(me) >= 0
            if columns.given:
                wanted = div(start(me), columns.half_cols * tile_order) == half
            if filled is not None:
                wanted &= filled(me)

            @pl.when(wanted)
            def _():
                depth = piece.shape[0]
                rows = pl.ds(pl.multiple_of(start(me), depth), depth)
                p_high[rows, :], p_low[rows, :] = split(piece[...])

    column = columns.column(step, me, row_partner, col_partner)
    rows = pl.ds(pl.multiple_of(column * tile_order, tile_order), tile_order)
    both = w_ref[step if columns.given else 0].reshape(2 * w_ref.shape[2], tile_order)
    block = product(both, p_high[rows, :], p_low[rows, :])
    half_cols = columns.half_cols
    if not packs:
        for index, out in enumerate(outs):

            @pl.when(jnp.minimum(step, half_cols) == index)
            def _():
                out[...] = block

        return
    branch, *outs = outs
    packed = refs[-3]
    first_row = half_of(True, me, row_partner) * half_rows
    first_col = columns.half(step, me, row_partner, col_partner) * half_cols
    for row in range(half_rows):
        place, _ = packed_place(
            slots, first_row, first_col, half_rows, half_cols, block_cols, step * half_rows + row
        )
        packed[place] = block[row * width : (row + 1) * width]

    @pl.when(step == half_cols - 1)
    def _():
        count = outs[0].shape[0]
        outs[0][...] = packed[:count]
        for index, out in enumerate(outs[1:]):
            out[...] = packed[count + index]
        keeps = (me[1] > col_partner[me[0], me[1]]).astype(jnp.int32)
        mate_row = half_of(False, me, row_partner) * half_rows
        quarter = half_rows, half_cols, block_cols
        most = jnp.maximum(
            quarter_live(slots, first_row, first_col, *quarter),
            quarter_live(mate_slots, mate_row, keeps * half_cols, *quarter),
        )
        choice = jnp.clip(most - count, 0, len(outs) - 1)
        branch[0] = ((me[0] ^ row_partner[me[0], me[1]]) - 1) * len(outs) + choice


def right_products(kind, tables, w, shards, half_rows, block_cols):
    _, _, height, tile_order = w.shape
    columns = Columns(kind, block_cols)
    half_cols = columns.half_cols
    width = shards[0][0].shape[1]
    blocks = half_rows * half_cols

    whole = pl.BlockSpec(memory_space=pltpu.VMEM)
    one_column = pl.BlockSpec((1, 2, height, tile_order), lambda i, *_: (i, 0, 0, 0))
    scratch = [pltpu.VMEM((block_cols * tile_order, width), BF16)] * 2
    if kind == Columns.REST:
        most = packed_first(blocks)
        shapes = [(most, width, width)] + [(width, width)] * (blocks - most)
        out_specs = [pl.BlockSpec(memory_space=pltpu.SMEM)]
        out_specs += [pl.BlockSpec(shape, lambda i, *_, n=len(shape): (0,) * n) for shape in shapes]
        scratch = [pltpu.VMEM((blocks, width, width), F32)] + scratch
    else:
        shapes = [(height, width)] * half_cols
        out_specs = [pl.BlockSpec((height, width), lambda i, *_: (0, 0))] * half_cols
        if kind == Columns.KEPT:
            shapes += [(height, half_cols * width)]
            out_specs += [
                pl.BlockSpec((height, width), lambda i, *_: (0, jnp.maximum(i - half_cols, 0)))
            ]
    out_shape = [jax.ShapeDtypeStruct(shape, F32) for shape in shapes]
    if kind == Columns.REST:
        out_shape = [jax.ShapeDtypeStruct((1,), jnp.int32)] + out_shape
    return pl.pallas_call(
        functools.partial(
            right_kernel, columns, block_cols, half_rows, [shard[1:] for shard in shards]
        ),
        grid_spec=pltpu.PrefetchScalarGridSpec(
            num_scalar_prefetch=5,
            grid=(columns.steps,),
            in_specs=[whole if columns.given else one_column] + [whole] * len(shards),
            out_specs=out_specs,
            scratch_shapes=scratch,
        ),
        out_shape=out_shape,
        compiler_params=PARAMS,
        cost_estimate=cost(6 * columns.steps * height * width * tile_order),
        name="right_products",
    )(*tables, w, *[shard[0] for shard in shards])


def comes_from(which, me, col_partner):
    distance = me[1] ^ col_partner[me[0], me[1]]
    core = rem(distance, 2) == 1
    return core if which == 0 else jnp.logical_not(core) & (div(distance, 2) == which - 1)


def sum_kernel(half_rows, block_cols, singles, sections, *refs):
    me, _, mate_slots, row_partner, col_partner, kept_ref, packed_ref = refs[:7]
    single_refs, section_refs, out = refs[7 : 7 + singles], refs[7 + singles : -1], refs[-1]
    half_cols = block_cols // 2
    step = pl.program_id(0)
    keeps = (me[1] > col_partner[me[0], me[1]]).astype(jnp.int32)
    first_row = half_of(False, me, row_partner) * half_rows
    place, live = packed_place(
        mate_slots, first_row, keeps * half_cols, half_rows, half_cols, block_cols, step
    )
    count = packed_ref.shape[0]
    at = 0
    for index, kind in enumerate(sections):
        for which in range(kind):
            section = section_refs[at + which]
            wanted = div(step, half_rows) == index
            if kind > 1:
                wanted &= comes_from(which, me, col_partner)

            @pl.when(wanted)
            def _():
                out[...] = kept_ref[...] + section[...].reshape(out.shape)

        at += kind

    @pl.when(live & (place < count))
    def _():
        out[...] += packed_ref[jnp.minimum(place, count - 1)]

    for index, single in enumerate(single_refs):

        @pl.when(live & (place == count + index))
        def _():
            out[...] += single[...]


def sum_blocks(tables, half_rows, block_cols, kept, packed, singles, sections):
    half_cols = block_cols // 2
    height, both = kept.shape
    width = both // half_cols
    block = pl.BlockSpec((width, width), lambda i, *_: (rem(i, half_rows), div(i, half_rows)))

    def section_spec(index, section, which=None):
        def section_at(i, me, slots, mate_slots, row_partner, col_partner):
            here = jnp.clip(i - index * half_rows, 0, half_rows - 1)
            if which is not None:
                here = jnp.where(comes_from(which, me, col_partner), here, 0)
            if section.ndim == 2:
                return here, 0
            return index if which == 0 else col_partner[me[0], me[1]], here, 0

        return pl.BlockSpec((1,) * (section.ndim - 2) + (width, width), section_at)

    return pl.pallas_call(
        functools.partial(
            sum_kernel, half_rows, block_cols, len(singles), [len(each) for each in sections]
        ),
        grid_spec=pltpu.PrefetchScalarGridSpec(
            num_scalar_prefetch=5,
            grid=(half_rows * half_cols,),
            in_specs=[block]
            + [pl.BlockSpec(memory_space=pltpu.VMEM)] * (1 + len(singles))
            + [
                section_spec(index, each, which if len(group) > 1 else None)
                for index, group in enumerate(sections)
                for which, each in enumerate(group)
            ],
            out_specs=block,
        ),
        out_shape=jax.ShapeDtypeStruct((height, both), F32),
        compiler_params=PARAMS,
        name="sum_blocks",
    )(*tables, kept, packed, *singles, *[each for group in sections for each in group])


def wished_kernel(wish, *refs):
    *sections, wanted = refs
    for index, section in enumerate(sections):

        @pl.when((pl.program_id(0) == index // 4) & (wish[0] == index % 4))
        def _():
            wanted[0] = section[...]


def wished(wish, overs):
    height, width = overs[0][0].shape
    steps = 2 if height % 16 == 0 else 1

    def chip_spec(column, chip):
        def chip_at(b, i, wish):
            here = jnp.where(b == column, i, jnp.where(b < column, 0, steps - 1))
            return jnp.where(wish[0] == chip, here, 0), 0

        return pl.BlockSpec((height // steps, width), chip_at)

    return pl.pallas_call(
        wished_kernel,
        grid_spec=pltpu.PrefetchScalarGridSpec(
            num_scalar_prefetch=1,
            grid=(len(overs), steps),
            in_specs=[chip_spec(b, chip) for b in range(len(overs)) for chip in range(4)],
            out_specs=pl.BlockSpec((1, height // steps, width), lambda b, i, _: (b, i, 0)),
        ),
        out_shape=jax.ShapeDtypeStruct((len(overs), height, width), F32),
        compiler_params=PARAMS,
        cost_estimate=cost(0),
        name="wished",
    )(wish, *[section for over in overs for section in over])


def flip(value, axis, size, mask):
    return lax.ppermute(value, axis, [(i, i ^ mask) for i in range(size)])


def hand_out(part, axis):
    return lax.ppermute(part, axis, [(1, 0), (2, 3)])


def first_prolong(shard, axis, size):
    if size != 4:
        return None
    part = shard.shape[0] // 2
    by_two = [flip(each, axis, size, 2) for each in (shard[:part], shard[part:])]
    near = [*by_two, flip(shard, axis, size, 1), lax.ppermute(shard, axis, [(1, 2), (2, 1)])]
    return near + [hand_out(by_two[0], axis)]


def gather_prolong(shard, near, axis, size):
    depth = shard.shape[0]
    if near is None:
        gathered = lax.all_gather(shard, axis)
        return [(gathered[i], lambda me, i=i: jnp.int32(i * depth), None) for i in range(size)]
    *by_two, by_one, middle, handed = near
    handed = [handed, hand_out(by_two[1], axis)]

    def at(mask, first=0):
        return lambda me: (me[0] ^ mask) * depth + first

    def inner(me):
        return (me[0] == 1) | (me[0] == 2)

    pieces = [(shard, at(0), None), (by_one, at(1), None), (middle, at(3), inner)]
    for index in range(2):
        first = index * (depth // 2)
        pieces.append((by_two[index], at(2, first), None))
        pieces.append((handed[index], at(3, first), lambda me: jnp.logical_not(inner(me))))
    return pieces


def gather_restrict(shard, near, slots, axis, size):
    over_x = flip(shard, axis, size, 2)
    over_y = flip(shard, axis, size, 4)
    if near is not None:
        over_x, near[0], near[2], slots = lax.optimization_barrier((over_x, near[0], near[2], slots))
    pieces = [shard, over_x, over_y, flip(over_x, axis, size, 4)]
    if near is not None:
        pieces, near[1], near[3:] = lax.optimization_barrier((pieces, near[1], near[3:]))
    mine = jnp.stack(pieces)
    return [mine, flip(mine, axis, size, 1)], slots


def pair_switch(index, size, branch, operand, choices=1):
    branches = [
        functools.partial(branch, mask, choice) for mask in range(1, size) for choice in range(choices)
    ]
    return lax.switch(index[0], branches, operand)


def solution(mesh):
    n_row = mesh.shape["row"]
    n_col = mesh.shape["col"]

    def body(tiles, coords, counts, restrict, prolong, row_partner, col_partner):
        tile_order = tiles.shape[1]
        block_rows = restrict.shape[0] * n_col // tile_order
        block_cols = prolong.shape[0] * n_row // tile_order
        half_rows, half_cols = block_rows // 2, block_cols // 2
        row = lax.axis_index("row").astype(jnp.int32)
        col = lax.axis_index("col").astype(jnp.int32)
        me = jnp.stack([row, col])

        row_partner, coords = row_partner.T, coords.T
        places = block_rows * block_cols
        slots, first, wish = make_tables(
            me, row_partner, col_partner, coords, counts, places, block_cols
        )
        near = first_prolong(prolong, "row", n_row)
        by_chip = n_col == 8 and block_rows == 4 and tile_order == 2 * restrict.shape[0]
        if by_chip:
            q_pieces, slots = gather_restrict(restrict, near, slots, "col", n_col)
        else:
            q_pieces = [lax.all_gather(restrict, "col", axis=0, tiled=True)]

        shards = gather_prolong(prolong, near, "row", n_row)

        def products(kind, mate_slots):
            tables = (me, slots, row_partner, col_partner)
            w = left_products(kind, tables, tiles, q_pieces, half_rows, block_cols)
            tables = (me, slots, mate_slots, row_partner, col_partner)
            return right_products(kind, tables, w, shards, half_rows, block_cols)

        def swap_first(mask, _, chunk):
            received = flip(chunk, "row", n_row, mask)
            return received, flip(slots, "row", n_row, mask), products(Columns.KEPT, slots)

        def swap_next(mask, _, operands):
            chunk, mate_slots = operands
            return flip(chunk, "row", n_row, mask), products(Columns.REST, mate_slots)

        def swap_more(mask, _, operands):
            return flip(operands[0], "row", n_row, mask), operands[1:]

        def swap_rest(mask, extra, rest):
            return [
                flip(array, "row", n_row, mask) if index <= extra else array
                for index, array in enumerate(rest)
            ]

        given = products(Columns.ON, slots)
        received, mate_slots, kept = pair_switch(first, n_row, swap_first, given[0])
        sections, rest = [], None
        for index in range(half_cols):
            section = kept[index] + received
            if n_col == 8:
                over = [section] + [flip(section, "col", n_col, 2 * chip) for chip in range(1, 4)]
            else:
                over = [lax.all_gather(section, "col")]
            sections.append(over)
            if index + 1 == half_cols:
                break
            chunk, section = lax.optimization_barrier((given[index + 1], section))
            if index == 0:
                received, rest = pair_switch(first, n_row, swap_next, (chunk, mate_slots))
            else:
                received, *_ = pair_switch(first, n_row, swap_more, (chunk,))
            sections[index], received = lax.optimization_barrier((sections[index], received))
        if rest is None:
            rest = products(Columns.REST, mate_slots)
        second, *rest = rest
        rest, section = lax.optimization_barrier((rest, section))
        rest = pair_switch(second, n_row, swap_rest, rest, len(rest))
        if n_col == 8:
            sections[-1], rest = lax.optimization_barrier((sections[-1], rest))
            handed = flip(wished(wish, sections), "col", n_col, 1)
            sections = [[handed] + over for over in sections]
        packed, *singles = rest
        tables = (me, slots, mate_slots, row_partner, col_partner)
        return sum_blocks(tables, half_rows, block_cols, kept[-1], packed, singles, sections)

    in_specs = (
        P(("row", "col"), None, None),
        P(("row", "col"), None),
        P(("row", "col")),
        P(("row", "col"), None),
        P(("col", "row"), None),
        P(),
        P(),
    )
    return jax.shard_map(
        body, mesh=mesh, in_specs=in_specs, out_specs=P("row", "col"), check_vma=False
    )
```

```python
import functools

import jax
import jax.numpy as jnp
from jax import lax
from jax.experimental import pallas as pl
from jax.experimental.pallas import tpu as pltpu
from jax.sharding import PartitionSpec as P

F32 = jnp.float32
BF16 = jnp.bfloat16
VMEM_BYTES = 48 * 1024 * 1024
PARAMS = pltpu.CompilerParams(vmem_limit_bytes=VMEM_BYTES)


def cost(flops):
    return pl.CostEstimate(flops=flops, bytes_accessed=0, transcendentals=0)


def split(value):
    high = value.astype(BF16)
    low = (value - high.astype(F32)).astype(BF16)
    return high, low


def dot(left, right):
    return jnp.dot(left, right, preferred_element_type=F32)


def product(left_both, right_high, right_low):
    half = left_both.shape[0] // 2
    total = dot(left_both[half:], right_high)
    total = total + dot(left_both[:half], right_low)
    return total + dot(left_both[:half], right_high)


def div(value, by):
    return lax.div(value, jnp.int32(by))


def rem(value, by):
    return lax.rem(value, jnp.int32(by))


def half_of(given, me, row_partner):
    mate = row_partner[me[0], me[1]]
    return ((mate > me[0]) if given else (me[0] > mate)).astype(jnp.int32)


def tables_kernel(block_cols, me, row_partner, col_partner, coords, counts, slots, first, wish):
    for place in range(slots.shape[0]):
        slots[place] = jnp.int32(-1)
    for slot in range(coords.shape[1]):

        @pl.when(slot < counts[0])
        def _():
            slots[coords[0, slot] * block_cols + coords[1, slot]] = jnp.int32(slot)

    first[0] = (me[0] ^ row_partner[me[0], me[1]]) - 1
    other = me[1] ^ 1
    wish[0] = div(other ^ col_partner[me[0], other], 2)


def make_tables(me, row_partner, col_partner, coords, counts, places, block_cols):
    smem = pl.BlockSpec(memory_space=pltpu.SMEM)
    return pl.pallas_call(
        functools.partial(tables_kernel, block_cols),
        in_specs=[smem] * 5,
        out_specs=[smem] * 3,
        out_shape=[jax.ShapeDtypeStruct((n,), jnp.int32) for n in (places, 1, 1)],
        cost_estimate=cost(0),
        name="make_tables",
    )(me, row_partner, col_partner, coords, counts)


class Columns:
    ON, REST, KEPT = range(3)

    def __init__(self, kind, block_cols):
        self.kind = kind
        self.given = kind != self.KEPT
        self.half_cols = block_cols // 2
        self.steps = block_cols if kind == self.KEPT else self.half_cols

    def half(self, step, me, row_partner, col_partner):
        if self.kind == self.KEPT:
            goes_on = (me[1] < col_partner[me[0], me[1]]).astype(jnp.int32)
            return goes_on ^ div(step, self.half_cols)
        goes_on = (me[1] < col_partner[row_partner[me[0], me[1]], me[1]]).astype(jnp.int32)
        return goes_on ^ (1 if self.kind == self.REST else 0)

    def column(self, step, me, row_partner, col_partner):
        half = self.half(step, me, row_partner, col_partner)
        return half * self.half_cols + rem(step, self.half_cols)


def left_kernel(columns, block_cols, half_rows, per_step, *refs):
    me, slots, row_partner, col_partner = refs[:4]
    tile_refs, q_refs, out, q_both = refs[4 : 4 + per_step], refs[4 + per_step : -2], refs[-2], refs[-1]
    group, step = pl.program_id(0), pl.program_id(1)
    width = q_both.shape[0] // 2

    block_row = half_of(columns.given, me, row_partner) * half_rows + group

    def put(value, first):
        high, low = split(value.T)
        q_both[:width, first : first + value.shape[0]] = high
        q_both[width:, first : first + value.shape[0]] = low

    if len(q_refs) == 1:

        @pl.when(step == 0)
        def _():
            put(q_refs[0][...], 0)

    else:
        distance = block_row ^ div(me[1], 2)
        for core in range(2):

            @pl.when((step == 0) & (rem(me[1], 2) == core))
            def _():
                depth = q_refs[0].shape[1]
                put(q_refs[0][distance], core * depth)
                put(q_refs[1][distance], (1 - core) * depth)

    for index, tile_ref in enumerate(tile_refs):
        column = columns.column(step * per_step + index, me, row_partner, col_partner)
        live = slots[block_row * block_cols + column] >= 0
        high, low = split(tile_ref[0])
        total = jnp.where(live, product(q_both[...], high, low), 0.0)
        out[index, 0], out[index, 1] = split(total)


def left_products(kind, tables, tiles, q_pieces, half_rows, block_cols):
    _, tile_order, _ = tiles.shape
    width = q_pieces[0].shape[-1]
    columns = Columns(kind, block_cols)
    per_step = 2 if columns.steps % 2 == 0 else 1

    def row_of(g, me, row_partner):
        return half_of(columns.given, me, row_partner) * half_rows + g

    def tile_spec(index):
        def tile_at(g, b, me, slots, row_partner, col_partner):
            column = columns.column(b * per_step + index, me, row_partner, col_partner)
            return jnp.maximum(slots[row_of(g, me, row_partner) * block_cols + column], 0), 0, 0

        return pl.BlockSpec((1, tile_order, tile_order), tile_at)

    if len(q_pieces) == 1:
        q_specs = [
            pl.BlockSpec(
                (tile_order, width),
                lambda g, b, me, slots, row_partner, _: (row_of(g, me, row_partner), 0),
            )
        ]
    else:
        q_specs = [pl.BlockSpec(memory_space=pltpu.VMEM)] * len(q_pieces)
    return pl.pallas_call(
        functools.partial(left_kernel, columns, block_cols, half_rows, per_step),
        grid_spec=pltpu.PrefetchScalarGridSpec(
            num_scalar_prefetch=4,
            grid=(half_rows, columns.steps // per_step),
            in_specs=[tile_spec(index) for index in range(per_step)] + q_specs,
            out_specs=pl.BlockSpec(
                (per_step, 2, width, tile_order), lambda g, b, *_: (b, 0, g, 0)
            ),
            scratch_shapes=[pltpu.VMEM((2 * width, tile_order), BF16)],
        ),
        out_shape=jax.ShapeDtypeStruct((columns.steps, 2, half_rows * width, tile_order), BF16),
        compiler_params=PARAMS,
        cost_estimate=cost(12 * half_rows * columns.steps * width * tile_order * tile_order),
        name="left_products",
    )(*tables, *[tiles] * per_step, *q_pieces)


def packed_first(blocks):
    return max(1, blocks * 3 // 4)


def packed_place(slots, first_row, first_col, half_rows, half_cols, block_cols, block):
    before = here = count = jnp.int32(0)
    for index in range(half_rows * half_cols):
        place = (first_row + index % half_rows) * block_cols + first_col + index // half_rows
        flag = (slots[place] >= 0).astype(jnp.int32)
        before = before + jnp.where(index < block, flag, 0)
        here = here + jnp.where(index == block, flag, 0)
        count = count + flag
    return jnp.where(here == 1, before, count + block - before), here == 1


def quarter_live(table, first_row, first_col, half_rows, half_cols, block_cols):
    count = jnp.int32(0)
    for index in range(half_rows * half_cols):
        place = (first_row + index % half_rows) * block_cols + first_col + index // half_rows
        count = count + (table[place] >= 0).astype(jnp.int32)
    return count


def right_kernel(columns, block_cols, half_rows, starts, *refs):
    me, slots, mate_slots, row_partner, col_partner, w_ref = refs[:6]
    pieces = refs[6 : 6 + len(starts)]
    step = pl.program_id(0)
    tile_order = w_ref.shape[3]
    width = pieces[0].shape[1]
    packs = columns.kind == Columns.REST
    outs = refs[6 + len(starts) : -3 if packs else -2]
    p_high, p_low = refs[-2:]

    @pl.when(step == 0)
    def _():
        half = columns.half(step, me, row_partner, col_partner)
        for (start, filled), piece in zip(starts, pieces):
            wanted = start(me) >= 0
            if columns.given:
                wanted = div(start(me), columns.half_cols * tile_order) == half
            if filled is not None:
                wanted &= filled(me)

            @pl.when(wanted)
            def _():
                depth = piece.shape[0]
                rows = pl.ds(pl.multiple_of(start(me), depth), depth)
                p_high[rows, :], p_low[rows, :] = split(piece[...])

    column = columns.column(step, me, row_partner, col_partner)
    rows = pl.ds(pl.multiple_of(column * tile_order, tile_order), tile_order)
    both = w_ref[step if columns.given else 0].reshape(2 * w_ref.shape[2], tile_order)
    block = product(both, p_high[rows, :], p_low[rows, :])
    half_cols = columns.half_cols
    if not packs:
        for index, out in enumerate(outs):

            @pl.when(jnp.minimum(step, half_cols) == index)
            def _():
                out[...] = block

        return
    branch, *outs = outs
    packed = refs[-3]
    first_row = half_of(True, me, row_partner) * half_rows
    first_col = columns.half(step, me, row_partner, col_partner) * half_cols
    for row in range(half_rows):
        place, _ = packed_place(
            slots, first_row, first_col, half_rows, half_cols, block_cols, step * half_rows + row
        )
        packed[place] = block[row * width : (row + 1) * width]

    @pl.when(step == half_cols - 1)
    def _():
        count = outs[0].shape[0]
        outs[0][...] = packed[:count]
        for index, out in enumerate(outs[1:]):
            out[...] = packed[count + index]
        keeps = (me[1] > col_partner[me[0], me[1]]).astype(jnp.int32)
        mate_row = half_of(False, me, row_partner) * half_rows
        quarter = half_rows, half_cols, block_cols
        most = jnp.maximum(
            quarter_live(slots, first_row, first_col, *quarter),
            quarter_live(mate_slots, mate_row, keeps * half_cols, *quarter),
        )
        choice = jnp.clip(most - count, 0, len(outs) - 1)
        branch[0] = ((me[0] ^ row_partner[me[0], me[1]]) - 1) * len(outs) + choice


def right_products(kind, tables, w, shards, half_rows, block_cols):
    _, _, height, tile_order = w.shape
    columns = Columns(kind, block_cols)
    half_cols = columns.half_cols
    width = shards[0][0].shape[1]
    blocks = half_rows * half_cols

    whole = pl.BlockSpec(memory_space=pltpu.VMEM)
    one_column = pl.BlockSpec((1, 2, height, tile_order), lambda i, *_: (i, 0, 0, 0))
    scratch = [pltpu.VMEM((block_cols * tile_order, width), BF16)] * 2
    if kind == Columns.REST:
        most = packed_first(blocks)
        shapes = [(most, width, width)] + [(width, width)] * (blocks - most)
        out_specs = [pl.BlockSpec(memory_space=pltpu.SMEM)]
        out_specs += [pl.BlockSpec(shape, lambda i, *_, n=len(shape): (0,) * n) for shape in shapes]
        scratch = [pltpu.VMEM((blocks, width, width), F32)] + scratch
    else:
        shapes = [(height, width)] * half_cols
        out_specs = [pl.BlockSpec((height, width), lambda i, *_: (0, 0))] * half_cols
        if kind == Columns.KEPT:
            shapes += [(height, half_cols * width)]
            out_specs += [
                pl.BlockSpec((height, width), lambda i, *_: (0, jnp.maximum(i - half_cols, 0)))
            ]
    out_shape = [jax.ShapeDtypeStruct(shape, F32) for shape in shapes]
    if kind == Columns.REST:
        out_shape = [jax.ShapeDtypeStruct((1,), jnp.int32)] + out_shape
    return pl.pallas_call(
        functools.partial(
            right_kernel, columns, block_cols, half_rows, [shard[1:] for shard in shards]
        ),
        grid_spec=pltpu.PrefetchScalarGridSpec(
            num_scalar_prefetch=5,
            grid=(columns.steps,),
            in_specs=[whole if columns.given else one_column] + [whole] * len(shards),
            out_specs=out_specs,
            scratch_shapes=scratch,
        ),
        out_shape=out_shape,
        compiler_params=PARAMS,
        cost_estimate=cost(6 * columns.steps * height * width * tile_order),
        name="right_products",
    )(*tables, w, *[shard[0] for shard in shards])


def comes_from(which, me, col_partner):
    distance = me[1] ^ col_partner[me[0], me[1]]
    core = rem(distance, 2) == 1
    return core if which == 0 else jnp.logical_not(core) & (div(distance, 2) == which - 1)


def sum_kernel(half_rows, block_cols, singles, sections, *refs):
    me, _, mate_slots, row_partner, col_partner, kept_ref, packed_ref = refs[:7]
    single_refs, section_refs, out = refs[7 : 7 + singles], refs[7 + singles : -1], refs[-1]
    half_cols = block_cols // 2
    step = pl.program_id(0)
    keeps = (me[1] > col_partner[me[0], me[1]]).astype(jnp.int32)
    first_row = half_of(False, me, row_partner) * half_rows
    place, live = packed_place(
        mate_slots, first_row, keeps * half_cols, half_rows, half_cols, block_cols, step
    )
    count = packed_ref.shape[0]
    at = 0
    for index, kind in enumerate(sections):
        for which in range(kind):
            section = section_refs[at + which]
            wanted = div(step, half_rows) == index
            if kind > 1:
                wanted &= comes_from(which, me, col_partner)

            @pl.when(wanted)
            def _():
                out[...] = kept_ref[...] + section[...].reshape(out.shape)

        at += kind

    @pl.when(live & (place < count))
    def _():
        out[...] += packed_ref[jnp.minimum(place, count - 1)]

    for index, single in enumerate(single_refs):

        @pl.when(live & (place == count + index))
        def _():
            out[...] += single[...]


def sum_blocks(tables, half_rows, block_cols, kept, packed, singles, sections):
    half_cols = block_cols // 2
    height, both = kept.shape
    width = both // half_cols
    block = pl.BlockSpec((width, width), lambda i, *_: (rem(i, half_rows), div(i, half_rows)))

    def section_spec(index, section, which=None):
        def section_at(i, me, slots, mate_slots, row_partner, col_partner):
            here = jnp.clip(i - index * half_rows, 0, half_rows - 1)
            if which is not None:
                here = jnp.where(comes_from(which, me, col_partner), here, 0)
            if section.ndim == 2:
                return here, 0
            return index if which == 0 else col_partner[me[0], me[1]], here, 0

        return pl.BlockSpec((1,) * (section.ndim - 2) + (width, width), section_at)

    return pl.pallas_call(
        functools.partial(
            sum_kernel, half_rows, block_cols, len(singles), [len(each) for each in sections]
        ),
        grid_spec=pltpu.PrefetchScalarGridSpec(
            num_scalar_prefetch=5,
            grid=(half_rows * half_cols,),
            in_specs=[block]
            + [pl.BlockSpec(memory_space=pltpu.VMEM)] * (1 + len(singles))
            + [
                section_spec(index, each, which if len(group) > 1 else None)
                for index, group in enumerate(sections)
                for which, each in enumerate(group)
            ],
            out_specs=block,
        ),
        out_shape=jax.ShapeDtypeStruct((height, both), F32),
        compiler_params=PARAMS,
        name="sum_blocks",
    )(*tables, kept, packed, *singles, *[each for group in sections for each in group])


def wished_kernel(wish, *refs):
    *sections, wanted = refs
    for index, section in enumerate(sections):

        @pl.when((pl.program_id(0) == index // 4) & (wish[0] == index % 4))
        def _():
            wanted[0] = section[...]


def wished(wish, overs):
    height, width = overs[0][0].shape
    steps = 2 if height % 16 == 0 else 1

    def chip_spec(column, chip):
        def chip_at(b, i, wish):
            here = jnp.where(b == column, i, jnp.where(b < column, 0, steps - 1))
            return jnp.where(wish[0] == chip, here, 0), 0

        return pl.BlockSpec((height // steps, width), chip_at)

    return pl.pallas_call(
        wished_kernel,
        grid_spec=pltpu.PrefetchScalarGridSpec(
            num_scalar_prefetch=1,
            grid=(len(overs), steps),
            in_specs=[chip_spec(b, chip) for b in range(len(overs)) for chip in range(4)],
            out_specs=pl.BlockSpec((1, height // steps, width), lambda b, i, _: (b, i, 0)),
        ),
        out_shape=jax.ShapeDtypeStruct((len(overs), height, width), F32),
        compiler_params=PARAMS,
        cost_estimate=cost(0),
        name="wished",
    )(wish, *[section for over in overs for section in over])


def flip(value, axis, size, mask):
    return lax.ppermute(value, axis, [(i, i ^ mask) for i in range(size)])


def hand_out(part, axis):
    return lax.ppermute(part, axis, [(1, 0), (2, 3)])


def first_prolong(shard, axis, size):
    if size != 4:
        return None
    part = shard.shape[0] // 2
    by_two = [flip(each, axis, size, 2) for each in (shard[:part], shard[part:])]
    near = [*by_two, flip(shard, axis, size, 1), lax.ppermute(shard, axis, [(1, 2), (2, 1)])]
    return near + [hand_out(by_two[0], axis)]


def gather_prolong(shard, near, axis, size):
    depth = shard.shape[0]
    if near is None:
        gathered = lax.all_gather(shard, axis)
        return [(gathered[i], lambda me, i=i: jnp.int32(i * depth), None) for i in range(size)]
    *by_two, by_one, middle, handed = near
    handed = [handed, hand_out(by_two[1], axis)]

    def at(mask, first=0):
        return lambda me: (me[0] ^ mask) * depth + first

    def inner(me):
        return (me[0] == 1) | (me[0] == 2)

    pieces = [(shard, at(0), None), (by_one, at(1), None), (middle, at(3), inner)]
    for index in range(2):
        first = index * (depth // 2)
        pieces.append((by_two[index], at(2, first), None))
        pieces.append((handed[index], at(3, first), lambda me: jnp.logical_not(inner(me))))
    return pieces


def gather_restrict(shard, near, slots, axis, size):
    over_x = flip(shard, axis, size, 2)
    over_y = flip(shard, axis, size, 4)
    if near is not None:
        over_x, near[0], slots = lax.optimization_barrier((over_x, near[0], slots))
    pieces = [shard, over_x, over_y, flip(over_x, axis, size, 4)]
    if near is not None:
        pieces, near[1:3], near[4] = lax.optimization_barrier((pieces, near[1:3], near[4]))
    mine = jnp.stack(pieces)
    return [mine, flip(mine, axis, size, 1)], slots


def pair_switch(index, size, branch, operand, choices=1):
    branches = [
        functools.partial(branch, mask, choice) for mask in range(1, size) for choice in range(choices)
    ]
    return lax.switch(index[0], branches, operand)


def solution(mesh):
    n_row = mesh.shape["row"]
    n_col = mesh.shape["col"]

    def body(tiles, coords, counts, restrict, prolong, row_partner, col_partner):
        tile_order = tiles.shape[1]
        block_rows = restrict.shape[0] * n_col // tile_order
        block_cols = prolong.shape[0] * n_row // tile_order
        half_rows, half_cols = block_rows // 2, block_cols // 2
        row = lax.axis_index("row").astype(jnp.int32)
        col = lax.axis_index("col").astype(jnp.int32)
        me = jnp.stack([row, col])

        row_partner, coords = row_partner.T, coords.T
        places = block_rows * block_cols
        slots, first, wish = make_tables(
            me, row_partner, col_partner, coords, counts, places, block_cols
        )
        near = first_prolong(prolong, "row", n_row)
        by_chip = n_col == 8 and block_rows == 4 and tile_order == 2 * restrict.shape[0]
        if by_chip:
            q_pieces, slots = gather_restrict(restrict, near, slots, "col", n_col)
        else:
            q_pieces = [lax.all_gather(restrict, "col", axis=0, tiled=True)]

        shards = gather_prolong(prolong, near, "row", n_row)

        def products(kind, mate_slots):
            tables = (me, slots, row_partner, col_partner)
            w = left_products(kind, tables, tiles, q_pieces, half_rows, block_cols)
            tables = (me, slots, mate_slots, row_partner, col_partner)
            return right_products(kind, tables, w, shards, half_rows, block_cols)

        def swap_first(mask, _, chunk):
            received = flip(chunk, "row", n_row, mask)
            return received, flip(slots, "row", n_row, mask), products(Columns.KEPT, slots)

        def swap_next(mask, _, operands):
            chunk, mate_slots = operands
            return flip(chunk, "row", n_row, mask), products(Columns.REST, mate_slots)

        def swap_more(mask, _, operands):
            return flip(operands[0], "row", n_row, mask), operands[1:]

        def swap_rest(mask, extra, rest):
            return [
                flip(array, "row", n_row, mask) if index <= extra else array
                for index, array in enumerate(rest)
            ]

        given = products(Columns.ON, slots)
        received, mate_slots, kept = pair_switch(first, n_row, swap_first, given[0])
        sections, rest = [], None
        for index in range(half_cols):
            section = kept[index] + received
            if n_col == 8:
                over = [section] + [flip(section, "col", n_col, 2 * chip) for chip in range(1, 4)]
            else:
                over = [lax.all_gather(section, "col")]
            sections.append(over)
            if index + 1 == half_cols:
                break
            chunk, section = lax.optimization_barrier((given[index + 1], section))
            if index == 0:
                received, rest = pair_switch(first, n_row, swap_next, (chunk, mate_slots))
            else:
                received, *_ = pair_switch(first, n_row, swap_more, (chunk,))
            sections[index], received = lax.optimization_barrier((sections[index], received))
        if rest is None:
            rest = products(Columns.REST, mate_slots)
        second, *rest = rest
        rest, section = lax.optimization_barrier((rest, section))
        rest = pair_switch(second, n_row, swap_rest, rest, len(rest))
        if n_col == 8:
            sections[-1], rest = lax.optimization_barrier((sections[-1], rest))
            handed = flip(wished(wish, sections), "col", n_col, 1)
            sections = [[handed] + over for over in sections]
        packed, *singles = rest
        tables = (me, slots, mate_slots, row_partner, col_partner)
        return sum_blocks(tables, half_rows, block_cols, kept[-1], packed, singles, sections)

    in_specs = (
        P(("row", "col"), None, None),
        P(("row", "col"), None),
        P(("row", "col")),
        P(("row", "col"), None),
        P(("col", "row"), None),
        P(),
        P(),
    )
    return jax.shard_map(
        body, mesh=mesh, in_specs=in_specs, out_specs=P("row", "col"), check_vma=False
    )
```

```python
import functools

import jax
import jax.numpy as jnp
from jax import lax
from jax.experimental import pallas as pl
from jax.experimental.pallas import tpu as pltpu
from jax.sharding import PartitionSpec as P

F32 = jnp.float32
BF16 = jnp.bfloat16
VMEM_BYTES = 48 * 1024 * 1024
PARAMS = pltpu.CompilerParams(vmem_limit_bytes=VMEM_BYTES)


def cost(flops):
    return pl.CostEstimate(flops=flops, bytes_accessed=0, transcendentals=0)


def split(value):
    high = value.astype(BF16)
    low = (value - high.astype(F32)).astype(BF16)
    return high, low


def dot(left, right):
    return jnp.dot(left, right, preferred_element_type=F32)


def product(left_both, right_high, right_low):
    half = left_both.shape[0] // 2
    total = dot(left_both[half:], right_high)
    total = total + dot(left_both[:half], right_low)
    return total + dot(left_both[:half], right_high)


def div(value, by):
    return lax.div(value, jnp.int32(by))


def rem(value, by):
    return lax.rem(value, jnp.int32(by))


def half_of(given, me, row_partner):
    mate = row_partner[me[0], me[1]]
    return ((mate > me[0]) if given else (me[0] > mate)).astype(jnp.int32)


def tables_kernel(block_cols, me, row_partner, col_partner, coords, counts, slots, first, wish):
    for place in range(slots.shape[0]):
        slots[place] = jnp.int32(-1)
    for slot in range(coords.shape[1]):

        @pl.when(slot < counts[0])
        def _():
            slots[coords[0, slot] * block_cols + coords[1, slot]] = jnp.int32(slot)

    first[0] = (me[0] ^ row_partner[me[0], me[1]]) - 1
    other = me[1] ^ 1
    wish[0] = div(other ^ col_partner[me[0], other], 2)


def make_tables(me, row_partner, col_partner, coords, counts, places, block_cols):
    smem = pl.BlockSpec(memory_space=pltpu.SMEM)
    return pl.pallas_call(
        functools.partial(tables_kernel, block_cols),
        in_specs=[smem] * 5,
        out_specs=[smem] * 3,
        out_shape=[jax.ShapeDtypeStruct((n,), jnp.int32) for n in (places, 1, 1)],
        cost_estimate=cost(0),
        name="make_tables",
    )(me, row_partner, col_partner, coords, counts)


class Columns:
    ON, REST, KEPT = range(3)

    def __init__(self, kind, block_cols):
        self.kind = kind
        self.given = kind != self.KEPT
        self.half_cols = block_cols // 2
        self.steps = block_cols if kind == self.KEPT else self.half_cols

    def half(self, step, me, row_partner, col_partner):
        if self.kind == self.KEPT:
            goes_on = (me[1] < col_partner[me[0], me[1]]).astype(jnp.int32)
            return goes_on ^ div(step, self.half_cols)
        goes_on = (me[1] < col_partner[row_partner[me[0], me[1]], me[1]]).astype(jnp.int32)
        return goes_on ^ (1 if self.kind == self.REST else 0)

    def column(self, step, me, row_partner, col_partner):
        half = self.half(step, me, row_partner, col_partner)
        return half * self.half_cols + rem(step, self.half_cols)


def left_kernel(columns, block_cols, half_rows, per_step, *refs):
    me, slots, row_partner, col_partner = refs[:4]
    tile_refs, q_refs, out, q_both = refs[4 : 4 + per_step], refs[4 + per_step : -2], refs[-2], refs[-1]
    group, step = pl.program_id(0), pl.program_id(1)
    width = q_both.shape[0] // 2

    block_row = half_of(columns.given, me, row_partner) * half_rows + group

    def put(value, first):
        high, low = split(value.T)
        q_both[:width, first : first + value.shape[0]] = high
        q_both[width:, first : first + value.shape[0]] = low

    if len(q_refs) == 1:

        @pl.when(step == 0)
        def _():
            put(q_refs[0][...], 0)

    else:
        distance = block_row ^ div(me[1], 2)
        for core in range(2):

            @pl.when((step == 0) & (rem(me[1], 2) == core))
            def _():
                depth = q_refs[0].shape[1]
                put(q_refs[0][distance], core * depth)
                put(q_refs[1][distance], (1 - core) * depth)

    for index, tile_ref in enumerate(tile_refs):
        column = columns.column(step * per_step + index, me, row_partner, col_partner)
        live = slots[block_row * block_cols + column] >= 0
        high, low = split(tile_ref[0])
        total = jnp.where(live, product(q_both[...], high, low), 0.0)
        out[index, 0], out[index, 1] = split(total)


def left_products(kind, tables, tiles, q_pieces, half_rows, block_cols):
    _, tile_order, _ = tiles.shape
    width = q_pieces[0].shape[-1]
    columns = Columns(kind, block_cols)
    per_step = 2 if columns.steps % 2 == 0 else 1

    def row_of(g, me, row_partner):
        return half_of(columns.given, me, row_partner) * half_rows + g

    def tile_spec(index):
        def tile_at(g, b, me, slots, row_partner, col_partner):
            column = columns.column(b * per_step + index, me, row_partner, col_partner)
            return jnp.maximum(slots[row_of(g, me, row_partner) * block_cols + column], 0), 0, 0

        return pl.BlockSpec((1, tile_order, tile_order), tile_at)

    if len(q_pieces) == 1:
        q_specs = [
            pl.BlockSpec(
                (tile_order, width),
                lambda g, b, me, slots, row_partner, _: (row_of(g, me, row_partner), 0),
            )
        ]
    else:
        q_specs = [pl.BlockSpec(memory_space=pltpu.VMEM)] * len(q_pieces)
    return pl.pallas_call(
        functools.partial(left_kernel, columns, block_cols, half_rows, per_step),
        grid_spec=pltpu.PrefetchScalarGridSpec(
            num_scalar_prefetch=4,
            grid=(half_rows, columns.steps // per_step),
            in_specs=[tile_spec(index) for index in range(per_step)] + q_specs,
            out_specs=pl.BlockSpec(
                (per_step, 2, width, tile_order), lambda g, b, *_: (b, 0, g, 0)
            ),
            scratch_shapes=[pltpu.VMEM((2 * width, tile_order), BF16)],
        ),
        out_shape=jax.ShapeDtypeStruct((columns.steps, 2, half_rows * width, tile_order), BF16),
        compiler_params=PARAMS,
        cost_estimate=cost(12 * half_rows * columns.steps * width * tile_order * tile_order),
        name="left_products",
    )(*tables, *[tiles] * per_step, *q_pieces)


def packed_first(blocks):
    return max(1, blocks * 3 // 4)


def packed_place(slots, first_row, first_col, half_rows, half_cols, block_cols, block):
    before = here = count = jnp.int32(0)
    for index in range(half_rows * half_cols):
        place = (first_row + index % half_rows) * block_cols + first_col + index // half_rows
        flag = (slots[place] >= 0).astype(jnp.int32)
        before = before + jnp.where(index < block, flag, 0)
        here = here + jnp.where(index == block, flag, 0)
        count = count + flag
    return jnp.where(here == 1, before, count + block - before), here == 1


def quarter_live(table, first_row, first_col, half_rows, half_cols, block_cols):
    count = jnp.int32(0)
    for index in range(half_rows * half_cols):
        place = (first_row + index % half_rows) * block_cols + first_col + index // half_rows
        count = count + (table[place] >= 0).astype(jnp.int32)
    return count


def right_kernel(columns, block_cols, half_rows, starts, *refs):
    me, slots, mate_slots, row_partner, col_partner, w_ref = refs[:6]
    pieces = refs[6 : 6 + len(starts)]
    step = pl.program_id(0)
    tile_order = w_ref.shape[3]
    width = pieces[0].shape[1]
    packs = columns.kind == Columns.REST
    outs = refs[6 + len(starts) : -3 if packs else -2]
    p_high, p_low = refs[-2:]

    @pl.when(step == 0)
    def _():
        half = columns.half(step, me, row_partner, col_partner)
        for (start, filled), piece in zip(starts, pieces):
            wanted = start(me) >= 0
            if columns.given:
                wanted = div(start(me), columns.half_cols * tile_order) == half
            if filled is not None:
                wanted &= filled(me)

            @pl.when(wanted)
            def _():
                depth = piece.shape[0]
                rows = pl.ds(pl.multiple_of(start(me), depth), depth)
                p_high[rows, :], p_low[rows, :] = split(piece[...])

    column = columns.column(step, me, row_partner, col_partner)
    rows = pl.ds(pl.multiple_of(column * tile_order, tile_order), tile_order)
    both = w_ref[step if columns.given else 0].reshape(2 * w_ref.shape[2], tile_order)
    block = product(both, p_high[rows, :], p_low[rows, :])
    half_cols = columns.half_cols
    if not packs:
        for index, out in enumerate(outs):

            @pl.when(jnp.minimum(step, half_cols) == index)
            def _():
                out[...] = block

        return
    branch, *outs = outs
    packed = refs[-3]
    first_row = half_of(True, me, row_partner) * half_rows
    first_col = columns.half(step, me, row_partner, col_partner) * half_cols
    for row in range(half_rows):
        place, _ = packed_place(
            slots, first_row, first_col, half_rows, half_cols, block_cols, step * half_rows + row
        )
        packed[place] = block[row * width : (row + 1) * width]

    @pl.when(step == half_cols - 1)
    def _():
        count = outs[0].shape[0]
        outs[0][...] = packed[:count]
        for index, out in enumerate(outs[1:]):
            out[...] = packed[count + index]
        keeps = (me[1] > col_partner[me[0], me[1]]).astype(jnp.int32)
        mate_row = half_of(False, me, row_partner) * half_rows
        quarter = half_rows, half_cols, block_cols
        most = jnp.maximum(
            quarter_live(slots, first_row, first_col, *quarter),
            quarter_live(mate_slots, mate_row, keeps * half_cols, *quarter),
        )
        choice = jnp.clip(most - count, 0, len(outs) - 1)
        branch[0] = ((me[0] ^ row_partner[me[0], me[1]]) - 1) * len(outs) + choice


def right_products(kind, tables, w, shards, half_rows, block_cols):
    _, _, height, tile_order = w.shape
    columns = Columns(kind, block_cols)
    half_cols = columns.half_cols
    width = shards[0][0].shape[1]
    blocks = half_rows * half_cols

    whole = pl.BlockSpec(memory_space=pltpu.VMEM)
    one_column = pl.BlockSpec((1, 2, height, tile_order), lambda i, *_: (i, 0, 0, 0))
    scratch = [pltpu.VMEM((block_cols * tile_order, width), BF16)] * 2
    if kind == Columns.REST:
        most = packed_first(blocks)
        shapes = [(most, width, width)] + [(width, width)] * (blocks - most)
        out_specs = [pl.BlockSpec(memory_space=pltpu.SMEM)]
        out_specs += [pl.BlockSpec(shape, lambda i, *_, n=len(shape): (0,) * n) for shape in shapes]
        scratch = [pltpu.VMEM((blocks, width, width), F32)] + scratch
    else:
        shapes = [(height, width)] * half_cols
        out_specs = [pl.BlockSpec((height, width), lambda i, *_: (0, 0))] * half_cols
        if kind == Columns.KEPT:
            shapes += [(height, half_cols * width)]
            out_specs += [
                pl.BlockSpec((height, width), lambda i, *_: (0, jnp.maximum(i - half_cols, 0)))
            ]
    out_shape = [jax.ShapeDtypeStruct(shape, F32) for shape in shapes]
    if kind == Columns.REST:
        out_shape = [jax.ShapeDtypeStruct((1,), jnp.int32)] + out_shape
    return pl.pallas_call(
        functools.partial(
            right_kernel, columns, block_cols, half_rows, [shard[1:] for shard in shards]
        ),
        grid_spec=pltpu.PrefetchScalarGridSpec(
            num_scalar_prefetch=5,
            grid=(columns.steps,),
            in_specs=[whole if columns.given else one_column] + [whole] * len(shards),
            out_specs=out_specs,
            scratch_shapes=scratch,
        ),
        out_shape=out_shape,
        compiler_params=PARAMS,
        cost_estimate=cost(6 * columns.steps * height * width * tile_order),
        name="right_products",
    )(*tables, w, *[shard[0] for shard in shards])


def comes_from(which, me, col_partner):
    distance = me[1] ^ col_partner[me[0], me[1]]
    core = rem(distance, 2) == 1
    return core if which == 0 else jnp.logical_not(core) & (div(distance, 2) == which - 1)


def sum_kernel(half_rows, block_cols, singles, sections, *refs):
    me, _, mate_slots, row_partner, col_partner, kept_ref, packed_ref = refs[:7]
    single_refs, section_refs, out = refs[7 : 7 + singles], refs[7 + singles : -1], refs[-1]
    half_cols = block_cols // 2
    step = pl.program_id(0)
    keeps = (me[1] > col_partner[me[0], me[1]]).astype(jnp.int32)
    first_row = half_of(False, me, row_partner) * half_rows
    place, live = packed_place(
        mate_slots, first_row, keeps * half_cols, half_rows, half_cols, block_cols, step
    )
    count = packed_ref.shape[0]
    at = 0
    for index, kind in enumerate(sections):
        for which in range(kind):
            section = section_refs[at + which]
            wanted = div(step, half_rows) == index
            if kind > 1:
                wanted &= comes_from(which, me, col_partner)

            @pl.when(wanted)
            def _():
                out[...] = kept_ref[...] + section[...].reshape(out.shape)

        at += kind

    @pl.when(live & (place < count))
    def _():
        out[...] += packed_ref[jnp.minimum(place, count - 1)]

    for index, single in enumerate(single_refs):

        @pl.when(live & (place == count + index))
        def _():
            out[...] += single[...]


def sum_blocks(tables, half_rows, block_cols, kept, packed, singles, sections):
    half_cols = block_cols // 2
    height, both = kept.shape
    width = both // half_cols
    block = pl.BlockSpec((width, width), lambda i, *_: (rem(i, half_rows), div(i, half_rows)))

    def section_spec(index, section, which=None):
        def section_at(i, me, slots, mate_slots, row_partner, col_partner):
            here = jnp.clip(i - index * half_rows, 0, half_rows - 1)
            if which is not None:
                here = jnp.where(comes_from(which, me, col_partner), here, 0)
            if section.ndim == 2:
                return here, 0
            return index if which == 0 else col_partner[me[0], me[1]], here, 0

        return pl.BlockSpec((1,) * (section.ndim - 2) + (width, width), section_at)

    return pl.pallas_call(
        functools.partial(
            sum_kernel, half_rows, block_cols, len(singles), [len(each) for each in sections]
        ),
        grid_spec=pltpu.PrefetchScalarGridSpec(
            num_scalar_prefetch=5,
            grid=(half_rows * half_cols,),
            in_specs=[block]
            + [pl.BlockSpec(memory_space=pltpu.VMEM)] * (1 + len(singles))
            + [
                section_spec(index, each, which if len(group) > 1 else None)
                for index, group in enumerate(sections)
                for which, each in enumerate(group)
            ],
            out_specs=block,
        ),
        out_shape=jax.ShapeDtypeStruct((height, both), F32),
        compiler_params=PARAMS,
        name="sum_blocks",
    )(*tables, kept, packed, *singles, *[each for group in sections for each in group])


def wished_kernel(wish, *refs):
    *sections, wanted = refs
    for index, section in enumerate(sections):

        @pl.when((pl.program_id(0) == index // 4) & (wish[0] == index % 4))
        def _():
            wanted[0] = section[...]


def wished(wish, overs):
    height, width = overs[0][0].shape
    steps = 2 if height % 16 == 0 else 1

    def chip_spec(column, chip):
        def chip_at(b, i, wish):
            here = jnp.where(b == column, i, jnp.where(b < column, 0, steps - 1))
            return jnp.where(wish[0] == chip, here, 0), 0

        return pl.BlockSpec((height // steps, width), chip_at)

    return pl.pallas_call(
        wished_kernel,
        grid_spec=pltpu.PrefetchScalarGridSpec(
            num_scalar_prefetch=1,
            grid=(len(overs), steps),
            in_specs=[chip_spec(b, chip) for b in range(len(overs)) for chip in range(4)],
            out_specs=pl.BlockSpec((1, height // steps, width), lambda b, i, _: (b, i, 0)),
        ),
        out_shape=jax.ShapeDtypeStruct((len(overs), height, width), F32),
        compiler_params=PARAMS,
        cost_estimate=cost(0),
        name="wished",
    )(wish, *[section for over in overs for section in over])


def flip(value, axis, size, mask):
    return lax.ppermute(value, axis, [(i, i ^ mask) for i in range(size)])


def first_prolong(shard, axis, size):
    if size != 4:
        return None
    by_two, by_one = flip(shard, axis, size, 2), flip(shard, axis, size, 1)
    return [by_two, by_one, lax.ppermute(shard, axis, [(1, 2), (2, 1)])]


def gather_prolong(shard, near, axis, size):
    depth = shard.shape[0]
    if near is None:
        gathered = lax.all_gather(shard, axis)
        return [(gathered[i], lambda me, i=i: jnp.int32(i * depth), None) for i in range(size)]
    by_two, by_one, middle = near
    handed = lax.ppermute(by_two, axis, [(1, 0), (2, 3)])

    def at(mask):
        return lambda me: (me[0] ^ mask) * depth

    def inner(me):
        return (me[0] == 1) | (me[0] == 2)

    return [
        (shard, at(0), None),
        (by_one, at(1), None),
        (by_two, at(2), None),
        (middle, at(3), inner),
        (handed, at(3), lambda me: jnp.logical_not(inner(me))),
    ]


def gather_restrict(shard, near, slots, axis, size):
    over_x = flip(shard, axis, size, 2)
    over_y = flip(shard, axis, size, 4)
    over_x, slots = lax.optimization_barrier((over_x, slots))
    pieces = [shard, over_x, over_y, flip(over_x, axis, size, 4)]
    if near is not None:
        pieces, near[:2] = lax.optimization_barrier((pieces, near[:2]))
    mine = jnp.stack(pieces)
    return [mine, flip(mine, axis, size, 1)], slots


def pair_switch(index, size, branch, operand, choices=1):
    branches = [
        functools.partial(branch, mask, choice) for mask in range(1, size) for choice in range(choices)
    ]
    return lax.switch(index[0], branches, operand)


def solution(mesh):
    n_row = mesh.shape["row"]
    n_col = mesh.shape["col"]

    def body(tiles, coords, counts, restrict, prolong, row_partner, col_partner):
        tile_order = tiles.shape[1]
        block_rows = restrict.shape[0] * n_col // tile_order
        block_cols = prolong.shape[0] * n_row // tile_order
        half_rows, half_cols = block_rows // 2, block_cols // 2
        row = lax.axis_index("row").astype(jnp.int32)
        col = lax.axis_index("col").astype(jnp.int32)
        me = jnp.stack([row, col])

        row_partner, coords = row_partner.T, coords.T
        places = block_rows * block_cols
        slots, first, wish = make_tables(
            me, row_partner, col_partner, coords, counts, places, block_cols
        )
        near = first_prolong(prolong, "row", n_row)
        by_chip = n_col == 8 and block_rows == 4 and tile_order == 2 * restrict.shape[0]
        if by_chip:
            q_pieces, slots = gather_restrict(restrict, near, slots, "col", n_col)
        else:
            q_pieces = [lax.all_gather(restrict, "col", axis=0, tiled=True)]

        shards = gather_prolong(prolong, near, "row", n_row)

        def products(kind, mate_slots):
            tables = (me, slots, row_partner, col_partner)
            w = left_products(kind, tables, tiles, q_pieces, half_rows, block_cols)
            tables = (me, slots, mate_slots, row_partner, col_partner)
            return right_products(kind, tables, w, shards, half_rows, block_cols)

        def swap_first(mask, _, chunk):
            received = flip(chunk, "row", n_row, mask)
            return received, flip(slots, "row", n_row, mask), products(Columns.KEPT, slots)

        def swap_next(mask, _, operands):
            chunk, mate_slots = operands
            return flip(chunk, "row", n_row, mask), products(Columns.REST, mate_slots)

        def swap_more(mask, _, operands):
            return flip(operands[0], "row", n_row, mask), operands[1:]

        def swap_rest(mask, extra, rest):
            return [
                flip(array, "row", n_row, mask) if index <= extra else array
                for index, array in enumerate(rest)
            ]

        given = products(Columns.ON, slots)
        received, mate_slots, kept = pair_switch(first, n_row, swap_first, given[0])
        sections, rest = [], None
        for index in range(half_cols):
            section = kept[index] + received
            if n_col == 8:
                over = [section] + [flip(section, "col", n_col, 2 * chip) for chip in range(1, 4)]
            else:
                over = [lax.all_gather(section, "col")]
            sections.append(over)
            if index + 1 == half_cols:
                break
            chunk, section = lax.optimization_barrier((given[index + 1], section))
            if index == 0:
                received, rest = pair_switch(first, n_row, swap_next, (chunk, mate_slots))
            else:
                received, *_ = pair_switch(first, n_row, swap_more, (chunk,))
            sections[index], received = lax.optimization_barrier((sections[index], received))
        if rest is None:
            rest = products(Columns.REST, mate_slots)
        second, *rest = rest
        rest, section = lax.optimization_barrier((rest, section))
        rest = pair_switch(second, n_row, swap_rest, rest, len(rest))
        if n_col == 8:
            sections[-1], rest = lax.optimization_barrier((sections[-1], rest))
            handed = flip(wished(wish, sections), "col", n_col, 1)
            sections = [[handed] + over for over in sections]
        packed, *singles = rest
        tables = (me, slots, mate_slots, row_partner, col_partner)
        return sum_blocks(tables, half_rows, block_cols, kept[-1], packed, singles, sections)

    in_specs = (
        P(("row", "col"), None, None),
        P(("row", "col"), None),
        P(("row", "col")),
        P(("row", "col"), None),
        P(("col", "row"), None),
        P(),
        P(),
    )
    return jax.shard_map(
        body, mesh=mesh, in_specs=in_specs, out_specs=P("row", "col"), check_vma=False
    )
```

```python
import functools

import jax
import jax.numpy as jnp
from jax import lax
from jax.experimental import pallas as pl
from jax.experimental.pallas import tpu as pltpu
from jax.sharding import PartitionSpec as P

F32 = jnp.float32
BF16 = jnp.bfloat16
VMEM_BYTES = 48 * 1024 * 1024
PARAMS = pltpu.CompilerParams(vmem_limit_bytes=VMEM_BYTES)


def cost(flops):
    return pl.CostEstimate(flops=flops, bytes_accessed=0, transcendentals=0)


def split(value):
    high = value.astype(BF16)
    low = (value - high.astype(F32)).astype(BF16)
    return high, low


def dot(left, right):
    return jnp.dot(left, right, preferred_element_type=F32)


def product(left_both, right_high, right_low):
    half = left_both.shape[0] // 2
    total = dot(left_both[half:], right_high)
    total = total + dot(left_both[:half], right_low)
    return total + dot(left_both[:half], right_high)


def div(value, by):
    return lax.div(value, jnp.int32(by))


def rem(value, by):
    return lax.rem(value, jnp.int32(by))


def half_of(given, me, row_partner):
    mate = row_partner[me[0], me[1]]
    return ((mate > me[0]) if given else (me[0] > mate)).astype(jnp.int32)


def tables_kernel(block_cols, me, row_partner, col_partner, coords, counts, slots, first, wish):
    for place in range(slots.shape[0]):
        slots[place] = jnp.int32(-1)
    for slot in range(coords.shape[1]):

        @pl.when(slot < counts[0])
        def _():
            slots[coords[0, slot] * block_cols + coords[1, slot]] = jnp.int32(slot)

    first[0] = (me[0] ^ row_partner[me[0], me[1]]) - 1
    other = me[1] ^ 1
    wish[0] = div(other ^ col_partner[me[0], other], 2)


def make_tables(me, row_partner, col_partner, coords, counts, places, block_cols):
    smem = pl.BlockSpec(memory_space=pltpu.SMEM)
    return pl.pallas_call(
        functools.partial(tables_kernel, block_cols),
        in_specs=[smem] * 5,
        out_specs=[smem] * 3,
        out_shape=[jax.ShapeDtypeStruct((n,), jnp.int32) for n in (places, 1, 1)],
        cost_estimate=cost(0),
        name="make_tables",
    )(me, row_partner, col_partner, coords, counts)


class Columns:
    FIRST, NEXT, REST, KEPT_ON, KEPT_REST = range(5)

    def __init__(self, kind, block_cols):
        self.kind = kind
        self.given = kind in (self.FIRST, self.NEXT, self.REST)
        self.half_cols = block_cols // 2
        self.skip = 1 if kind == self.NEXT else 0
        self.steps = 1 if kind == self.FIRST else self.half_cols - self.skip

    def half(self, me, row_partner, col_partner):
        holder = row_partner[me[0], me[1]] if self.given else me[0]
        goes_on = (me[1] < col_partner[holder, me[1]]).astype(jnp.int32)
        return goes_on ^ (1 if self.kind in (self.REST, self.KEPT_REST) else 0)

    def column(self, step, me, row_partner, col_partner):
        return self.half(me, row_partner, col_partner) * self.half_cols + self.skip + step


def left_kernel(columns, block_cols, half_rows, per_step, *refs):
    me, slots, row_partner, col_partner = refs[:4]
    tile_refs, q_refs, out, q_both = refs[4 : 4 + per_step], refs[4 + per_step : -2], refs[-2], refs[-1]
    group, step = pl.program_id(0), pl.program_id(1)
    width = q_both.shape[0] // 2

    block_row = half_of(columns.given, me, row_partner) * half_rows + group

    def put(value, first):
        high, low = split(value.T)
        q_both[:width, first : first + value.shape[0]] = high
        q_both[width:, first : first + value.shape[0]] = low

    if len(q_refs) == 1:

        @pl.when(step == 0)
        def _():
            put(q_refs[0][...], 0)

    else:
        distance = block_row ^ div(me[1], 2)
        for core in range(2):

            @pl.when((step == 0) & (rem(me[1], 2) == core))
            def _():
                depth = q_refs[0].shape[1]
                put(q_refs[0][distance], core * depth)
                put(q_refs[1][distance], (1 - core) * depth)

    for index, tile_ref in enumerate(tile_refs):
        column = columns.column(step * per_step + index, me, row_partner, col_partner)
        live = slots[block_row * block_cols + column] >= 0
        high, low = split(tile_ref[0])
        total = jnp.where(live, product(q_both[...], high, low), 0.0)
        out[index, 0], out[index, 1] = split(total)


def left_products(kind, tables, tiles, q_pieces, half_rows, block_cols):
    _, tile_order, _ = tiles.shape
    width = q_pieces[0].shape[-1]
    columns = Columns(kind, block_cols)
    per_step = 2 if columns.steps % 2 == 0 else 1

    def row_of(g, me, row_partner):
        return half_of(columns.given, me, row_partner) * half_rows + g

    def tile_spec(index):
        def tile_at(g, b, me, slots, row_partner, col_partner):
            column = columns.column(b * per_step + index, me, row_partner, col_partner)
            return jnp.maximum(slots[row_of(g, me, row_partner) * block_cols + column], 0), 0, 0

        return pl.BlockSpec((1, tile_order, tile_order), tile_at)

    if len(q_pieces) == 1:
        q_specs = [
            pl.BlockSpec(
                (tile_order, width),
                lambda g, b, me, slots, row_partner, _: (row_of(g, me, row_partner), 0),
            )
        ]
    else:
        q_specs = [pl.BlockSpec(memory_space=pltpu.VMEM)] * len(q_pieces)
    return pl.pallas_call(
        functools.partial(left_kernel, columns, block_cols, half_rows, per_step),
        grid_spec=pltpu.PrefetchScalarGridSpec(
            num_scalar_prefetch=4,
            grid=(half_rows, columns.steps // per_step),
            in_specs=[tile_spec(index) for index in range(per_step)] + q_specs,
            out_specs=pl.BlockSpec(
                (per_step, 2, width, tile_order), lambda g, b, *_: (b, 0, g, 0)
            ),
            scratch_shapes=[pltpu.VMEM((2 * width, tile_order), BF16)],
        ),
        out_shape=jax.ShapeDtypeStruct((columns.steps, 2, half_rows * width, tile_order), BF16),
        compiler_params=PARAMS,
        cost_estimate=cost(12 * half_rows * columns.steps * width * tile_order * tile_order),
        name="left_products",
    )(*tables, *[tiles] * per_step, *q_pieces)


def packed_first(blocks):
    return max(1, blocks * 3 // 4)


def packed_place(slots, first_row, first_col, half_rows, half_cols, block_cols, block):
    before = here = count = jnp.int32(0)
    for index in range(half_rows * half_cols):
        place = (first_row + index % half_rows) * block_cols + first_col + index // half_rows
        flag = (slots[place] >= 0).astype(jnp.int32)
        before = before + jnp.where(index < block, flag, 0)
        here = here + jnp.where(index == block, flag, 0)
        count = count + flag
    return jnp.where(here == 1, before, count + block - before), here == 1


def quarter_live(table, first_row, first_col, half_rows, half_cols, block_cols):
    count = jnp.int32(0)
    for index in range(half_rows * half_cols):
        place = (first_row + index % half_rows) * block_cols + first_col + index // half_rows
        count = count + (table[place] >= 0).astype(jnp.int32)
    return count


def right_kernel(columns, block_cols, half_rows, starts, *refs):
    me, slots, mate_slots, row_partner, col_partner, w_ref = refs[:6]
    pieces = refs[6 : 6 + len(starts)]
    step = pl.program_id(0)
    tile_order = w_ref.shape[3]
    width = pieces[0].shape[1]
    packs = columns.kind == Columns.REST
    outs = refs[6 + len(starts) : -3 if packs else -2]
    p_high, p_low = refs[-2:]

    @pl.when(step == 0)
    def _():
        low = columns.column(0, me, row_partner, col_partner) * tile_order
        for (start, filled), piece in zip(starts, pieces):
            begin = start(me)
            wanted = (begin < low + columns.steps * tile_order) & (begin + piece.shape[0] > low)
            if filled is not None:
                wanted &= filled(me)

            @pl.when(wanted)
            def _():
                depth = piece.shape[0]
                rows = pl.ds(pl.multiple_of(begin, depth), depth)
                p_high[rows, :], p_low[rows, :] = split(piece[...])

    column = columns.column(step, me, row_partner, col_partner)
    rows = pl.ds(pl.multiple_of(column * tile_order, tile_order), tile_order)
    both = w_ref[step].reshape(2 * w_ref.shape[2], tile_order)
    block = product(both, p_high[rows, :], p_low[rows, :])
    half_cols = columns.half_cols
    if not packs:
        for index, out in enumerate(outs):

            @pl.when((step == index) | (len(outs) == 1))
            def _():
                out[...] = block

        return
    branch, *outs = outs
    packed = refs[-3]
    first_row = half_of(True, me, row_partner) * half_rows
    first_col = columns.half(me, row_partner, col_partner) * half_cols
    for row in range(half_rows):
        place, _ = packed_place(
            slots, first_row, first_col, half_rows, half_cols, block_cols, step * half_rows + row
        )
        packed[place] = block[row * width : (row + 1) * width]

    @pl.when(step == half_cols - 1)
    def _():
        count = outs[0].shape[0]
        outs[0][...] = packed[:count]
        for index, out in enumerate(outs[1:]):
            out[...] = packed[count + index]
        keeps = (me[1] > col_partner[me[0], me[1]]).astype(jnp.int32)
        mate_row = half_of(False, me, row_partner) * half_rows
        quarter = half_rows, half_cols, block_cols
        most = jnp.maximum(
            quarter_live(slots, first_row, first_col, *quarter),
            quarter_live(mate_slots, mate_row, keeps * half_cols, *quarter),
        )
        choice = jnp.clip(most - count, 0, len(outs) - 1)
        branch[0] = ((me[0] ^ row_partner[me[0], me[1]]) - 1) * len(outs) + choice


def right_products(kind, tables, w, shards, half_rows, block_cols):
    _, _, height, tile_order = w.shape
    columns = Columns(kind, block_cols)
    half_cols = columns.half_cols
    width = shards[0][0].shape[1]
    blocks = half_rows * half_cols

    whole = pl.BlockSpec(memory_space=pltpu.VMEM)
    scratch = [pltpu.VMEM((block_cols * tile_order, width), BF16)] * 2
    if kind == Columns.REST:
        most = packed_first(blocks)
        shapes = [(most, width, width)] + [(width, width)] * (blocks - most)
        out_specs = [pl.BlockSpec(memory_space=pltpu.SMEM)]
        out_specs += [pl.BlockSpec(shape, lambda i, *_, n=len(shape): (0,) * n) for shape in shapes]
        scratch = [pltpu.VMEM((blocks, width, width), F32)] + scratch
    elif kind == Columns.KEPT_REST:
        shapes = [(height, columns.steps * width)]
        out_specs = [pl.BlockSpec((height, width), lambda i, *_: (0, i))]
    else:
        shapes = [(height, width)] * columns.steps
        out_specs = [pl.BlockSpec((height, width), lambda i, *_: (0, 0))] * columns.steps
    out_shape = [jax.ShapeDtypeStruct(shape, F32) for shape in shapes]
    if kind == Columns.REST:
        out_shape = [jax.ShapeDtypeStruct((1,), jnp.int32)] + out_shape
    return pl.pallas_call(
        functools.partial(
            right_kernel, columns, block_cols, half_rows, [shard[1:] for shard in shards]
        ),
        grid_spec=pltpu.PrefetchScalarGridSpec(
            num_scalar_prefetch=5,
            grid=(columns.steps,),
            in_specs=[whole] * (1 + len(shards)),
            out_specs=out_specs,
            scratch_shapes=scratch,
        ),
        out_shape=out_shape,
        compiler_params=PARAMS,
        cost_estimate=cost(6 * columns.steps * height * width * tile_order),
        name="right_products",
    )(*tables, w, *[shard[0] for shard in shards])


def comes_from(which, me, col_partner):
    distance = me[1] ^ col_partner[me[0], me[1]]
    core = rem(distance, 2) == 1
    return core if which == 0 else jnp.logical_not(core) & (div(distance, 2) == which - 1)


def sum_kernel(half_rows, block_cols, singles, sections, *refs):
    me, _, mate_slots, row_partner, col_partner, kept_ref, packed_ref = refs[:7]
    single_refs, section_refs, out = refs[7 : 7 + singles], refs[7 + singles : -1], refs[-1]
    half_cols = block_cols // 2
    step = pl.program_id(0)
    keeps = (me[1] > col_partner[me[0], me[1]]).astype(jnp.int32)
    first_row = half_of(False, me, row_partner) * half_rows
    place, live = packed_place(
        mate_slots, first_row, keeps * half_cols, half_rows, half_cols, block_cols, step
    )
    count = packed_ref.shape[0]
    at = 0
    for index, kind in enumerate(sections):
        for which in range(kind):
            section = section_refs[at + which]
            wanted = div(step, half_rows) == index
            if kind > 1:
                wanted &= comes_from(which, me, col_partner)

            @pl.when(wanted)
            def _():
                out[...] = kept_ref[...] + section[...].reshape(out.shape)

        at += kind

    @pl.when(live & (place < count))
    def _():
        out[...] += packed_ref[jnp.minimum(place, count - 1)]

    for index, single in enumerate(single_refs):

        @pl.when(live & (place == count + index))
        def _():
            out[...] += single[...]


def sum_blocks(tables, half_rows, block_cols, kept, packed, singles, sections):
    half_cols = block_cols // 2
    height, both = kept.shape
    width = both // half_cols
    block = pl.BlockSpec((width, width), lambda i, *_: (rem(i, half_rows), div(i, half_rows)))

    def section_spec(index, section, which=None):
        def section_at(i, me, slots, mate_slots, row_partner, col_partner):
            here = jnp.clip(i - index * half_rows, 0, half_rows - 1)
            if which is not None:
                here = jnp.where(comes_from(which, me, col_partner), here, 0)
            if section.ndim == 2:
                return here, 0
            return index if which == 0 else col_partner[me[0], me[1]], here, 0

        return pl.BlockSpec((1,) * (section.ndim - 2) + (width, width), section_at)

    return pl.pallas_call(
        functools.partial(
            sum_kernel, half_rows, block_cols, len(singles), [len(each) for each in sections]
        ),
        grid_spec=pltpu.PrefetchScalarGridSpec(
            num_scalar_prefetch=5,
            grid=(half_rows * half_cols,),
            in_specs=[block]
            + [pl.BlockSpec(memory_space=pltpu.VMEM)] * (1 + len(singles))
            + [
                section_spec(index, each, which if len(group) > 1 else None)
                for index, group in enumerate(sections)
                for which, each in enumerate(group)
            ],
            out_specs=block,
        ),
        out_shape=jax.ShapeDtypeStruct((height, both), F32),
        compiler_params=PARAMS,
        name="sum_blocks",
    )(*tables, kept, packed, *singles, *[each for group in sections for each in group])


def wished_kernel(wish, *refs):
    *sections, wanted = refs
    for index, section in enumerate(sections):

        @pl.when((pl.program_id(0) == index // 4) & (wish[0] == index % 4))
        def _():
            wanted[0] = section[...]


def wished(wish, overs):
    height, width = overs[0][0].shape
    steps = 2 if height % 16 == 0 else 1

    def chip_spec(column, chip):
        def chip_at(b, i, wish):
            here = jnp.where(b == column, i, jnp.where(b < column, 0, steps - 1))
            return jnp.where(wish[0] == chip, here, 0), 0

        return pl.BlockSpec((height // steps, width), chip_at)

    return pl.pallas_call(
        wished_kernel,
        grid_spec=pltpu.PrefetchScalarGridSpec(
            num_scalar_prefetch=1,
            grid=(len(overs), steps),
            in_specs=[chip_spec(b, chip) for b in range(len(overs)) for chip in range(4)],
            out_specs=pl.BlockSpec((1, height // steps, width), lambda b, i, _: (b, i, 0)),
        ),
        out_shape=jax.ShapeDtypeStruct((len(overs), height, width), F32),
        compiler_params=PARAMS,
        cost_estimate=cost(0),
        name="wished",
    )(wish, *[section for over in overs for section in over])


def flip(value, axis, size, mask):
    return lax.ppermute(value, axis, [(i, i ^ mask) for i in range(size)])


def first_prolong(shard, axis, size):
    if size != 4:
        return None
    by_two, by_one = flip(shard, axis, size, 2), flip(shard, axis, size, 1)
    return [by_two, by_one, lax.ppermute(shard, axis, [(1, 2), (2, 1)])]


def gather_prolong(shard, near, axis, size):
    depth = shard.shape[0]
    if near is None:
        gathered = lax.all_gather(shard, axis)
        return [(gathered[i], lambda me, i=i: jnp.int32(i * depth), None) for i in range(size)]
    by_two, by_one, middle = near
    handed = lax.ppermute(by_two, axis, [(1, 0), (2, 3)])

    def at(mask):
        return lambda me: (me[0] ^ mask) * depth

    def inner(me):
        return (me[0] == 1) | (me[0] == 2)

    return [
        (shard, at(0), None),
        (by_one, at(1), None),
        (by_two, at(2), None),
        (middle, at(3), inner),
        (handed, at(3), lambda me: jnp.logical_not(inner(me))),
    ]


def gather_restrict(shard, near, slots, axis, size):
    over_x = flip(shard, axis, size, 2)
    over_y = flip(shard, axis, size, 4)
    over_x, slots = lax.optimization_barrier((over_x, slots))
    pieces = [shard, over_x, over_y, flip(over_x, axis, size, 4)]
    if near is not None:
        pieces, near[:2] = lax.optimization_barrier((pieces, near[:2]))
    mine = jnp.stack(pieces)
    return [mine, flip(mine, axis, size, 1)], slots


def pair_switch(index, size, branch, operand, choices=1):
    branches = [
        functools.partial(branch, mask, choice) for mask in range(1, size) for choice in range(choices)
    ]
    return lax.switch(index[0], branches, operand)


def solution(mesh):
    n_row = mesh.shape["row"]
    n_col = mesh.shape["col"]

    def body(tiles, coords, counts, restrict, prolong, row_partner, col_partner):
        tile_order = tiles.shape[1]
        block_rows = restrict.shape[0] * n_col // tile_order
        block_cols = prolong.shape[0] * n_row // tile_order
        half_rows, half_cols = block_rows // 2, block_cols // 2
        row = lax.axis_index("row").astype(jnp.int32)
        col = lax.axis_index("col").astype(jnp.int32)
        me = jnp.stack([row, col])

        row_partner, coords = row_partner.T, coords.T
        places = block_rows * block_cols
        slots, first, wish = make_tables(
            me, row_partner, col_partner, coords, counts, places, block_cols
        )
        near = first_prolong(prolong, "row", n_row)
        by_chip = n_col == 8 and block_rows == 4 and tile_order == 2 * restrict.shape[0]
        if by_chip:
            q_pieces, slots = gather_restrict(restrict, near, slots, "col", n_col)
        else:
            q_pieces = [lax.all_gather(restrict, "col", axis=0, tiled=True)]

        shards = gather_prolong(prolong, near, "row", n_row)

        def products(kind, mate_slots):
            tables = (me, slots, row_partner, col_partner)
            w = left_products(kind, tables, tiles, q_pieces, half_rows, block_cols)
            tables = (me, slots, mate_slots, row_partner, col_partner)
            return right_products(kind, tables, w, shards, half_rows, block_cols)

        def swap_first(mask, _, chunk):
            received = flip(chunk, "row", n_row, mask), flip(slots, "row", n_row, mask)
            return *received, products(Columns.NEXT, slots), products(Columns.KEPT_ON, slots)

        def swap_next(mask, _, operands):
            chunk, mate_slots = operands
            return flip(chunk, "row", n_row, mask), products(Columns.REST, mate_slots)

        def swap_more(mask, _, operands):
            return flip(operands[0], "row", n_row, mask), operands[1:]

        def swap_rest(mask, extra, rest):
            received = [
                flip(array, "row", n_row, mask) if index <= extra else array
                for index, array in enumerate(rest)
            ]
            return received, products(Columns.KEPT_REST, slots)

        given = products(Columns.FIRST, slots)
        received, mate_slots, others, kept = pair_switch(first, n_row, swap_first, given[0])
        given = [*given, *others]
        sections, rest = [], None
        for index in range(half_cols):
            section = kept[index] + received
            if n_col == 8:
                over = [section] + [flip(section, "col", n_col, 2 * chip) for chip in range(1, 4)]
            else:
                over = [lax.all_gather(section, "col")]
            sections.append(over)
            if index + 1 == half_cols:
                break
            chunk, section = lax.optimization_barrier((given[index + 1], section))
            if index == 0:
                received, rest = pair_switch(first, n_row, swap_next, (chunk, mate_slots))
            else:
                received, *_ = pair_switch(first, n_row, swap_more, (chunk,))
            sections[index], received = lax.optimization_barrier((sections[index], received))
        if rest is None:
            rest = products(Columns.REST, mate_slots)
        second, *rest = rest
        rest, section = lax.optimization_barrier((rest, section))
        rest, (stays,) = pair_switch(second, n_row, swap_rest, rest, len(rest))
        if n_col == 8:
            sections[-1], rest = lax.optimization_barrier((sections[-1], rest))
            handed = flip(wished(wish, sections), "col", n_col, 1)
            sections = [[handed] + over for over in sections]
        packed, *singles = rest
        tables = (me, slots, mate_slots, row_partner, col_partner)
        return sum_blocks(tables, half_rows, block_cols, stays, packed, singles, sections)

    in_specs = (
        P(("row", "col"), None, None),
        P(("row", "col"), None),
        P(("row", "col")),
        P(("row", "col"), None),
        P(("col", "row"), None),
        P(),
        P(),
    )
    return jax.shard_map(
        body, mesh=mesh, in_specs=in_specs, out_specs=P("row", "col"), check_vma=False
    )
```

```python
import functools

import jax
import jax.numpy as jnp
from jax import lax
from jax.experimental import pallas as pl
from jax.experimental.pallas import tpu as pltpu
from jax.sharding import PartitionSpec as P

F32 = jnp.float32
BF16 = jnp.bfloat16
VMEM_BYTES = 48 * 1024 * 1024
PARAMS = pltpu.CompilerParams(vmem_limit_bytes=VMEM_BYTES)


def cost(flops):
    return pl.CostEstimate(flops=flops, bytes_accessed=0, transcendentals=0)


def split(value):
    high = value.astype(BF16)
    low = (value - high.astype(F32)).astype(BF16)
    return high, low


def dot(left, right):
    return jnp.dot(left, right, preferred_element_type=F32)


def product(left_both, right_high, right_low):
    half = left_both.shape[0] // 2
    total = dot(left_both[half:], right_high)
    total = total + dot(left_both[:half], right_low)
    return total + dot(left_both[:half], right_high)


def div(value, by):
    return lax.div(value, jnp.int32(by))


def rem(value, by):
    return lax.rem(value, jnp.int32(by))


def half_of(given, me, row_partner):
    mate = row_partner[me[0], me[1]]
    return ((mate > me[0]) if given else (me[0] > mate)).astype(jnp.int32)


def tables_kernel(block_cols, me, row_partner, col_partner, coords, counts, slots, first, wish):
    for place in range(slots.shape[0]):
        slots[place] = jnp.int32(-1)
    for slot in range(coords.shape[1]):

        @pl.when(slot < counts[0])
        def _():
            slots[coords[0, slot] * block_cols + coords[1, slot]] = jnp.int32(slot)

    first[0] = (me[0] ^ row_partner[me[0], me[1]]) - 1
    other = me[1] ^ 1
    wish[0] = div(other ^ col_partner[me[0], other], 2)


def make_tables(me, row_partner, col_partner, coords, counts, places, block_cols):
    smem = pl.BlockSpec(memory_space=pltpu.SMEM)
    return pl.pallas_call(
        functools.partial(tables_kernel, block_cols),
        in_specs=[smem] * 5,
        out_specs=[smem] * 3,
        out_shape=[jax.ShapeDtypeStruct((n,), jnp.int32) for n in (places, 1, 1)],
        cost_estimate=cost(0),
        name="make_tables",
    )(me, row_partner, col_partner, coords, counts)


class Columns:
    FIRST, NEXT, REST, KEPT = range(4)

    def __init__(self, kind, block_cols):
        self.kind = kind
        self.given = kind != self.KEPT
        self.half_cols = block_cols // 2
        self.skip = 1 if kind == self.NEXT else 0
        self.steps = 1 if kind == self.FIRST else self.half_cols - self.skip
        if kind == self.KEPT:
            self.steps = block_cols

    def half(self, step, me, row_partner, col_partner):
        holder = row_partner[me[0], me[1]] if self.given else me[0]
        goes_on = (me[1] < col_partner[holder, me[1]]).astype(jnp.int32)
        if self.kind == self.KEPT:
            return goes_on ^ div(step, self.half_cols)
        return goes_on ^ (1 if self.kind == self.REST else 0)

    def column(self, step, me, row_partner, col_partner):
        half = self.half(step, me, row_partner, col_partner)
        return half * self.half_cols + self.skip + rem(step, self.half_cols)


def left_kernel(columns, block_cols, half_rows, per_step, *refs):
    me, slots, row_partner, col_partner = refs[:4]
    tile_refs, q_refs, out, q_both = refs[4 : 4 + per_step], refs[4 + per_step : -2], refs[-2], refs[-1]
    group, step = pl.program_id(0), pl.program_id(1)
    width = q_both.shape[0] // 2

    block_row = half_of(columns.given, me, row_partner) * half_rows + group

    def put(value, first):
        high, low = split(value.T)
        q_both[:width, first : first + value.shape[0]] = high
        q_both[width:, first : first + value.shape[0]] = low

    if len(q_refs) == 1:

        @pl.when(step == 0)
        def _():
            put(q_refs[0][...], 0)

    else:
        distance = block_row ^ div(me[1], 2)
        for core in range(2):

            @pl.when((step == 0) & (rem(me[1], 2) == core))
            def _():
                depth = q_refs[0].shape[1]
                put(q_refs[0][distance], core * depth)
                put(q_refs[1][distance], (1 - core) * depth)

    for index, tile_ref in enumerate(tile_refs):
        column = columns.column(step * per_step + index, me, row_partner, col_partner)
        live = slots[block_row * block_cols + column] >= 0
        high, low = split(tile_ref[0])
        total = jnp.where(live, product(q_both[...], high, low), 0.0)
        out[index, 0], out[index, 1] = split(total)


def left_products(kind, tables, tiles, q_pieces, half_rows, block_cols):
    _, tile_order, _ = tiles.shape
    width = q_pieces[0].shape[-1]
    columns = Columns(kind, block_cols)
    per_step = 2 if columns.steps % 2 == 0 else 1

    def row_of(g, me, row_partner):
        return half_of(columns.given, me, row_partner) * half_rows + g

    def tile_spec(index):
        def tile_at(g, b, me, slots, row_partner, col_partner):
            column = columns.column(b * per_step + index, me, row_partner, col_partner)
            return jnp.maximum(slots[row_of(g, me, row_partner) * block_cols + column], 0), 0, 0

        return pl.BlockSpec((1, tile_order, tile_order), tile_at)

    if len(q_pieces) == 1:
        q_specs = [
            pl.BlockSpec(
                (tile_order, width),
                lambda g, b, me, slots, row_partner, _: (row_of(g, me, row_partner), 0),
            )
        ]
    else:
        q_specs = [pl.BlockSpec(memory_space=pltpu.VMEM)] * len(q_pieces)
    return pl.pallas_call(
        functools.partial(left_kernel, columns, block_cols, half_rows, per_step),
        grid_spec=pltpu.PrefetchScalarGridSpec(
            num_scalar_prefetch=4,
            grid=(half_rows, columns.steps // per_step),
            in_specs=[tile_spec(index) for index in range(per_step)] + q_specs,
            out_specs=pl.BlockSpec(
                (per_step, 2, width, tile_order), lambda g, b, *_: (b, 0, g, 0)
            ),
            scratch_shapes=[pltpu.VMEM((2 * width, tile_order), BF16)],
        ),
        out_shape=jax.ShapeDtypeStruct((columns.steps, 2, half_rows * width, tile_order), BF16),
        compiler_params=PARAMS,
        cost_estimate=cost(12 * half_rows * columns.steps * width * tile_order * tile_order),
        name="left_products",
    )(*tables, *[tiles] * per_step, *q_pieces)


def packed_first(blocks):
    return max(1, blocks * 3 // 4)


def packed_place(slots, first_row, first_col, half_rows, half_cols, block_cols, block):
    before = here = count = jnp.int32(0)
    for index in range(half_rows * half_cols):
        place = (first_row + index % half_rows) * block_cols + first_col + index // half_rows
        flag = (slots[place] >= 0).astype(jnp.int32)
        before = before + jnp.where(index < block, flag, 0)
        here = here + jnp.where(index == block, flag, 0)
        count = count + flag
    return jnp.where(here == 1, before, count + block - before), here == 1


def quarter_live(table, first_row, first_col, half_rows, half_cols, block_cols):
    count = jnp.int32(0)
    for index in range(half_rows * half_cols):
        place = (first_row + index % half_rows) * block_cols + first_col + index // half_rows
        count = count + (table[place] >= 0).astype(jnp.int32)
    return count


def right_kernel(columns, block_cols, half_rows, starts, *refs):
    me, slots, mate_slots, row_partner, col_partner, w_ref = refs[:6]
    pieces = refs[6 : 6 + len(starts)]
    step = pl.program_id(0)
    tile_order = w_ref.shape[3]
    width = pieces[0].shape[1]
    packs = columns.kind == Columns.REST
    outs = refs[6 + len(starts) : -3 if packs else -2]
    p_high, p_low = refs[-2:]

    @pl.when(step == 0)
    def _():
        low = columns.column(0, me, row_partner, col_partner) * tile_order
        for (start, filled), piece in zip(starts, pieces):
            begin = start(me)
            wanted = begin >= 0
            if columns.given:
                wanted = (begin < low + columns.steps * tile_order) & (begin + piece.shape[0] > low)
            if filled is not None:
                wanted &= filled(me)

            @pl.when(wanted)
            def _():
                depth = piece.shape[0]
                rows = pl.ds(pl.multiple_of(begin, depth), depth)
                p_high[rows, :], p_low[rows, :] = split(piece[...])

    column = columns.column(step, me, row_partner, col_partner)
    rows = pl.ds(pl.multiple_of(column * tile_order, tile_order), tile_order)
    both = w_ref[step if columns.given else 0].reshape(2 * w_ref.shape[2], tile_order)
    block = product(both, p_high[rows, :], p_low[rows, :])
    half_cols = columns.half_cols
    if not packs:
        for index, out in enumerate(outs):

            @pl.when(jnp.minimum(step, half_cols) == index)
            def _():
                out[...] = block

        return
    branch, *outs = outs
    packed = refs[-3]
    first_row = half_of(True, me, row_partner) * half_rows
    first_col = columns.half(step, me, row_partner, col_partner) * half_cols
    for row in range(half_rows):
        place, _ = packed_place(
            slots, first_row, first_col, half_rows, half_cols, block_cols, step * half_rows + row
        )
        packed[place] = block[row * width : (row + 1) * width]

    @pl.when(step == half_cols - 1)
    def _():
        count = outs[0].shape[0]
        outs[0][...] = packed[:count]
        for index, out in enumerate(outs[1:]):
            out[...] = packed[count + index]
        keeps = (me[1] > col_partner[me[0], me[1]]).astype(jnp.int32)
        mate_row = half_of(False, me, row_partner) * half_rows
        quarter = half_rows, half_cols, block_cols
        most = jnp.maximum(
            quarter_live(slots, first_row, first_col, *quarter),
            quarter_live(mate_slots, mate_row, keeps * half_cols, *quarter),
        )
        choice = jnp.clip(most - count, 0, len(outs) - 1)
        branch[0] = ((me[0] ^ row_partner[me[0], me[1]]) - 1) * len(outs) + choice


def right_products(kind, tables, w, shards, half_rows, block_cols):
    _, _, height, tile_order = w.shape
    columns = Columns(kind, block_cols)
    half_cols = columns.half_cols
    width = shards[0][0].shape[1]
    blocks = half_rows * half_cols

    whole = pl.BlockSpec(memory_space=pltpu.VMEM)
    one_column = pl.BlockSpec((1, 2, height, tile_order), lambda i, *_: (i, 0, 0, 0))
    scratch = [pltpu.VMEM((block_cols * tile_order, width), BF16)] * 2
    if kind == Columns.REST:
        most = packed_first(blocks)
        shapes = [(most, width, width)] + [(width, width)] * (blocks - most)
        out_specs = [pl.BlockSpec(memory_space=pltpu.SMEM)]
        out_specs += [pl.BlockSpec(shape, lambda i, *_, n=len(shape): (0,) * n) for shape in shapes]
        scratch = [pltpu.VMEM((blocks, width, width), F32)] + scratch
    else:
        count = min(columns.steps, half_cols)
        shapes = [(height, width)] * count
        out_specs = [pl.BlockSpec((height, width), lambda i, *_: (0, 0))] * count
        if kind == Columns.KEPT:
            shapes += [(height, half_cols * width)]
            out_specs += [
                pl.BlockSpec((height, width), lambda i, *_: (0, jnp.maximum(i - half_cols, 0)))
            ]
    out_shape = [jax.ShapeDtypeStruct(shape, F32) for shape in shapes]
    if kind == Columns.REST:
        out_shape = [jax.ShapeDtypeStruct((1,), jnp.int32)] + out_shape
    return pl.pallas_call(
        functools.partial(
            right_kernel, columns, block_cols, half_rows, [shard[1:] for shard in shards]
        ),
        grid_spec=pltpu.PrefetchScalarGridSpec(
            num_scalar_prefetch=5,
            grid=(columns.steps,),
            in_specs=[whole if columns.given else one_column] + [whole] * len(shards),
            out_specs=out_specs,
            scratch_shapes=scratch,
        ),
        out_shape=out_shape,
        compiler_params=PARAMS,
        cost_estimate=cost(6 * columns.steps * height * width * tile_order),
        name="right_products",
    )(*tables, w, *[shard[0] for shard in shards])


def comes_from(which, me, col_partner):
    distance = me[1] ^ col_partner[me[0], me[1]]
    core = rem(distance, 2) == 1
    return core if which == 0 else jnp.logical_not(core) & (div(distance, 2) == which - 1)


def sum_kernel(half_rows, block_cols, singles, sections, *refs):
    me, _, mate_slots, row_partner, col_partner, kept_ref, packed_ref = refs[:7]
    single_refs, section_refs, out = refs[7 : 7 + singles], refs[7 + singles : -1], refs[-1]
    half_cols = block_cols // 2
    step = pl.program_id(0)
    keeps = (me[1] > col_partner[me[0], me[1]]).astype(jnp.int32)
    first_row = half_of(False, me, row_partner) * half_rows
    place, live = packed_place(
        mate_slots, first_row, keeps * half_cols, half_rows, half_cols, block_cols, step
    )
    count = packed_ref.shape[0]
    at = 0
    for index, kind in enumerate(sections):
        for which in range(kind):
            section = section_refs[at + which]
            wanted = div(step, half_rows) == index
            if kind > 1:
                wanted &= comes_from(which, me, col_partner)

            @pl.when(wanted)
            def _():
                out[...] = kept_ref[...] + section[...].reshape(out.shape)

        at += kind

    @pl.when(live & (place < count))
    def _():
        out[...] += packed_ref[jnp.minimum(place, count - 1)]

    for index, single in enumerate(single_refs):

        @pl.when(live & (place == count + index))
        def _():
            out[...] += single[...]


def sum_blocks(tables, half_rows, block_cols, kept, packed, singles, sections):
    half_cols = block_cols // 2
    height, both = kept.shape
    width = both // half_cols
    block = pl.BlockSpec((width, width), lambda i, *_: (rem(i, half_rows), div(i, half_rows)))

    def section_spec(index, section, which=None):
        def section_at(i, me, slots, mate_slots, row_partner, col_partner):
            here = jnp.clip(i - index * half_rows, 0, half_rows - 1)
            if which is not None:
                here = jnp.where(comes_from(which, me, col_partner), here, 0)
            if section.ndim == 2:
                return here, 0
            return index if which == 0 else col_partner[me[0], me[1]], here, 0

        return pl.BlockSpec((1,) * (section.ndim - 2) + (width, width), section_at)

    return pl.pallas_call(
        functools.partial(
            sum_kernel, half_rows, block_cols, len(singles), [len(each) for each in sections]
        ),
        grid_spec=pltpu.PrefetchScalarGridSpec(
            num_scalar_prefetch=5,
            grid=(half_rows * half_cols,),
            in_specs=[block]
            + [pl.BlockSpec(memory_space=pltpu.VMEM)] * (1 + len(singles))
            + [
                section_spec(index, each, which if len(group) > 1 else None)
                for index, group in enumerate(sections)
                for which, each in enumerate(group)
            ],
            out_specs=block,
        ),
        out_shape=jax.ShapeDtypeStruct((height, both), F32),
        compiler_params=PARAMS,
        name="sum_blocks",
    )(*tables, kept, packed, *singles, *[each for group in sections for each in group])


def wished_kernel(wish, *refs):
    *sections, wanted = refs
    for index, section in enumerate(sections):

        @pl.when((pl.program_id(0) == index // 4) & (wish[0] == index % 4))
        def _():
            wanted[0] = section[...]


def wished(wish, overs):
    height, width = overs[0][0].shape
    steps = 2 if height % 16 == 0 else 1

    def chip_spec(column, chip):
        def chip_at(b, i, wish):
            here = jnp.where(b == column, i, jnp.where(b < column, 0, steps - 1))
            return jnp.where(wish[0] == chip, here, 0), 0

        return pl.BlockSpec((height // steps, width), chip_at)

    return pl.pallas_call(
        wished_kernel,
        grid_spec=pltpu.PrefetchScalarGridSpec(
            num_scalar_prefetch=1,
            grid=(len(overs), steps),
            in_specs=[chip_spec(b, chip) for b in range(len(overs)) for chip in range(4)],
            out_specs=pl.BlockSpec((1, height // steps, width), lambda b, i, _: (b, i, 0)),
        ),
        out_shape=jax.ShapeDtypeStruct((len(overs), height, width), F32),
        compiler_params=PARAMS,
        cost_estimate=cost(0),
        name="wished",
    )(wish, *[section for over in overs for section in over])


def flip(value, axis, size, mask):
    return lax.ppermute(value, axis, [(i, i ^ mask) for i in range(size)])


def first_prolong(shard, axis, size):
    if size != 4:
        return None
    by_two, by_one = flip(shard, axis, size, 2), flip(shard, axis, size, 1)
    return [by_two, by_one, lax.ppermute(shard, axis, [(1, 2), (2, 1)])]


def gather_prolong(shard, near, axis, size):
    depth = shard.shape[0]
    if near is None:
        gathered = lax.all_gather(shard, axis)
        return [(gathered[i], lambda me, i=i: jnp.int32(i * depth), None) for i in range(size)]
    by_two, by_one, middle = near
    handed = lax.ppermute(by_two, axis, [(1, 0), (2, 3)])

    def at(mask):
        return lambda me: (me[0] ^ mask) * depth

    def inner(me):
        return (me[0] == 1) | (me[0] == 2)

    return [
        (shard, at(0), None),
        (by_one, at(1), None),
        (by_two, at(2), None),
        (middle, at(3), inner),
        (handed, at(3), lambda me: jnp.logical_not(inner(me))),
    ]


def gather_restrict(shard, near, slots, axis, size):
    over_x = flip(shard, axis, size, 2)
    over_y = flip(shard, axis, size, 4)
    over_x, slots = lax.optimization_barrier((over_x, slots))
    pieces = [shard, over_x, over_y, flip(over_x, axis, size, 4)]
    if near is not None:
        pieces, near[:2] = lax.optimization_barrier((pieces, near[:2]))
    mine = jnp.stack(pieces)
    return [mine, flip(mine, axis, size, 1)], slots


def pair_switch(index, size, branch, operand, choices=1):
    branches = [
        functools.partial(branch, mask, choice) for mask in range(1, size) for choice in range(choices)
    ]
    return lax.switch(index[0], branches, operand)


def solution(mesh):
    n_row = mesh.shape["row"]
    n_col = mesh.shape["col"]

    def body(tiles, coords, counts, restrict, prolong, row_partner, col_partner):
        tile_order = tiles.shape[1]
        block_rows = restrict.shape[0] * n_col // tile_order
        block_cols = prolong.shape[0] * n_row // tile_order
        half_rows, half_cols = block_rows // 2, block_cols // 2
        row = lax.axis_index("row").astype(jnp.int32)
        col = lax.axis_index("col").astype(jnp.int32)
        me = jnp.stack([row, col])

        row_partner, coords = row_partner.T, coords.T
        places = block_rows * block_cols
        slots, first, wish = make_tables(
            me, row_partner, col_partner, coords, counts, places, block_cols
        )
        near = first_prolong(prolong, "row", n_row)
        by_chip = n_col == 8 and block_rows == 4 and tile_order == 2 * restrict.shape[0]
        if by_chip:
            q_pieces, slots = gather_restrict(restrict, near, slots, "col", n_col)
        else:
            q_pieces = [lax.all_gather(restrict, "col", axis=0, tiled=True)]

        shards = gather_prolong(prolong, near, "row", n_row)

        def products(kind, mate_slots):
            tables = (me, slots, row_partner, col_partner)
            w = left_products(kind, tables, tiles, q_pieces, half_rows, block_cols)
            tables = (me, slots, mate_slots, row_partner, col_partner)
            return right_products(kind, tables, w, shards, half_rows, block_cols)

        def swap_first(mask, _, chunk):
            received = flip(chunk, "row", n_row, mask), flip(slots, "row", n_row, mask)
            return *received, products(Columns.NEXT, slots), products(Columns.KEPT, slots)

        def swap_next(mask, _, operands):
            chunk, mate_slots = operands
            return flip(chunk, "row", n_row, mask), products(Columns.REST, mate_slots)

        def swap_more(mask, _, operands):
            return flip(operands[0], "row", n_row, mask), operands[1:]

        def swap_rest(mask, extra, rest):
            return [
                flip(array, "row", n_row, mask) if index <= extra else array
                for index, array in enumerate(rest)
            ]

        given = products(Columns.FIRST, slots)
        received, mate_slots, others, kept = pair_switch(first, n_row, swap_first, given[0])
        given = [*given, *others]
        sections, rest = [], None
        for index in range(half_cols):
            section = kept[index] + received
            if n_col == 8:
                over = [section] + [flip(section, "col", n_col, 2 * chip) for chip in range(1, 4)]
            else:
                over = [lax.all_gather(section, "col")]
            sections.append(over)
            if index + 1 == half_cols:
                break
            chunk, section = lax.optimization_barrier((given[index + 1], section))
            if index == 0:
                received, rest = pair_switch(first, n_row, swap_next, (chunk, mate_slots))
            else:
                received, *_ = pair_switch(first, n_row, swap_more, (chunk,))
            sections[index], received = lax.optimization_barrier((sections[index], received))
        if rest is None:
            rest = products(Columns.REST, mate_slots)
        second, *rest = rest
        rest, section = lax.optimization_barrier((rest, section))
        rest = pair_switch(second, n_row, swap_rest, rest, len(rest))
        if n_col == 8:
            sections[-1], rest = lax.optimization_barrier((sections[-1], rest))
            handed = flip(wished(wish, sections), "col", n_col, 1)
            sections = [[handed] + over for over in sections]
        packed, *singles = rest
        tables = (me, slots, mate_slots, row_partner, col_partner)
        return sum_blocks(tables, half_rows, block_cols, kept[-1], packed, singles, sections)

    in_specs = (
        P(("row", "col"), None, None),
        P(("row", "col"), None),
        P(("row", "col")),
        P(("row", "col"), None),
        P(("col", "row"), None),
        P(),
        P(),
    )
    return jax.shard_map(
        body, mesh=mesh, in_specs=in_specs, out_specs=P("row", "col"), check_vma=False
    )
```

```python
import functools

import jax
import jax.numpy as jnp
from jax import lax
from jax.experimental import pallas as pl
from jax.experimental.pallas import tpu as pltpu
from jax.sharding import PartitionSpec as P

F32 = jnp.float32
BF16 = jnp.bfloat16
VMEM_BYTES = 48 * 1024 * 1024
PARAMS = pltpu.CompilerParams(vmem_limit_bytes=VMEM_BYTES)


def cost(flops):
    return pl.CostEstimate(flops=flops, bytes_accessed=0, transcendentals=0)


def split(value):
    high = value.astype(BF16)
    low = (value - high.astype(F32)).astype(BF16)
    return high, low


def dot(left, right):
    return jnp.dot(left, right, preferred_element_type=F32)


def product(left_both, right_high, right_low):
    half = left_both.shape[0] // 2
    total = dot(left_both[half:], right_high)
    total = total + dot(left_both[:half], right_low)
    return total + dot(left_both[:half], right_high)


def div(value, by):
    return lax.div(value, jnp.int32(by))


def rem(value, by):
    return lax.rem(value, jnp.int32(by))


def half_of(given, me, row_partner):
    mate = row_partner[me[0], me[1]]
    return ((mate > me[0]) if given else (me[0] > mate)).astype(jnp.int32)


def tables_kernel(block_cols, me, row_partner, col_partner, coords, counts, slots, first, wish):
    for place in range(slots.shape[0]):
        slots[place] = jnp.int32(-1)
    for slot in range(coords.shape[1]):

        @pl.when(slot < counts[0])
        def _():
            slots[coords[0, slot] * block_cols + coords[1, slot]] = jnp.int32(slot)

    first[0] = (me[0] ^ row_partner[me[0], me[1]]) - 1
    other = me[1] ^ 1
    wish[0] = div(other ^ col_partner[me[0], other], 2)


def make_tables(me, row_partner, col_partner, coords, counts, places, block_cols):
    smem = pl.BlockSpec(memory_space=pltpu.SMEM)
    return pl.pallas_call(
        functools.partial(tables_kernel, block_cols),
        in_specs=[smem] * 5,
        out_specs=[smem] * 3,
        out_shape=[jax.ShapeDtypeStruct((n,), jnp.int32) for n in (places, 1, 1)],
        cost_estimate=cost(0),
        name="make_tables",
    )(me, row_partner, col_partner, coords, counts)


class Columns:
    FIRST, NEXT, REST, KEPT, ON = range(5)

    def __init__(self, kind, block_cols):
        self.kind = kind
        self.given = kind != self.KEPT
        self.half_cols = block_cols // 2
        self.skip = 1 if kind == self.NEXT else 0
        self.steps = 1 if kind == self.FIRST else self.half_cols - self.skip
        if kind == self.KEPT:
            self.steps = block_cols

    def half(self, step, me, row_partner, col_partner):
        holder = row_partner[me[0], me[1]] if self.given else me[0]
        goes_on = (me[1] < col_partner[holder, me[1]]).astype(jnp.int32)
        if self.kind == self.KEPT:
            return goes_on ^ div(step, self.half_cols)
        return goes_on ^ (1 if self.kind == self.REST else 0)

    def column(self, step, me, row_partner, col_partner):
        half = self.half(step, me, row_partner, col_partner)
        return half * self.half_cols + self.skip + rem(step, self.half_cols)


def left_kernel(columns, block_cols, half_rows, per_step, *refs):
    me, slots, row_partner, col_partner = refs[:4]
    tile_refs, q_refs, out, q_both = refs[4 : 4 + per_step], refs[4 + per_step : -2], refs[-2], refs[-1]
    group, step = pl.program_id(0), pl.program_id(1)
    width = q_both.shape[0] // 2

    block_row = half_of(columns.given, me, row_partner) * half_rows + group

    def put(value, first):
        high, low = split(value.T)
        q_both[:width, first : first + value.shape[0]] = high
        q_both[width:, first : first + value.shape[0]] = low

    if len(q_refs) == 1:

        @pl.when(step == 0)
        def _():
            put(q_refs[0][...], 0)

    else:
        distance = block_row ^ div(me[1], 2)
        for core in range(2):

            @pl.when((step == 0) & (rem(me[1], 2) == core))
            def _():
                depth = q_refs[0].shape[1]
                put(q_refs[0][distance], core * depth)
                put(q_refs[1][distance], (1 - core) * depth)

    for index, tile_ref in enumerate(tile_refs):
        column = columns.column(step * per_step + index, me, row_partner, col_partner)
        live = slots[block_row * block_cols + column] >= 0
        high, low = split(tile_ref[0])
        total = jnp.where(live, product(q_both[...], high, low), 0.0)
        out[index, 0], out[index, 1] = split(total)


def left_products(kind, tables, tiles, q_pieces, half_rows, block_cols):
    _, tile_order, _ = tiles.shape
    width = q_pieces[0].shape[-1]
    columns = Columns(kind, block_cols)
    per_step = 2 if columns.steps % 2 == 0 else 1

    def row_of(g, me, row_partner):
        return half_of(columns.given, me, row_partner) * half_rows + g

    def tile_spec(index):
        def tile_at(g, b, me, slots, row_partner, col_partner):
            column = columns.column(b * per_step + index, me, row_partner, col_partner)
            return jnp.maximum(slots[row_of(g, me, row_partner) * block_cols + column], 0), 0, 0

        return pl.BlockSpec((1, tile_order, tile_order), tile_at)

    if len(q_pieces) == 1:
        q_specs = [
            pl.BlockSpec(
                (tile_order, width),
                lambda g, b, me, slots, row_partner, _: (row_of(g, me, row_partner), 0),
            )
        ]
    else:
        q_specs = [pl.BlockSpec(memory_space=pltpu.VMEM)] * len(q_pieces)
    return pl.pallas_call(
        functools.partial(left_kernel, columns, block_cols, half_rows, per_step),
        grid_spec=pltpu.PrefetchScalarGridSpec(
            num_scalar_prefetch=4,
            grid=(half_rows, columns.steps // per_step),
            in_specs=[tile_spec(index) for index in range(per_step)] + q_specs,
            out_specs=pl.BlockSpec(
                (per_step, 2, width, tile_order), lambda g, b, *_: (b, 0, g, 0)
            ),
            scratch_shapes=[pltpu.VMEM((2 * width, tile_order), BF16)],
        ),
        out_shape=jax.ShapeDtypeStruct((columns.steps, 2, half_rows * width, tile_order), BF16),
        compiler_params=PARAMS,
        cost_estimate=cost(12 * half_rows * columns.steps * width * tile_order * tile_order),
        name="left_products",
    )(*tables, *[tiles] * per_step, *q_pieces)


def packed_first(blocks):
    return max(1, blocks * 3 // 4)


def packed_place(slots, first_row, first_col, half_rows, half_cols, block_cols, block):
    before = here = count = jnp.int32(0)
    for index in range(half_rows * half_cols):
        place = (first_row + index % half_rows) * block_cols + first_col + index // half_rows
        flag = (slots[place] >= 0).astype(jnp.int32)
        before = before + jnp.where(index < block, flag, 0)
        here = here + jnp.where(index == block, flag, 0)
        count = count + flag
    return jnp.where(here == 1, before, count + block - before), here == 1


def quarter_live(table, first_row, first_col, half_rows, half_cols, block_cols):
    count = jnp.int32(0)
    for index in range(half_rows * half_cols):
        place = (first_row + index % half_rows) * block_cols + first_col + index // half_rows
        count = count + (table[place] >= 0).astype(jnp.int32)
    return count


def right_kernel(columns, block_cols, half_rows, starts, *refs):
    me, slots, mate_slots, row_partner, col_partner, w_ref = refs[:6]
    pieces = refs[6 : 6 + len(starts)]
    step = pl.program_id(0)
    tile_order = w_ref.shape[3]
    width = pieces[0].shape[1]
    packs = columns.kind == Columns.REST
    outs = refs[6 + len(starts) : -3 if packs else -2]
    p_high, p_low = refs[-2:]

    @pl.when(step == 0)
    def _():
        low = columns.column(0, me, row_partner, col_partner) * tile_order
        for (start, filled), piece in zip(starts, pieces):
            begin = start(me)
            wanted = begin >= 0
            if columns.given:
                wanted = (begin < low + columns.steps * tile_order) & (begin + piece.shape[0] > low)
            if filled is not None:
                wanted &= filled(me)

            @pl.when(wanted)
            def _():
                depth = piece.shape[0]
                rows = pl.ds(pl.multiple_of(begin, depth), depth)
                p_high[rows, :], p_low[rows, :] = split(piece[...])

    column = columns.column(step, me, row_partner, col_partner)
    rows = pl.ds(pl.multiple_of(column * tile_order, tile_order), tile_order)
    both = w_ref[columns.skip + step if columns.given else 0].reshape(2 * w_ref.shape[2], tile_order)
    block = product(both, p_high[rows, :], p_low[rows, :])
    half_cols = columns.half_cols
    if not packs:
        for index, out in enumerate(outs):

            @pl.when(jnp.minimum(step, half_cols) == index)
            def _():
                out[...] = block

        return
    branch, *outs = outs
    packed = refs[-3]
    first_row = half_of(True, me, row_partner) * half_rows
    first_col = columns.half(step, me, row_partner, col_partner) * half_cols
    for row in range(half_rows):
        place, _ = packed_place(
            slots, first_row, first_col, half_rows, half_cols, block_cols, step * half_rows + row
        )
        packed[place] = block[row * width : (row + 1) * width]

    @pl.when(step == half_cols - 1)
    def _():
        count = outs[0].shape[0]
        outs[0][...] = packed[:count]
        for index, out in enumerate(outs[1:]):
            out[...] = packed[count + index]
        keeps = (me[1] > col_partner[me[0], me[1]]).astype(jnp.int32)
        mate_row = half_of(False, me, row_partner) * half_rows
        quarter = half_rows, half_cols, block_cols
        most = jnp.maximum(
            quarter_live(slots, first_row, first_col, *quarter),
            quarter_live(mate_slots, mate_row, keeps * half_cols, *quarter),
        )
        choice = jnp.clip(most - count, 0, len(outs) - 1)
        branch[0] = ((me[0] ^ row_partner[me[0], me[1]]) - 1) * len(outs) + choice


def right_products(kind, tables, w, shards, half_rows, block_cols):
    _, _, height, tile_order = w.shape
    columns = Columns(kind, block_cols)
    half_cols = columns.half_cols
    width = shards[0][0].shape[1]
    blocks = half_rows * half_cols

    whole = pl.BlockSpec(memory_space=pltpu.VMEM)
    one_column = pl.BlockSpec((1, 2, height, tile_order), lambda i, *_: (i, 0, 0, 0))
    scratch = [pltpu.VMEM((block_cols * tile_order, width), BF16)] * 2
    if kind == Columns.REST:
        most = packed_first(blocks)
        shapes = [(most, width, width)] + [(width, width)] * (blocks - most)
        out_specs = [pl.BlockSpec(memory_space=pltpu.SMEM)]
        out_specs += [pl.BlockSpec(shape, lambda i, *_, n=len(shape): (0,) * n) for shape in shapes]
        scratch = [pltpu.VMEM((blocks, width, width), F32)] + scratch
    else:
        count = min(columns.steps, half_cols)
        shapes = [(height, width)] * count
        out_specs = [pl.BlockSpec((height, width), lambda i, *_: (0, 0))] * count
        if kind == Columns.KEPT:
            shapes += [(height, half_cols * width)]
            out_specs += [
                pl.BlockSpec((height, width), lambda i, *_: (0, jnp.maximum(i - half_cols, 0)))
            ]
    out_shape = [jax.ShapeDtypeStruct(shape, F32) for shape in shapes]
    if kind == Columns.REST:
        out_shape = [jax.ShapeDtypeStruct((1,), jnp.int32)] + out_shape
    return pl.pallas_call(
        functools.partial(
            right_kernel, columns, block_cols, half_rows, [shard[1:] for shard in shards]
        ),
        grid_spec=pltpu.PrefetchScalarGridSpec(
            num_scalar_prefetch=5,
            grid=(columns.steps,),
            in_specs=[whole if columns.given else one_column] + [whole] * len(shards),
            out_specs=out_specs,
            scratch_shapes=scratch,
        ),
        out_shape=out_shape,
        compiler_params=PARAMS,
        cost_estimate=cost(6 * columns.steps * height * width * tile_order),
        name="right_products",
    )(*tables, w, *[shard[0] for shard in shards])


def comes_from(which, me, col_partner):
    distance = me[1] ^ col_partner[me[0], me[1]]
    core = rem(distance, 2) == 1
    return core if which == 0 else jnp.logical_not(core) & (div(distance, 2) == which - 1)


def sum_kernel(half_rows, block_cols, singles, sections, *refs):
    me, _, mate_slots, row_partner, col_partner, kept_ref, packed_ref = refs[:7]
    single_refs, section_refs, out = refs[7 : 7 + singles], refs[7 + singles : -1], refs[-1]
    half_cols = block_cols // 2
    step = pl.program_id(0)
    keeps = (me[1] > col_partner[me[0], me[1]]).astype(jnp.int32)
    first_row = half_of(False, me, row_partner) * half_rows
    place, live = packed_place(
        mate_slots, first_row, keeps * half_cols, half_rows, half_cols, block_cols, step
    )
    count = packed_ref.shape[0]
    at = 0
    for index, kind in enumerate(sections):
        for which in range(kind):
            section = section_refs[at + which]
            wanted = div(step, half_rows) == index
            if kind > 1:
                wanted &= comes_from(which, me, col_partner)

            @pl.when(wanted)
            def _():
                out[...] = kept_ref[...] + section[...].reshape(out.shape)

        at += kind

    @pl.when(live & (place < count))
    def _():
        out[...] += packed_ref[jnp.minimum(place, count - 1)]

    for index, single in enumerate(single_refs):

        @pl.when(live & (place == count + index))
        def _():
            out[...] += single[...]


def sum_blocks(tables, half_rows, block_cols, kept, packed, singles, sections):
    half_cols = block_cols // 2
    height, both = kept.shape
    width = both // half_cols
    block = pl.BlockSpec((width, width), lambda i, *_: (rem(i, half_rows), div(i, half_rows)))

    def section_spec(index, section, which=None):
        def section_at(i, me, slots, mate_slots, row_partner, col_partner):
            here = jnp.clip(i - index * half_rows, 0, half_rows - 1)
            if which is not None:
                here = jnp.where(comes_from(which, me, col_partner), here, 0)
            if section.ndim == 2:
                return here, 0
            return index if which == 0 else col_partner[me[0], me[1]], here, 0

        return pl.BlockSpec((1,) * (section.ndim - 2) + (width, width), section_at)

    return pl.pallas_call(
        functools.partial(
            sum_kernel, half_rows, block_cols, len(singles), [len(each) for each in sections]
        ),
        grid_spec=pltpu.PrefetchScalarGridSpec(
            num_scalar_prefetch=5,
            grid=(half_rows * half_cols,),
            in_specs=[block]
            + [pl.BlockSpec(memory_space=pltpu.VMEM)] * (1 + len(singles))
            + [
                section_spec(index, each, which if len(group) > 1 else None)
                for index, group in enumerate(sections)
                for which, each in enumerate(group)
            ],
            out_specs=block,
        ),
        out_shape=jax.ShapeDtypeStruct((height, both), F32),
        compiler_params=PARAMS,
        name="sum_blocks",
    )(*tables, kept, packed, *singles, *[each for group in sections for each in group])


def wished_kernel(wish, *refs):
    *sections, wanted = refs
    for index, section in enumerate(sections):

        @pl.when((pl.program_id(0) == index // 4) & (wish[0] == index % 4))
        def _():
            wanted[0] = section[...]


def wished(wish, overs):
    height, width = overs[0][0].shape
    steps = 2 if height % 16 == 0 else 1

    def chip_spec(column, chip):
        def chip_at(b, i, wish):
            here = jnp.where(b == column, i, jnp.where(b < column, 0, steps - 1))
            return jnp.where(wish[0] == chip, here, 0), 0

        return pl.BlockSpec((height // steps, width), chip_at)

    return pl.pallas_call(
        wished_kernel,
        grid_spec=pltpu.PrefetchScalarGridSpec(
            num_scalar_prefetch=1,
            grid=(len(overs), steps),
            in_specs=[chip_spec(b, chip) for b in range(len(overs)) for chip in range(4)],
            out_specs=pl.BlockSpec((1, height // steps, width), lambda b, i, _: (b, i, 0)),
        ),
        out_shape=jax.ShapeDtypeStruct((len(overs), height, width), F32),
        compiler_params=PARAMS,
        cost_estimate=cost(0),
        name="wished",
    )(wish, *[section for over in overs for section in over])


def flip(value, axis, size, mask):
    return lax.ppermute(value, axis, [(i, i ^ mask) for i in range(size)])


def first_prolong(shard, axis, size):
    if size != 4:
        return None
    by_two, by_one = flip(shard, axis, size, 2), flip(shard, axis, size, 1)
    return [by_two, by_one, lax.ppermute(shard, axis, [(1, 2), (2, 1)])]


def gather_prolong(shard, near, axis, size):
    depth = shard.shape[0]
    if near is None:
        gathered = lax.all_gather(shard, axis)
        return [(gathered[i], lambda me, i=i: jnp.int32(i * depth), None) for i in range(size)]
    by_two, by_one, middle = near
    handed = lax.ppermute(by_two, axis, [(1, 0), (2, 3)])

    def at(mask):
        return lambda me: (me[0] ^ mask) * depth

    def inner(me):
        return (me[0] == 1) | (me[0] == 2)

    return [
        (shard, at(0), None),
        (by_one, at(1), None),
        (by_two, at(2), None),
        (middle, at(3), inner),
        (handed, at(3), lambda me: jnp.logical_not(inner(me))),
    ]


def gather_restrict(shard, near, slots, axis, size):
    over_x = flip(shard, axis, size, 2)
    over_y = flip(shard, axis, size, 4)
    over_x, slots = lax.optimization_barrier((over_x, slots))
    pieces = [shard, over_x, over_y, flip(over_x, axis, size, 4)]
    if near is not None:
        pieces, near[:2] = lax.optimization_barrier((pieces, near[:2]))
    mine = jnp.stack(pieces)
    return [mine, flip(mine, axis, size, 1)], slots


def pair_switch(index, size, branch, operand, choices=1):
    branches = [
        functools.partial(branch, mask, choice) for mask in range(1, size) for choice in range(choices)
    ]
    return lax.switch(index[0], branches, operand)


def solution(mesh):
    n_row = mesh.shape["row"]
    n_col = mesh.shape["col"]

    def body(tiles, coords, counts, restrict, prolong, row_partner, col_partner):
        tile_order = tiles.shape[1]
        block_rows = restrict.shape[0] * n_col // tile_order
        block_cols = prolong.shape[0] * n_row // tile_order
        half_rows, half_cols = block_rows // 2, block_cols // 2
        row = lax.axis_index("row").astype(jnp.int32)
        col = lax.axis_index("col").astype(jnp.int32)
        me = jnp.stack([row, col])

        row_partner, coords = row_partner.T, coords.T
        places = block_rows * block_cols
        slots, first, wish = make_tables(
            me, row_partner, col_partner, coords, counts, places, block_cols
        )
        near = first_prolong(prolong, "row", n_row)
        by_chip = n_col == 8 and block_rows == 4 and tile_order == 2 * restrict.shape[0]
        if by_chip:
            q_pieces, slots = gather_restrict(restrict, near, slots, "col", n_col)
        else:
            q_pieces = [lax.all_gather(restrict, "col", axis=0, tiled=True)]

        shards = gather_prolong(prolong, near, "row", n_row)

        def left(kind):
            tables = (me, slots, row_partner, col_partner)
            return left_products(kind, tables, tiles, q_pieces, half_rows, block_cols)

        def right(kind, mate_slots, w):
            tables = (me, slots, mate_slots, row_partner, col_partner)
            return right_products(kind, tables, w, shards, half_rows, block_cols)

        def products(kind, mate_slots):
            return right(kind, mate_slots, left(kind))

        def swap_first(mask, _, chunk):
            received = flip(chunk, "row", n_row, mask), flip(slots, "row", n_row, mask)
            return *received, right(Columns.NEXT, slots, w_on), products(Columns.KEPT, slots)

        def swap_next(mask, _, operands):
            chunk, mate_slots = operands
            return flip(chunk, "row", n_row, mask), products(Columns.REST, mate_slots)

        def swap_more(mask, _, operands):
            return flip(operands[0], "row", n_row, mask), operands[1:]

        def swap_rest(mask, extra, rest):
            return [
                flip(array, "row", n_row, mask) if index <= extra else array
                for index, array in enumerate(rest)
            ]

        w_on = left(Columns.ON)
        given = right(Columns.FIRST, slots, w_on)
        received, mate_slots, others, kept = pair_switch(first, n_row, swap_first, given[0])
        given = [*given, *others]
        sections, rest = [], None
        for index in range(half_cols):
            section = kept[index] + received
            if n_col == 8:
                over = [section] + [flip(section, "col", n_col, 2 * chip) for chip in range(1, 4)]
            else:
                over = [lax.all_gather(section, "col")]
            sections.append(over)
            if index + 1 == half_cols:
                break
            chunk, section = lax.optimization_barrier((given[index + 1], section))
            if index == 0:
                received, rest = pair_switch(first, n_row, swap_next, (chunk, mate_slots))
            else:
                received, *_ = pair_switch(first, n_row, swap_more, (chunk,))
            sections[index], received = lax.optimization_barrier((sections[index], received))
        if rest is None:
            rest = products(Columns.REST, mate_slots)
        second, *rest = rest
        rest, section = lax.optimization_barrier((rest, section))
        rest = pair_switch(second, n_row, swap_rest, rest, len(rest))
        if n_col == 8:
            sections[-1], rest = lax.optimization_barrier((sections[-1], rest))
            handed = flip(wished(wish, sections), "col", n_col, 1)
            sections = [[handed] + over for over in sections]
        packed, *singles = rest
        tables = (me, slots, mate_slots, row_partner, col_partner)
        return sum_blocks(tables, half_rows, block_cols, kept[-1], packed, singles, sections)

    in_specs = (
        P(("row", "col"), None, None),
        P(("row", "col"), None),
        P(("row", "col")),
        P(("row", "col"), None),
        P(("col", "row"), None),
        P(),
        P(),
    )
    return jax.shard_map(
        body, mesh=mesh, in_specs=in_specs, out_specs=P("row", "col"), check_vma=False
    )
```

```python
import functools

import jax
import jax.numpy as jnp
from jax import lax
from jax.experimental import pallas as pl
from jax.experimental.pallas import tpu as pltpu
from jax.sharding import PartitionSpec as P

F32 = jnp.float32
BF16 = jnp.bfloat16
VMEM_BYTES = 48 * 1024 * 1024
PARAMS = pltpu.CompilerParams(vmem_limit_bytes=VMEM_BYTES)


def cost(flops):
    return pl.CostEstimate(flops=flops, bytes_accessed=0, transcendentals=0)


def split(value):
    high = value.astype(BF16)
    low = (value - high.astype(F32)).astype(BF16)
    return high, low


def dot(left, right):
    return jnp.dot(left, right, preferred_element_type=F32)


def product(left_both, right_high, right_low):
    half = left_both.shape[0] // 2
    total = dot(left_both[half:], right_high)
    total = total + dot(left_both[:half], right_low)
    return total + dot(left_both[:half], right_high)


def div(value, by):
    return lax.div(value, jnp.int32(by))


def rem(value, by):
    return lax.rem(value, jnp.int32(by))


def half_of(given, me, row_partner):
    mate = row_partner[me[0], me[1]]
    return ((mate > me[0]) if given else (me[0] > mate)).astype(jnp.int32)


def tables_kernel(block_cols, me, row_partner, col_partner, coords, counts, slots, first, wish):
    for place in range(slots.shape[0]):
        slots[place] = jnp.int32(-1)
    for slot in range(coords.shape[1]):

        @pl.when(slot < counts[0])
        def _():
            slots[coords[0, slot] * block_cols + coords[1, slot]] = jnp.int32(slot)

    first[0] = (me[0] ^ row_partner[me[0], me[1]]) - 1
    other = me[1] ^ 1
    wish[0] = div(other ^ col_partner[me[0], other], 2)


def make_tables(me, row_partner, col_partner, coords, counts, places, block_cols):
    smem = pl.BlockSpec(memory_space=pltpu.SMEM)
    return pl.pallas_call(
        functools.partial(tables_kernel, block_cols),
        in_specs=[smem] * 5,
        out_specs=[smem] * 3,
        out_shape=[jax.ShapeDtypeStruct((n,), jnp.int32) for n in (places, 1, 1)],
        cost_estimate=cost(0),
        name="make_tables",
    )(me, row_partner, col_partner, coords, counts)


class Columns:
    FIRST, NEXT, REST, KEPT, ON = range(5)

    def __init__(self, kind, block_cols):
        self.kind = kind
        self.given = kind != self.KEPT
        self.half_cols = block_cols // 2
        self.skip = 1 if kind == self.NEXT else 0
        self.steps = 1 if kind == self.FIRST else self.half_cols - self.skip
        if kind == self.KEPT:
            self.steps = block_cols

    def half(self, step, me, row_partner, col_partner):
        holder = row_partner[me[0], me[1]] if self.given else me[0]
        goes_on = (me[1] < col_partner[holder, me[1]]).astype(jnp.int32)
        if self.kind == self.KEPT:
            return goes_on ^ div(step, self.half_cols)
        return goes_on ^ (1 if self.kind == self.REST else 0)

    def column(self, step, me, row_partner, col_partner):
        half = self.half(step, me, row_partner, col_partner)
        return half * self.half_cols + self.skip + rem(step, self.half_cols)


def left_kernel(columns, block_cols, half_rows, per_step, *refs):
    me, slots, row_partner, col_partner = refs[:4]
    tile_refs, q_refs, out, q_both = refs[4 : 4 + per_step], refs[4 + per_step : -2], refs[-2], refs[-1]
    group, step = pl.program_id(0), pl.program_id(1)
    width = q_both.shape[0] // 2

    block_row = half_of(columns.given, me, row_partner) * half_rows + group

    def put(value, first):
        high, low = split(value.T)
        q_both[:width, first : first + value.shape[0]] = high
        q_both[width:, first : first + value.shape[0]] = low

    if len(q_refs) == 1:

        @pl.when(step == 0)
        def _():
            put(q_refs[0][...], 0)

    else:
        distance = block_row ^ div(me[1], 2)
        for core in range(2):

            @pl.when((step == 0) & (rem(me[1], 2) == core))
            def _():
                depth = q_refs[0].shape[1]
                put(q_refs[0][distance], core * depth)
                put(q_refs[1][distance], (1 - core) * depth)

    for index, tile_ref in enumerate(tile_refs):
        column = columns.column(step * per_step + index, me, row_partner, col_partner)
        live = slots[block_row * block_cols + column] >= 0
        high, low = split(tile_ref[0])
        total = jnp.where(live, product(q_both[...], high, low), 0.0)
        out[index, 0], out[index, 1] = split(total)


def left_products(kind, tables, tiles, q_pieces, half_rows, block_cols):
    _, tile_order, _ = tiles.shape
    width = q_pieces[0].shape[-1]
    columns = Columns(kind, block_cols)
    per_step = 2 if columns.steps % 2 == 0 else 1

    def row_of(g, me, row_partner):
        return half_of(columns.given, me, row_partner) * half_rows + g

    def tile_spec(index):
        def tile_at(g, b, me, slots, row_partner, col_partner):
            column = columns.column(b * per_step + index, me, row_partner, col_partner)
            return jnp.maximum(slots[row_of(g, me, row_partner) * block_cols + column], 0), 0, 0

        return pl.BlockSpec((1, tile_order, tile_order), tile_at)

    if len(q_pieces) == 1:
        q_specs = [
            pl.BlockSpec(
                (tile_order, width),
                lambda g, b, me, slots, row_partner, _: (row_of(g, me, row_partner), 0),
            )
        ]
    else:
        q_specs = [pl.BlockSpec(memory_space=pltpu.VMEM)] * len(q_pieces)
    return pl.pallas_call(
        functools.partial(left_kernel, columns, block_cols, half_rows, per_step),
        grid_spec=pltpu.PrefetchScalarGridSpec(
            num_scalar_prefetch=4,
            grid=(half_rows, columns.steps // per_step),
            in_specs=[tile_spec(index) for index in range(per_step)] + q_specs,
            out_specs=pl.BlockSpec(
                (per_step, 2, width, tile_order), lambda g, b, *_: (b, 0, g, 0)
            ),
            scratch_shapes=[pltpu.VMEM((2 * width, tile_order), BF16)],
        ),
        out_shape=jax.ShapeDtypeStruct((columns.steps, 2, half_rows * width, tile_order), BF16),
        compiler_params=PARAMS,
        cost_estimate=cost(12 * half_rows * columns.steps * width * tile_order * tile_order),
        name="left_products",
    )(*tables, *[tiles] * per_step, *q_pieces)


def packed_first(blocks):
    return max(1, blocks * 3 // 4)


def packed_place(slots, first_row, first_col, half_rows, half_cols, block_cols, block):
    before = here = count = jnp.int32(0)
    for index in range(half_rows * half_cols):
        place = (first_row + index % half_rows) * block_cols + first_col + index // half_rows
        flag = (slots[place] >= 0).astype(jnp.int32)
        before = before + jnp.where(index < block, flag, 0)
        here = here + jnp.where(index == block, flag, 0)
        count = count + flag
    return jnp.where(here == 1, before, count + block - before), here == 1


def quarter_live(table, first_row, first_col, half_rows, half_cols, block_cols):
    count = jnp.int32(0)
    for index in range(half_rows * half_cols):
        place = (first_row + index % half_rows) * block_cols + first_col + index // half_rows
        count = count + (table[place] >= 0).astype(jnp.int32)
    return count


def right_kernel(columns, block_cols, half_rows, starts, *refs):
    me, slots, mate_slots, row_partner, col_partner, w_ref = refs[:6]
    pieces = refs[6 : 6 + len(starts)]
    step = pl.program_id(0)
    tile_order = w_ref.shape[3]
    width = pieces[0].shape[1]
    packs = columns.kind == Columns.REST
    outs = refs[6 + len(starts) : -3 if packs else -2]
    p_high, p_low = refs[-2:]

    @pl.when(step == 0)
    def _():
        low = columns.column(0, me, row_partner, col_partner) * tile_order
        for (start, filled), piece in zip(starts, pieces):
            begin = start(me)
            wanted = begin >= 0
            if columns.given:
                wanted = (begin < low + columns.steps * tile_order) & (begin + piece.shape[0] > low)
            if filled is not None:
                wanted &= filled(me)

            @pl.when(wanted)
            def _():
                depth = piece.shape[0]
                rows = pl.ds(pl.multiple_of(begin, depth), depth)
                p_high[rows, :], p_low[rows, :] = split(piece[...])

    column = columns.column(step, me, row_partner, col_partner)
    rows = pl.ds(pl.multiple_of(column * tile_order, tile_order), tile_order)
    both = w_ref[columns.skip + step if columns.given else 0].reshape(2 * w_ref.shape[2], tile_order)
    block = product(both, p_high[rows, :], p_low[rows, :])
    half_cols = columns.half_cols
    if not packs:
        for index, out in enumerate(outs):

            @pl.when(jnp.minimum(step, half_cols) == index)
            def _():
                out[...] = block

        return
    branch, *outs = outs
    packed = refs[-3]
    first_row = half_of(True, me, row_partner) * half_rows
    first_col = columns.half(step, me, row_partner, col_partner) * half_cols
    for row in range(half_rows):
        place, _ = packed_place(
            slots, first_row, first_col, half_rows, half_cols, block_cols, step * half_rows + row
        )
        packed[place] = block[row * width : (row + 1) * width]

    @pl.when(step == half_cols - 1)
    def _():
        count = outs[0].shape[0]
        outs[0][...] = packed[:count]
        for index, out in enumerate(outs[1:]):
            out[...] = packed[count + index]
        keeps = (me[1] > col_partner[me[0], me[1]]).astype(jnp.int32)
        mate_row = half_of(False, me, row_partner) * half_rows
        quarter = half_rows, half_cols, block_cols
        most = jnp.maximum(
            quarter_live(slots, first_row, first_col, *quarter),
            quarter_live(mate_slots, mate_row, keeps * half_cols, *quarter),
        )
        choice = jnp.clip(most - count, 0, len(outs) - 1)
        branch[0] = ((me[0] ^ row_partner[me[0], me[1]]) - 1) * len(outs) + choice


def right_products(kind, tables, w, shards, half_rows, block_cols):
    _, _, height, tile_order = w.shape
    columns = Columns(kind, block_cols)
    half_cols = columns.half_cols
    width = shards[0][0].shape[1]
    blocks = half_rows * half_cols

    whole = pl.BlockSpec(memory_space=pltpu.VMEM)
    one_column = pl.BlockSpec((1, 2, height, tile_order), lambda i, *_: (i, 0, 0, 0))
    scratch = [pltpu.VMEM((block_cols * tile_order, width), BF16)] * 2
    if kind == Columns.REST:
        most = packed_first(blocks)
        shapes = [(most, width, width)] + [(width, width)] * (blocks - most)
        out_specs = [pl.BlockSpec(memory_space=pltpu.SMEM)]
        out_specs += [pl.BlockSpec(shape, lambda i, *_, n=len(shape): (0,) * n) for shape in shapes]
        scratch = [pltpu.VMEM((blocks, width, width), F32)] + scratch
    else:
        count = min(columns.steps, half_cols)
        shapes = [(height, width)] * count
        out_specs = [pl.BlockSpec((height, width), lambda i, *_: (0, 0))] * count
        if kind == Columns.KEPT:
            shapes += [(height, half_cols * width)]
            out_specs += [
                pl.BlockSpec((height, width), lambda i, *_: (0, jnp.maximum(i - half_cols, 0)))
            ]
    out_shape = [jax.ShapeDtypeStruct(shape, F32) for shape in shapes]
    if kind == Columns.REST:
        out_shape = [jax.ShapeDtypeStruct((1,), jnp.int32)] + out_shape
    return pl.pallas_call(
        functools.partial(
            right_kernel, columns, block_cols, half_rows, [shard[1:] for shard in shards]
        ),
        grid_spec=pltpu.PrefetchScalarGridSpec(
            num_scalar_prefetch=5,
            grid=(columns.steps,),
            in_specs=[whole if columns.given else one_column] + [whole] * len(shards),
            out_specs=out_specs,
            scratch_shapes=scratch,
        ),
        out_shape=out_shape,
        compiler_params=PARAMS,
        cost_estimate=cost(6 * columns.steps * height * width * tile_order),
        name="right_products",
    )(*tables, w, *[shard[0] for shard in shards])


def comes_from(which, me, col_partner):
    distance = me[1] ^ col_partner[me[0], me[1]]
    core = rem(distance, 2) == 1
    return core if which == 0 else jnp.logical_not(core) & (div(distance, 2) == which - 1)


def sum_kernel(half_rows, block_cols, singles, sections, *refs):
    me, _, mate_slots, row_partner, col_partner, kept_ref, packed_ref = refs[:7]
    single_refs, section_refs, out = refs[7 : 7 + singles], refs[7 + singles : -1], refs[-1]
    half_cols = block_cols // 2
    step = pl.program_id(0)
    keeps = (me[1] > col_partner[me[0], me[1]]).astype(jnp.int32)
    first_row = half_of(False, me, row_partner) * half_rows
    place, live = packed_place(
        mate_slots, first_row, keeps * half_cols, half_rows, half_cols, block_cols, step
    )
    count = packed_ref.shape[0]
    at = 0
    for index, kind in enumerate(sections):
        for which in range(kind):
            section = section_refs[at + which]
            wanted = div(step, half_rows) == index
            if kind > 1:
                wanted &= comes_from(which, me, col_partner)

            @pl.when(wanted)
            def _():
                out[...] = kept_ref[...] + section[...].reshape(out.shape)

        at += kind

    @pl.when(live & (place < count))
    def _():
        out[...] += packed_ref[jnp.minimum(place, count - 1)]

    for index, single in enumerate(single_refs):

        @pl.when(live & (place == count + index))
        def _():
            out[...] += single[...]


def sum_blocks(tables, half_rows, block_cols, kept, packed, singles, sections):
    half_cols = block_cols // 2
    height, both = kept.shape
    width = both // half_cols
    block = pl.BlockSpec((width, width), lambda i, *_: (rem(i, half_rows), div(i, half_rows)))

    def section_spec(index, section, which=None):
        def section_at(i, me, slots, mate_slots, row_partner, col_partner):
            here = jnp.clip(i - index * half_rows, 0, half_rows - 1)
            if which is not None:
                here = jnp.where(comes_from(which, me, col_partner), here, 0)
            if section.ndim == 2:
                return here, 0
            return index if which == 0 else col_partner[me[0], me[1]], here, 0

        return pl.BlockSpec((1,) * (section.ndim - 2) + (width, width), section_at)

    return pl.pallas_call(
        functools.partial(
            sum_kernel, half_rows, block_cols, len(singles), [len(each) for each in sections]
        ),
        grid_spec=pltpu.PrefetchScalarGridSpec(
            num_scalar_prefetch=5,
            grid=(half_rows * half_cols,),
            in_specs=[block]
            + [pl.BlockSpec(memory_space=pltpu.VMEM)] * (1 + len(singles))
            + [
                section_spec(index, each, which if len(group) > 1 else None)
                for index, group in enumerate(sections)
                for which, each in enumerate(group)
            ],
            out_specs=block,
        ),
        out_shape=jax.ShapeDtypeStruct((height, both), F32),
        compiler_params=PARAMS,
        name="sum_blocks",
    )(*tables, kept, packed, *singles, *[each for group in sections for each in group])


def wished_kernel(wish, *refs):
    *sections, wanted, sems = refs
    columns = wanted.shape[0]
    for column in range(columns):
        for chip in range(4):

            @pl.when(wish[0] == chip)
            def _():
                section = sections[4 * column + chip]
                pltpu.make_async_copy(section, wanted.at[column], sems.at[column]).start()

    for column in range(columns):
        pltpu.make_async_copy(sections[4 * column], wanted.at[column], sems.at[column]).wait()


def wished(wish, overs):
    height, width = overs[0][0].shape
    sections = [section for over in overs for section in over]
    anywhere = pl.BlockSpec(memory_space=pl.ANY)
    return pl.pallas_call(
        wished_kernel,
        in_specs=[pl.BlockSpec(memory_space=pltpu.SMEM)] + [anywhere] * len(sections),
        out_specs=anywhere,
        out_shape=jax.ShapeDtypeStruct((len(overs), height, width), F32),
        scratch_shapes=[pltpu.SemaphoreType.DMA((len(overs),))],
        compiler_params=PARAMS,
        cost_estimate=cost(0),
        name="wished",
    )(wish, *sections)


def flip(value, axis, size, mask):
    return lax.ppermute(value, axis, [(i, i ^ mask) for i in range(size)])


def first_prolong(shard, axis, size):
    if size != 4:
        return None
    by_two, by_one = flip(shard, axis, size, 2), flip(shard, axis, size, 1)
    return [by_two, by_one, lax.ppermute(shard, axis, [(1, 2), (2, 1)])]


def gather_prolong(shard, near, axis, size):
    depth = shard.shape[0]
    if near is None:
        gathered = lax.all_gather(shard, axis)
        return [(gathered[i], lambda me, i=i: jnp.int32(i * depth), None) for i in range(size)]
    by_two, by_one, middle = near
    handed = lax.ppermute(by_two, axis, [(1, 0), (2, 3)])

    def at(mask):
        return lambda me: (me[0] ^ mask) * depth

    def inner(me):
        return (me[0] == 1) | (me[0] == 2)

    return [
        (shard, at(0), None),
        (by_one, at(1), None),
        (by_two, at(2), None),
        (middle, at(3), inner),
        (handed, at(3), lambda me: jnp.logical_not(inner(me))),
    ]


def gather_restrict(shard, near, slots, axis, size):
    over_x = flip(shard, axis, size, 2)
    over_y = flip(shard, axis, size, 4)
    over_x, slots = lax.optimization_barrier((over_x, slots))
    pieces = [shard, over_x, over_y, flip(over_x, axis, size, 4)]
    if near is not None:
        pieces, near[:2] = lax.optimization_barrier((pieces, near[:2]))
    mine = jnp.stack(pieces)
    return [mine, flip(mine, axis, size, 1)], slots


def pair_switch(index, size, branch, operand, choices=1):
    branches = [
        functools.partial(branch, mask, choice) for mask in range(1, size) for choice in range(choices)
    ]
    return lax.switch(index[0], branches, operand)


def solution(mesh):
    n_row = mesh.shape["row"]
    n_col = mesh.shape["col"]

    def body(tiles, coords, counts, restrict, prolong, row_partner, col_partner):
        tile_order = tiles.shape[1]
        block_rows = restrict.shape[0] * n_col // tile_order
        block_cols = prolong.shape[0] * n_row // tile_order
        half_rows, half_cols = block_rows // 2, block_cols // 2
        row = lax.axis_index("row").astype(jnp.int32)
        col = lax.axis_index("col").astype(jnp.int32)
        me = jnp.stack([row, col])

        row_partner, coords = row_partner.T, coords.T
        places = block_rows * block_cols
        slots, first, wish = make_tables(
            me, row_partner, col_partner, coords, counts, places, block_cols
        )
        near = first_prolong(prolong, "row", n_row)
        by_chip = n_col == 8 and block_rows == 4 and tile_order == 2 * restrict.shape[0]
        if by_chip:
            q_pieces, slots = gather_restrict(restrict, near, slots, "col", n_col)
        else:
            q_pieces = [lax.all_gather(restrict, "col", axis=0, tiled=True)]

        shards = gather_prolong(prolong, near, "row", n_row)

        def left(kind):
            tables = (me, slots, row_partner, col_partner)
            return left_products(kind, tables, tiles, q_pieces, half_rows, block_cols)

        def right(kind, mate_slots, w):
            tables = (me, slots, mate_slots, row_partner, col_partner)
            return right_products(kind, tables, w, shards, half_rows, block_cols)

        def products(kind, mate_slots):
            return right(kind, mate_slots, left(kind))

        def swap_first(mask, _, chunk):
            received = flip(chunk, "row", n_row, mask), flip(slots, "row", n_row, mask)
            return *received, right(Columns.NEXT, slots, w_on), products(Columns.KEPT, slots)

        def swap_next(mask, _, operands):
            chunk, mate_slots = operands
            return flip(chunk, "row", n_row, mask), products(Columns.REST, mate_slots)

        def swap_more(mask, _, operands):
            return flip(operands[0], "row", n_row, mask), operands[1:]

        def swap_rest(mask, extra, rest):
            return [
                flip(array, "row", n_row, mask) if index <= extra else array
                for index, array in enumerate(rest)
            ]

        w_on = left(Columns.ON)
        given = right(Columns.FIRST, slots, w_on)
        received, mate_slots, others, kept = pair_switch(first, n_row, swap_first, given[0])
        given = [*given, *others]
        sections, rest = [], None
        for index in range(half_cols):
            section = kept[index] + received
            if n_col == 8:
                over = [section] + [flip(section, "col", n_col, 2 * chip) for chip in range(1, 4)]
            else:
                over = [lax.all_gather(section, "col")]
            sections.append(over)
            if index + 1 == half_cols:
                break
            chunk, section = lax.optimization_barrier((given[index + 1], section))
            if index == 0:
                received, rest = pair_switch(first, n_row, swap_next, (chunk, mate_slots))
            else:
                received, *_ = pair_switch(first, n_row, swap_more, (chunk,))
            sections[index], received = lax.optimization_barrier((sections[index], received))
        if rest is None:
            rest = products(Columns.REST, mate_slots)
        second, *rest = rest
        rest, section = lax.optimization_barrier((rest, section))
        rest = pair_switch(second, n_row, swap_rest, rest, len(rest))
        if n_col == 8:
            sections[-1], rest = lax.optimization_barrier((sections[-1], rest))
            handed = flip(wished(wish, sections), "col", n_col, 1)
            sections = [[handed] + over for over in sections]
        packed, *singles = rest
        tables = (me, slots, mate_slots, row_partner, col_partner)
        return sum_blocks(tables, half_rows, block_cols, kept[-1], packed, singles, sections)

    in_specs = (
        P(("row", "col"), None, None),
        P(("row", "col"), None),
        P(("row", "col")),
        P(("row", "col"), None),
        P(("col", "row"), None),
        P(),
        P(),
    )
    return jax.shard_map(
        body, mesh=mesh, in_specs=in_specs, out_specs=P("row", "col"), check_vma=False
    )
```
